32 devices in a mesh: len: 4 (over x, core), brick: 8 (over z, y).
Axes of the slice: x: 2, y: 2, z: 4, core: 2. Of those that a mesh axis runs over, the one named last changes fastest.
Arguments:
- forces: float32 [3, 32, 128, 128], P(None, 'len', 'brick'), may hold values from -6 to 6
- modulus: float32 [32, 128, 128], P('len', 'brick'), may hold values from 1 to 10
- occupancy: int32 [32, 128, 128], P('len', 'brick'), may hold values 0 or 1
- bonded: int32 [32, 128, 128], P('len', 'brick'), may hold values 0 or 1
Outputs:
- solution: float32 [3, 32, 128, 128], P(None, 'len', 'brick')
The draws below stay inside these ranges and needn't reach their ends.
All inputs are finite; a program needn't handle non-finite values. No bound on the sum of `occupancy` or of `bonded` on one device may be relied on, other than what follows from the above.
Results may differ from the reference program's by a relative error of at most 0.0001.
Values sent between devices are 32-bit elements; how exact they have to be, the bound alone decides.
No kernel may reach another device: no remote copies, remote signals or barrier semaphores. Data moves between devices by JAX's collectives and lax.ppermute only.
A program may use at most 64 MiB of HBM per device.

```python
import math
import jax
import jax.numpy as jnp
from jax import lax

CZ = 128
LEVELS = 3
PRE_SWEEPS = 2
POST_SWEEPS = 2
COARSE_SWEEPS = 4
NX = 32
NY = 128


def place_ends(values, rng, low, largest):
    index_at = [jax.random.randint(jax.random.fold_in(rng, axis), (), 0, length) for axis, length in enumerate(values.shape)]
    longest = values.shape.index(max(values.shape))
    beside = index_at[:longest] + [(index_at[longest] + 1) % values.shape[longest]] + index_at[longest + 1:]
    return values.at[tuple(index_at)].set(low).at[tuple(beside)].set(largest)


def level_of(stream_key, shape, cuts, low, high):
    loudness, own = 1.0, jax.random.fold_in(stream_key, 6)
    for position, shards_of in cuts:
        heights = jnp.exp(jax.random.uniform(jax.random.fold_in(own, position), (shards_of,), jnp.float32, low / len(cuts), high / len(cuts)))
        loudness = loudness * jnp.repeat(heights, shape[position] // shards_of).reshape([-1 if axis == position else 1 for axis in range(len(shape))])
    return loudness


def gaussian(stream_key, dims, deviation, reach, shards=(), dtype=jnp.bfloat16):
    factor_of = level_of(stream_key, dims, shards, -0.22, 0.18) if shards else 1.0
    drawn = jax.random.normal(stream_key, dims, jnp.float32) * deviation * factor_of
    return jnp.minimum(jnp.maximum(drawn, -reach), reach).astype(dtype)


def setup_inputs(seed: int = 0) -> dict:
    keys = jax.random.split(jax.random.key(seed), 5)
    return {
        "forces": gaussian(keys[0], (3, NX, NY, CZ), 1.0, 6.0, ((1, 4), (2, 8)), jnp.float32),
        "modulus": jnp.clip(jnp.exp(math.log(10.0) - 2.3025851 * jax.random.uniform(keys[1], (NX, NY, CZ), jnp.float32) ** level_of(keys[1], (NX, NY, CZ), ((0, 4), (1, 8)), -0.2, 0.2)), 1.0, 10.0),
        "occupancy": place_ends((jax.random.randint(keys[2], (NX, NY, CZ), 0, 4) < 3).astype(jnp.int32), jax.random.fold_in(keys[2], 1), 0, 1),
        "bonded": place_ends((jax.random.randint(keys[3], (NX, NY, CZ), 0, 16) < 1).astype(jnp.int32), jax.random.fold_in(keys[3], 1), 0, 1),
    }


DAMPING = 0.6
COUPLING = 0.2
MASS_TERM = 0.1
PENALTY = 20.0
COARSE_SCALE = 0.25


def smooth(extended):
    ndims = extended.ndim
    padded = jnp.pad(extended, [(0, 0)] * (ndims - 1) + [(1, 1)])
    depth = padded.shape[-1]
    total = extended + 0.5 * (lax.slice_in_dim(padded, 0, depth - 2, axis=ndims - 1) + lax.slice_in_dim(padded, 2, depth, axis=ndims - 1))
    for axis_now in (ndims - 2, ndims - 3):
        extent = total.shape[axis_now]
        total = lax.slice_in_dim(total, 1, extent - 1, axis=axis_now) + 0.5 * (lax.slice_in_dim(total, 0, extent - 2, axis=axis_now) + lax.slice_in_dim(total, 2, extent, axis=axis_now))
    return total


def weights_only(coeff_ext):
    centre = coeff_ext[1:-1, 1:-1, :]
    weight_total = 6.0 * centre + smooth(coeff_ext)
    return centre, weight_total


def stencil(field_ext, coeff_ext):
    centre, weight_total = weights_only(coeff_ext)
    field_mid = field_ext[:, 1:-1, 1:-1, :]
    product_ext = coeff_ext[None] * field_ext
    product_mid = product_ext[:, 1:-1, 1:-1, :]
    gathered_sum = centre * (smooth(field_ext) - field_mid) + smooth(product_ext) - product_mid
    return centre, weight_total, gathered_sum


def apply_operator(field_ext, coeff_ext, shift_term):
    centre, weight_total, gathered_sum = stencil(field_ext, coeff_ext)
    field_mid = field_ext[:, 1:-1, 1:-1, :]
    return (weight_total + shift_term) * field_mid - gathered_sum + COUPLING * centre * jnp.sum(field_mid, axis=0)


def jacobi_step(field_ext, coeff_ext, shift_term, source, extra):
    centre, weight_total, gathered_sum = stencil(field_ext, coeff_ext)
    field_mid = field_ext[:, 1:-1, 1:-1, :]
    applied = (weight_total + shift_term) * field_mid - gathered_sum + COUPLING * centre * jnp.sum(field_mid, axis=0)
    return field_mid + DAMPING * (source - applied) / (weight_total + shift_term + COUPLING * centre + extra)


def first_step(coeff_ext, shift_term, source):
    centre, weight_total = weights_only(coeff_ext)
    return DAMPING * source / (weight_total + shift_term + COUPLING * centre)


def restrict_field(values):
    shaped = values.reshape(values.shape[0], values.shape[1] // 2, 2, values.shape[2] // 2, 2, values.shape[3] // 2, 2)
    return jnp.mean(shaped, axis=(2, 4, 6))


def restrict_cells(values):
    return restrict_field(values[None])[0]


def prolong(values):
    return jnp.repeat(jnp.repeat(jnp.repeat(values, 2, axis=1), 2, axis=2), 2, axis=3)


def pad_field(values):
    return jnp.pad(values, ((0, 0), (1, 1), (1, 1), (0, 0)))


def pad_coeff(values):
    return jnp.pad(values, ((1, 1), (1, 1), (0, 0)))


def reference(forces, modulus, occupancy, bonded):
    coeffs = [modulus * occupancy.astype(jnp.float32)]
    shifts = [MASS_TERM + PENALTY * bonded.astype(jnp.float32)]
    for tier_index in range(LEVELS):
        coeffs.append(COARSE_SCALE * restrict_cells(coeffs[-1]))
        shifts.append(restrict_cells(shifts[-1]))

    def coarsest_solve(source):
        coeff_ext = pad_coeff(coeffs[LEVELS])
        shift_term = shifts[LEVELS]
        iterate = first_step(coeff_ext, shift_term, source)
        for repeat_idx in range(COARSE_SWEEPS - 1):
            iterate = jacobi_step(pad_field(iterate), coeff_ext, shift_term, source, 0.0)
        return iterate

    def multigrid_pass(tier_index, source):
        coeff_ext = pad_coeff(coeffs[tier_index])
        shift_term = shifts[tier_index]
        iterate = first_step(coeff_ext, shift_term, source)
        for repeat_idx in range(PRE_SWEEPS - 1):
            iterate = jacobi_step(pad_field(iterate), coeff_ext, shift_term, source, 0.0)
        residual = source - apply_operator(pad_field(iterate), coeff_ext, shift_term)
        coarse_source = restrict_field(residual)
        if tier_index + 1 == LEVELS:
            correction = coarsest_solve(coarse_source)
        else:
            correction = multigrid_pass(tier_index + 1, coarse_source)
        iterate = iterate + prolong(correction)
        for repeat_idx in range(POST_SWEEPS):
            iterate = jacobi_step(pad_field(iterate), coeff_ext, shift_term, source, 0.0)
        return iterate

    return multigrid_pass(0, forces)
```

```python
import functools

import jax
import jax.numpy as jnp
from jax import lax
from jax.experimental import pallas as pl
from jax.experimental.pallas import tpu as pltpu
from jax.sharding import PartitionSpec as P

DAMPING = 0.6
COUPLING = 0.2
MASS_TERM = 0.1
PENALTY = 20.0

HALO = 4
LANES = 128
F32 = jnp.float32
BOTH = ("len", "brick")


def lane_ids(shape):
    return lax.broadcasted_iota(jnp.int32, shape, len(shape) - 1)


def turn(x, by, axis):
    return pltpu.roll(x, by % x.shape[axis], axis)


class Lane:
    def __init__(self, rows, wide):
        ids = lane_ids((rows, LANES))
        self.wide = wide
        self.low = jnp.where(ids >= wide, 0.5, 0.0).astype(F32)
        self.high = jnp.where(ids < LANES - wide, 0.5, 0.0).astype(F32)
        self.first = (ids & wide) == 0

    def smooth(self, x):
        return x + self.low * turn(x, self.wide, 1) + self.high * turn(x, -self.wide, 1)

    def pair(self, x):
        return x + jnp.where(self.first, turn(x, -self.wide, 1), turn(x, self.wide, 1))


def smooth_rows(x):
    pair = x + turn(x, 1, 0)
    return pair + turn(pair, -1, 0)


def smooth_planes(get, p):
    below, here, above = get(p - 1), get(p), get(p + 1)
    total = here + here
    if below is not None:
        total = total + below
    if above is not None:
        total = total + above
    return total


def remember(get):
    seen = {}

    def cached(p):
        if p not in seen:
            seen[p] = get(p)
        return seen[p]

    return cached


def within(get, low, high):
    return lambda p: get(p) if low <= p < high else None


def gathered(field, quarter, planes, bounds, lane):
    low, high = bounds
    q_at = remember(within(lambda p: quarter[p], low, high))
    v_at = [remember(within(lambda p, k=k: field(k, p), low, high)) for k in range(3)]
    w_at = [
        remember(within(lambda p, k=k: q_at(p) * v_at[k](p), low, high)) for k in range(3)
    ]
    for p in planes:
        q = q_at(p)
        sums = []
        for k in range(3):
            x = smooth_rows(smooth_planes(v_at[k], p))
            y = smooth_rows(smooth_planes(w_at[k], p))
            sums.append(q * lane.smooth(x) + lane.smooth(y))
        yield p, [v_at[k](p) for k in range(3)], q, sums


def defects(field, quarter, weight, source, planes, bounds, lane):
    for p, v, q, sums in gathered(field, quarter, planes, bounds, lane):
        coupled = (4.0 * COUPLING) * q * (v[0] + v[1] + v[2])
        e = weight[p]
        yield p, v, [source[k, p] - e * v[k] + sums[k] - coupled for k in range(3)]


def sweep(field, quarter, weight, step, source, planes, bounds, lane, put):
    for p, v, r in defects(field, quarter, weight, source, planes, bounds, lane):
        s = step[p]
        for k in range(3):
            put(k, p, v[k] + s * r[k])


def stiffness_sum(quarter, planes, bounds, lane):
    q_at = remember(within(lambda p: quarter[p], *bounds))
    for p in planes:
        yield p, 24.0 * q_at(p) + lane.smooth(smooth_rows(smooth_planes(q_at, p)))


def step_of(inside, diagonal):
    return jnp.where(inside > 0.0, DAMPING / diagonal, 0.0)


def odd(axis):
    return lax.rem(lax.axis_index(axis), 2) == 1


def vmem(shape):
    return pltpu.VMEM(shape, F32)


def raw_field(forces, modulus, occupancy, bonded, k, p, rows):
    if k < 3:
        return forces[k, p, rows, :]
    if k == 3:
        return modulus[p, rows, :] * occupancy[p, rows, :].astype(F32)
    return MASS_TERM + PENALTY * bonded[p, rows, :].astype(F32)


def pack_planes(forces, modulus, occupancy, bonded, to_a, to_b):
    planes, rows = modulus.shape[0], modulus.shape[1]
    last = planes - HALO
    is_odd = lax.rem(lax.axis_index("len"), 2)
    start_a, start_b = (1 - is_odd) * last, is_odd * last
    for i in range(HALO):
        for k in range(5):
            to_a[k, i] = raw_field(
                forces, modulus, occupancy, bonded, k, start_a + i, slice(0, rows)
            )
            to_b[k, i] = raw_field(
                forces, modulus, occupancy, bonded, k, start_b + i, slice(0, rows)
            )


def extended_rows(own, from_a, from_b, planes, is_odd):
    def get(k, p, rows):
        if p < HALO:
            return jnp.where(is_odd, from_a[k, p, rows, :], from_b[k, p, rows, :])
        if p >= HALO + planes:
            i = p - HALO - planes
            return jnp.where(is_odd, from_b[k, i, rows, :], from_a[k, i, rows, :])
        return own(k, p - HALO, rows)

    return get


def pack_rows_from(get, planes, rows, to_c, to_d):
    is_odd = odd("brick")
    for k in range(5):
        for p in range(planes + 2 * HALO):
            first = get(k, p, slice(0, HALO))
            last = get(k, p, slice(rows - HALO, rows))
            to_c[k, p] = jnp.where(is_odd, first, last)
            to_d[k, p] = jnp.where(is_odd, last, first)


def pack_rows_fine(forces, modulus, occupancy, bonded, from_a, from_b, to_c, to_d):
    planes, rows = modulus.shape[0], modulus.shape[1]
    own = functools.partial(raw_field, forces, modulus, occupancy, bonded)
    pack_rows_from(
        extended_rows(own, from_a, from_b, planes, odd("len")), planes, rows, to_c, to_d
    )


def pack_rows_coarse(own, from_a, from_b, to_c, to_d):
    planes, rows = own.shape[1], own.shape[2]
    get = extended_rows(lambda k, p, r: own[k, p, r, :], from_a, from_b, planes, odd("len"))
    pack_rows_from(get, planes, rows, to_c, to_d)


def spread_rows(get, from_c, from_d, planes, rows, put):
    is_odd = odd("brick")
    for p in range(planes + 2 * HALO):
        for k in range(5):
            low = jnp.where(is_odd, from_c[k, p], from_d[k, p])
            high = jnp.where(is_odd, from_d[k, p], from_c[k, p])
            put(k, p, slice(0, HALO), low)
            put(k, p, slice(HALO, HALO + rows), get(k, p, slice(0, rows)))
            put(k, p, slice(HALO + rows, 2 * HALO + rows), high)


def fine_before(
    forces, modulus, occupancy, bonded, from_a, from_b, from_c, from_d,
    own_coarse, cells, v2, source, quarter, weight, step,
    shift, v1, work, coarse_q,
):
    planes, rows = modulus.shape[0], modulus.shape[1]
    ext_planes, ext_rows = planes + 2 * HALO, rows + 2 * HALO
    lane = Lane(ext_rows, 1)
    own = functools.partial(raw_field, forces, modulus, occupancy, bonded)

    def put(k, p, r, value):
        if k < 3:
            source[k, p, r, :] = value
        elif k == 3:
            quarter[p, r, :] = 0.25 * value
        else:
            shift[p, r, :] = value

    get = extended_rows(own, from_a, from_b, planes, odd("len"))
    spread_rows(get, from_c, from_d, planes, rows, put)

    bounds = (0, ext_planes)
    for p, w in stiffness_sum(quarter, range(1, ext_planes - 1), bounds, lane):
        q, s = quarter[p], shift[p]
        total = w + s
        weight[p] = total + 8.0 * q
        st = step_of(s, total + (4.0 * COUPLING) * q)
        step[p] = st
        for k in range(3):
            v1[k, p] = st * source[k, p]

    def put_v2(k, p, value):
        v2[k, p] = value

    sweep(
        lambda k, p: v1[k, p], quarter, weight, step, source,
        range(2, ext_planes - 2), bounds, lane, put_v2,
    )

    held = {}
    half = rows // 2
    for p, _, r in defects(
        lambda k, p: v2[k, p], quarter, weight, source,
        range(HALO, HALO + planes), bounds, lane,
    ):
        if p % 2 == 0:
            held = r
            continue
        i = (p - HALO) // 2
        for k in range(3):
            work[k, i] = lane.pair(held[k] + r[k])
    for i in range(planes // 2):
        for k in range(3):
            own_coarse[k, i] = 0.125 * (
                work[k, i, pl.ds(HALO, half, stride=2), :]
                + work[k, i, pl.ds(HALO + 1, half, stride=2), :]
            )

    reach = planes // 2 + 2
    for j in range(reach):
        p = 2 * j + 2
        work[0, j] = lane.pair(quarter[p] + quarter[p + 1])
        coarse_q[j, pl.ds(6, ext_rows // 2), :] = (0.25 * 0.125) * (
            work[0, j, pl.ds(0, ext_rows // 2, stride=2), :]
            + work[0, j, pl.ds(1, ext_rows // 2, stride=2), :]
        )
    for i in range(planes // 2):
        p = HALO + 2 * i
        work[1, i] = lane.pair(shift[p] + shift[p + 1])
    lane1 = Lane(half, 2)
    shift1, q1 = [], []
    for i in range(planes // 2):
        s = 0.125 * (
            work[1, i, pl.ds(HALO, half, stride=2), :]
            + work[1, i, pl.ds(HALO + 1, half, stride=2), :]
        )
        sides = smooth_planes(lambda j: coarse_q[j, pl.ds(7, half), :], i + 1)
        here = smooth_planes(lambda j: coarse_q[j, pl.ds(8, half), :], i + 1)
        others = smooth_planes(lambda j: coarse_q[j, pl.ds(9, half), :], i + 1)
        q = coarse_q[i + 1, pl.ds(8, half), :]
        w = 24.0 * q + lane1.smooth(sides + 2.0 * here + others)
        own_coarse[3, i] = q
        own_coarse[4, i] = w + s
        shift1.append(s)
        q1.append(q)

    quarter_rows = half // 2
    for i in range(planes // 4):
        work[2, 0, pl.ds(0, half), :] = lane1.pair(q1[2 * i] + q1[2 * i + 1])
        work[2, 1, pl.ds(0, half), :] = lane1.pair(shift1[2 * i] + shift1[2 * i + 1])
        cells[0, i] = (0.25 * 0.125) * (
            work[2, 0, pl.ds(0, quarter_rows, stride=2), :]
            + work[2, 0, pl.ds(1, quarter_rows, stride=2), :]
        )
        cells[1, i] = 0.125 * (
            work[2, 1, pl.ds(0, quarter_rows, stride=2), :]
            + work[2, 1, pl.ds(1, quarter_rows, stride=2), :]
        )


def middle_before(
    own, cells, from_a, from_b, from_c, from_d,
    to_all, v2, source, quarter, weight, step,
    v1, work,
):
    planes, rows = own.shape[1], own.shape[2]
    ext_planes, ext_rows = planes + 2 * HALO, rows + 2 * HALO
    lane = Lane(ext_rows, 2)

    def put(k, p, r, value):
        if k < 3:
            source[k, p, r, :] = value
        elif k == 3:
            quarter[p, r, :] = value
        else:
            weight[p, r, :] = value

    get = extended_rows(lambda k, p, r: own[k, p, r, :], from_a, from_b, planes, odd("len"))
    spread_rows(get, from_c, from_d, planes, rows, put)

    for p in range(ext_planes):
        q, total = quarter[p], weight[p]
        st = step_of(total, total + (4.0 * COUPLING) * q)
        step[p] = st
        weight[p] = total + 8.0 * q
        for k in range(3):
            v1[k, p] = st * source[k, p]

    def put_v2(k, p, value):
        v2[k, p] = value

    bounds = (0, ext_planes)
    sweep(
        lambda k, p: v1[k, p], quarter, weight, step, source,
        range(1, ext_planes - 1), bounds, lane, put_v2,
    )
    held = {}
    half = rows // 2
    ids = lane_ids((half, LANES))
    mine = (ids & 3) == lax.broadcasted_iota(jnp.int32, (half, LANES), 0)
    slots = 2 * to_all.shape[0] // (5 * (planes // 2))

    def send(row, value):
        packed = jnp.sum(jnp.where(mine, value, 0.0), axis=0, keepdims=True)
        for s in range(slots):
            at = s * (5 * (planes // 2)) + row
            to_all[at // 2, at % 2 : at % 2 + 1, :] = packed

    for p, _, r in defects(
        lambda k, p: v2[k, p], quarter, weight, source,
        range(HALO, HALO + planes), bounds, lane,
    ):
        if p % 2 == 0:
            held = r
            continue
        i = (p - HALO) // 2
        for k in range(3):
            work[k, i] = lane.pair(held[k] + r[k])
    for i in range(planes // 2):
        for k in range(3):
            send(
                k * (planes // 2) + i,
                0.125
                * (
                    work[k, i, pl.ds(HALO, half, stride=2), :]
                    + work[k, i, pl.ds(HALO + 1, half, stride=2), :]
                ),
            )
        for k in range(2):
            send((3 + k) * (planes // 2) + i, cells[k, i])


def prolong_rows(coarse, put):
    rows = coarse.shape[0]
    put(pl.ds(0, rows, stride=2), coarse)
    put(pl.ds(1, rows, stride=2), coarse)


def coarse_and_after(
    bricks_before,
    table, v2_mid, source_mid, quarter_mid, weight_mid, step_mid,
    v2_fine, source_fine, quarter_fine, weight_fine, step_fine,
    out,
    b2, q2, s2, e2, x2, u2, t2, b3, q3, s3, e3, x3, u3, grown, u_mid, x_mid, u_fine, x_fine,
):
    brick = lax.axis_index("brick")
    slab = lax.axis_index("len")
    slabs, bricks, lines = table.shape[0], table.shape[1], table.shape[2]
    depth = lines // 5
    rows_each = 4
    planes2 = slabs * depth
    all_rows = b2.shape[2]
    used = rows_each * bricks + 2 * HALO
    pad = HALO

    ids = lane_ids((bricks, LANES))
    first1, first2 = (ids & 1) == 0, (ids & 2) == 0
    zero_rows = jnp.zeros((pad, LANES), F32)
    zero_tail = jnp.zeros((all_rows - pad - rows_each * bricks, LANES), F32)
    for f in range(5):
        for i in range(planes2):
            target = b2.at[f, i] if f < 3 else (q2.at[i] if f == 3 else s2.at[i])
            target[pl.ds(0, pad), :] = zero_rows
            target[pl.ds(pad + rows_each * bricks, zero_tail.shape[0]), :] = zero_tail
            line = table[i // depth, :, f * depth + i % depth, :]
            for row in range(rows_each):
                x = jnp.where((ids & 3) == row, line, 0.0)
                x = x + jnp.where(first1, turn(x, -1, 1), turn(x, 1, 1))
                x = x + jnp.where(first2, turn(x, -2, 1), turn(x, 2, 1))
                target[pl.ds(pad + row, bricks, stride=rows_each), :] = x

    lane2 = Lane(all_rows, 4)
    bounds = (0, planes2)
    everything = range(planes2)
    for p, w in stiffness_sum(q2, everything, bounds, lane2):
        q, s = q2[p], s2[p]
        total = w + s
        e2[p] = total + 8.0 * q
        st = step_of(s, total + (4.0 * COUPLING) * q)
        x2[p] = st
        for k in range(3):
            u2[k, p] = st * b2[k, p]

    def put_t2(k, p, value):
        t2[k, p] = value

    sweep(lambda k, p: u2[k, p], q2, e2, x2, b2, everything, bounds, lane2, put_t2)

    rows3 = all_rows // 2
    planes3 = planes2 // 2
    held = {}
    for p, _, r in defects(lambda k, p: t2[k, p], q2, e2, b2, everything, bounds, lane2):
        if p % 2 == 0:
            held = r
            continue
        for k in range(3):
            u2[k, p] = lane2.pair(held[k] + r[k])
    for i in range(planes3):
        grown[0] = lane2.pair(q2[2 * i] + q2[2 * i + 1])
        grown[1] = lane2.pair(s2[2 * i] + s2[2 * i + 1])
        q3[i] = (0.25 * 0.125) * (
            grown[0, pl.ds(0, rows3, stride=2), :] + grown[0, pl.ds(1, rows3, stride=2), :]
        )
        s3[i] = 0.125 * (
            grown[1, pl.ds(0, rows3, stride=2), :] + grown[1, pl.ds(1, rows3, stride=2), :]
        )
        for k in range(3):
            b3[k, i] = 0.125 * (
                u2[k, 2 * i + 1, pl.ds(0, rows3, stride=2), :]
                + u2[k, 2 * i + 1, pl.ds(1, rows3, stride=2), :]
            )

    lane3 = Lane(rows3, 8)
    bounds3 = (0, planes3)
    for p, w in stiffness_sum(q3, range(planes3), bounds3, lane3):
        q, s = q3[p], s3[p]
        total = w + s
        e3[p] = total + 8.0 * q
        st = step_of(s, total + (4.0 * COUPLING) * q)
        x3[p] = st
        for k in range(3):
            u3[0, k, p] = st * b3[k, p]
    for turn_at in range(3):

        def put_u3(k, p, value, turn_at=turn_at):
            u3[(turn_at + 1) % 2, k, p] = value

        sweep(
            lambda k, p: u3[turn_at % 2, k, p], q3, e3, x3, b3,
            range(planes3), bounds3, lane3, put_u3,
        )

    for k in range(3):
        for i in range(planes3):
            coarse = u3[1, k, i]
            for half in range(2):
                u2[k, 2 * i, pl.ds(half, rows3, stride=2), :] = coarse
            both = u2[k, 2 * i]
            t2[k, 2 * i] = t2[k, 2 * i] + both
            t2[k, 2 * i + 1] = t2[k, 2 * i + 1] + both

    def put_u2(k, p, value):
        u2[k, p] = value

    zero_plane = jnp.zeros((all_rows, LANES), F32)
    sweep(lambda k, p: t2[k, p], q2, e2, x2, b2, everything, bounds, lane2, put_u2)

    def put_wide(k, p, value):
        t2[k, p + 2] = value

    for k in range(3):
        for p in (0, 1, planes2 + 2, planes2 + 3):
            t2[k, p] = zero_plane
    sweep(lambda k, p: u2[k, p], q2, e2, x2, b2, everything, bounds, lane2, put_wide)

    planes1 = v2_mid.shape[1]
    rows1 = v2_mid.shape[2]
    lane1 = Lane(rows1, 2)
    bounds1 = (0, planes1)
    row_at = rows_each * (brick - bricks_before(brick)) + pad - 2
    for k in range(3):
        for i in range(planes1 // 2):
            piece = t2[k, depth * slab + i, pl.ds(row_at, rows1 // 2), :]
            for half in range(2):
                x_mid[k, i, pl.ds(half, rows1 // 2, stride=2), :] = piece
            both = x_mid[k, i]
            for p in (2 * i, 2 * i + 1):
                if 1 <= p < planes1 - 1:
                    u_mid[k, p] = v2_mid[k, p] + both

    def put_mid(k, p, value):
        x_mid[k, p] = value

    sweep(
        lambda k, p: u_mid[k, p], quarter_mid, weight_mid, step_mid, source_mid,
        range(2, planes1 - 2), bounds1, lane1, put_mid,
    )

    def put_mid_last(k, p, value):
        u_mid[k, p] = value

    sweep(
        lambda k, p: x_mid[k, p], quarter_mid, weight_mid, step_mid, source_mid,
        range(3, planes1 - 3), bounds1, lane1, put_mid_last,
    )

    planes0, rows0 = v2_fine.shape[1], v2_fine.shape[2]
    lane0 = Lane(rows0, 1)
    bounds0 = (0, planes0)
    half_rows = rows0 // 2
    for k in range(3):
        for i in range(3, planes1 - 3):
            piece = u_mid[k, i, pl.ds(2, half_rows), :]
            p = 2 * i - HALO
            for half in range(2):
                x_fine[k, p, pl.ds(half, half_rows, stride=2), :] = piece
            both = x_fine[k, p]
            for at in (p, p + 1):
                u_fine[k, at] = v2_fine[k, at] + both

    def put_fine(k, p, value):
        x_fine[k, p] = value

    sweep(
        lambda k, p: u_fine[k, p], quarter_fine, weight_fine, step_fine, source_fine,
        range(3, planes0 - 3), bounds0, lane0, put_fine,
    )

    def put_out(k, p, value):
        out[k, p - HALO] = value[HALO : rows0 - HALO]

    sweep(
        lambda k, p: x_fine[k, p], quarter_fine, weight_fine, step_fine, source_fine,
        range(HALO, planes0 - HALO), bounds0, lane0, put_out,
    )


def call(kernel, outs, scratch=(), name=None):
    return pl.pallas_call(
        kernel,
        out_shape=[jax.ShapeDtypeStruct(shape, F32) for shape in outs],
        scratch_shapes=[vmem(shape) for shape in scratch],
        compiler_params=pltpu.CompilerParams(vmem_limit_bytes=48 * 1024 * 1024),
        name=name,
    )


def swap(x, axis, first):
    count = lax.axis_size(axis)
    pairs = []
    for i in range(first, count - 1, 2):
        pairs += [(i, i + 1), (i + 1, i)]
    return lax.ppermute(x, axis, pairs)


def body(forces, modulus, occupancy, bonded):
    planes, rows = modulus.shape[0], modulus.shape[1]
    slabs, bricks = lax.axis_size("len"), lax.axis_size("brick")
    raw = (forces, modulus, occupancy, bonded)
    ext, ext_rows = planes + 2 * HALO, rows + 2 * HALO
    half, half_rows = planes // 2, rows // 2
    mid, mid_rows = half + 2 * HALO, half_rows + 2 * HALO

    side = (5, HALO, rows, LANES)
    to_a, to_b = call(pack_planes, [side, side], name="pack_planes")(*raw)
    from_a, from_b = swap(to_a, "len", 0), swap(to_b, "len", 1)
    side = (5, ext, HALO, LANES)
    to_c, to_d = call(pack_rows_fine, [side, side], name="pack_rows_fine")(*raw, from_a, from_b)
    from_c, from_d = swap(to_c, "brick", 0), swap(to_d, "brick", 1)

    field, cell = (3, ext, ext_rows, LANES), (ext, ext_rows, LANES)
    own, cells, *fine = call(
        fine_before,
        [(5, half, half_rows, LANES), (2, half // 2, half_rows // 2, LANES)]
        + [field, field, cell, cell, cell],
        [cell, field, (3, half + 2, ext_rows, LANES), (half + 2, ext_rows, LANES)],
        name="fine_before",
    )(*raw, from_a, from_b, from_c, from_d)

    from_a, from_b = swap(own, "len", 0), swap(own, "len", 1)
    side = (5, mid, HALO, LANES)
    to_c, to_d = call(pack_rows_coarse, [side, side], name="pack_rows_coarse")(
        own, from_a, from_b
    )
    from_c, from_d = swap(to_c, "brick", 0), swap(to_d, "brick", 1)

    field1, cell1 = (3, mid, mid_rows, LANES), (mid, mid_rows, LANES)
    depth = half // 2
    lines = 5 * depth
    to_all, *middle = call(
        middle_before,
        [(slabs * bricks * lines // 2, 2, LANES)] + [field1, field1, cell1, cell1, cell1],
        [field1, (3, depth, mid_rows, LANES)],
        name="middle_before",
    )(own, cells, from_a, from_b, from_c, from_d)

    table = lax.all_to_all(to_all, BOTH, 0, 0, tiled=True)
    table = table.reshape(slabs, bricks, lines, LANES)
    window = bricks if bricks <= 8 else 16

    def first_brick(brick):
        return jnp.clip(brick - 4, 0, bricks - window)

    if window < bricks:
        table = lax.dynamic_slice_in_dim(
            table, first_brick(lax.axis_index("brick")), window, axis=1
        )
    planes2 = slabs * depth
    rows2 = -(-(4 * window + 2 * HALO) // 16) * 16
    f2, c2 = (3, planes2, rows2, LANES), (planes2, rows2, LANES)
    f3, c3 = (3, planes2 // 2, rows2 // 2, LANES), (planes2 // 2, rows2 // 2, LANES)
    (out,) = call(
        functools.partial(coarse_and_after, first_brick),
        [forces.shape],
        [f2, c2, c2, c2, c2, f2, (3, planes2 + 4, rows2, LANES)]
        + [f3, c3, c3, c3, c3, (2,) + f3]
        + [(2, rows2, LANES), field1, field1, field, field],
        name="coarse_and_after",
    )(table, *middle, *fine)
    return out


def solution(mesh):
    cells = P("len", "brick", None)
    forces = P(None, "len", "brick", None)
    return jax.shard_map(
        body, mesh=mesh, in_specs=(forces, cells, cells, cells), out_specs=forces, check_vma=False
    )
```

```python
import functools

import jax
import jax.numpy as jnp
from jax import lax
from jax.experimental import pallas as pl
from jax.experimental.pallas import tpu as pltpu
from jax.sharding import PartitionSpec as P

DAMPING = 0.6
COUPLING = 0.2
MASS_TERM = 0.1
PENALTY = 20.0

HALO = 4
LANES = 128
F32 = jnp.float32
BOTH = ("len", "brick")


def lane_ids(shape):
    return lax.broadcasted_iota(jnp.int32, shape, len(shape) - 1)


def turn(x, by, axis):
    return pltpu.roll(x, by % x.shape[axis], axis)


class Lane:
    def __init__(self, rows, wide):
        ids = lane_ids((rows, LANES))
        self.wide = wide
        self.low = jnp.where(ids >= wide, 0.5, 0.0).astype(F32)
        self.high = jnp.where(ids < LANES - wide, 0.5, 0.0).astype(F32)
        self.first = (ids & wide) == 0

    def smooth(self, x):
        return x + self.low * turn(x, self.wide, 1) + self.high * turn(x, -self.wide, 1)

    def pair(self, x):
        return x + swap_lanes(x, self.wide, self.first)

    def rows(self, x):
        pair = x + turn(x, 1, 0)
        return pair + turn(pair, -1, 0)


def swap_lanes(x, by, first):
    return jnp.where(first, turn(x, -by, 1), turn(x, by, 1))


class Packed:
    def __init__(self, bricks, wide):
        shape = (1, bricks, LANES)
        ids = lane_ids(shape)
        line = lax.broadcasted_iota(jnp.int32, shape, 1)
        self.wide, self.across = wide, 4 * wide
        row = ids & (4 - wide)
        top, bottom = row == 0, row == 4 - wide

        def number(mask, value):
            return jnp.where(mask, value, 0.0).astype(F32)

        self.low = number(ids >= self.across, 0.5)
        self.high = number(ids < LANES - self.across, 0.5)
        self.not_top, self.not_bottom = number(~top, 1.0), number(~bottom, 1.0)
        self.top = number(top & (line > 0), 1.0)
        self.bottom = number(bottom & (line < bricks - 1), 1.0)
        self.odd_row, self.odd_lane = number((ids & 1) > 0, 1.0), number((ids & 4) > 0, 1.0)

    def smooth(self, x):
        return x + (self.low * turn(x, self.across, 2) + self.high * turn(x, -self.across, 2))

    def rows(self, x):
        back, ahead = turn(x, self.wide, 2), turn(x, -self.wide, 2)
        if self.wide == 2:
            far_back, far_ahead = ahead, back
        else:
            far_back, far_ahead = turn(x, -3, 2), turn(x, 3, 2)
        before = self.not_top * back + self.top * turn(far_back, 1, 1)
        after = self.not_bottom * ahead + self.bottom * turn(far_ahead, -1, 1)
        return (x + x) + (before + after)

    def pair(self, x):
        for by, is_odd in ((1, self.odd_row), (4, self.odd_lane)):
            x = x + (is_odd * turn(x, by, 2) + (1.0 - is_odd) * turn(x, -by, 2))
        return x

    def planes(self, x):
        none = jnp.zeros_like(x[:1])
        above = jnp.concatenate([x[1:], none], axis=0)
        below = jnp.concatenate([none, x[:-1]], axis=0)
        return (x + x) + (above + below)

    def full(self, x):
        return self.smooth(self.rows(self.planes(x)))

    def terms(self, q, s):
        total = 24.0 * q + self.full(q) + s
        return total + 8.0 * q, DAMPING / (total + (4.0 * COUPLING) * q)

    def defects(self, v, q, weight, source):
        count = q.shape[0]
        stack = [self.planes(x) for x in v] + [self.planes(q * x) for x in v]
        both = self.smooth(self.rows(jnp.concatenate(stack, axis=0)))
        part = [both[i * count : (i + 1) * count] for i in range(6)]
        coupled = (4.0 * COUPLING) * q * (v[0] + v[1] + v[2])
        return [
            source[k] - weight * v[k] + (q * part[k] + part[3 + k]) - coupled for k in range(3)
        ]

    def sweep(self, v, q, weight, step, source):
        r = self.defects(v, q, weight, source)
        return [v[k] + step * r[k] for k in range(3)]

    def restrict(self, x):
        x = x.reshape((x.shape[0] // 2, 2) + x.shape[1:])
        return 0.125 * self.pair(x[:, 0] + x[:, 1])


def twice_planes(x):
    return jnp.concatenate([x[i // 2 : i // 2 + 1] for i in range(2 * x.shape[0])], axis=0)


def smooth_planes(get, p):
    below, here, above = get(p - 1), get(p), get(p + 1)
    total = here + here
    if below is not None:
        total = total + below
    if above is not None:
        total = total + above
    return total


def remember(get):
    seen = {}

    def cached(p):
        if p not in seen:
            seen[p] = get(p)
        return seen[p]

    return cached


def within(get, low, high):
    return lambda p: get(p) if low <= p < high else None


def gathered(field, quarter, planes, bounds, lane):
    low, high = bounds
    q_at = remember(within(lambda p: quarter[p], low, high))
    v_at = [remember(within(lambda p, k=k: field(k, p), low, high)) for k in range(3)]
    w_at = [
        remember(within(lambda p, k=k: q_at(p) * v_at[k](p), low, high)) for k in range(3)
    ]
    for p in planes:
        q = q_at(p)
        sums = []
        for k in range(3):
            x = lane.rows(smooth_planes(v_at[k], p))
            y = lane.rows(smooth_planes(w_at[k], p))
            sums.append(q * lane.smooth(x) + lane.smooth(y))
        yield p, [v_at[k](p) for k in range(3)], q, sums


def defects(field, quarter, weight, source, planes, bounds, lane):
    for p, v, q, sums in gathered(field, quarter, planes, bounds, lane):
        coupled = (4.0 * COUPLING) * q * (v[0] + v[1] + v[2])
        e = weight[p]
        yield p, v, [source[k, p] - e * v[k] + sums[k] - coupled for k in range(3)]


def sweep(field, quarter, weight, step, source, planes, bounds, lane, put):
    for p, v, r in defects(field, quarter, weight, source, planes, bounds, lane):
        s = step[p]
        for k in range(3):
            put(k, p, v[k] + s * r[k])


def stiffness_sum(quarter, planes, bounds, lane):
    q_at = remember(within(lambda p: quarter[p], *bounds))
    for p in planes:
        yield p, 24.0 * q_at(p) + lane.smooth(lane.rows(smooth_planes(q_at, p)))


def step_of(inside, diagonal):
    return jnp.where(inside > 0.0, DAMPING / diagonal, 0.0)


def odd(axis):
    return lax.rem(lax.axis_index(axis), 2) == 1


def vmem(shape):
    return pltpu.VMEM(shape, F32)


def raw_field(forces, modulus, occupancy, bonded, k, p, rows):
    if k < 3:
        return forces[k, p, rows, :]
    if k == 3:
        return modulus[p, rows, :] * occupancy[p, rows, :].astype(F32)
    return MASS_TERM + PENALTY * bonded[p, rows, :].astype(F32)


def pack_planes(forces, modulus, occupancy, bonded, to_a, to_b):
    planes, rows = modulus.shape[0], modulus.shape[1]
    last = planes - HALO
    is_odd = lax.rem(lax.axis_index("len"), 2)
    start_a, start_b = (1 - is_odd) * last, is_odd * last
    for i in range(HALO):
        for k in range(5):
            to_a[k, i] = raw_field(
                forces, modulus, occupancy, bonded, k, start_a + i, slice(0, rows)
            )
            to_b[k, i] = raw_field(
                forces, modulus, occupancy, bonded, k, start_b + i, slice(0, rows)
            )


def extended_rows(own, from_a, from_b, planes, is_odd):
    def get(k, p, rows):
        if p < HALO:
            return jnp.where(is_odd, from_a[k, p, rows, :], from_b[k, p, rows, :])
        if p >= HALO + planes:
            i = p - HALO - planes
            return jnp.where(is_odd, from_b[k, i, rows, :], from_a[k, i, rows, :])
        return own(k, p - HALO, rows)

    return get


def pack_rows_from(get, planes, rows, to_c, to_d):
    is_odd = odd("brick")
    for k in range(5):
        for p in range(planes + 2 * HALO):
            first = get(k, p, slice(0, HALO))
            last = get(k, p, slice(rows - HALO, rows))
            to_c[k, p] = jnp.where(is_odd, first, last)
            to_d[k, p] = jnp.where(is_odd, last, first)


def pack_rows_fine(forces, modulus, occupancy, bonded, from_a, from_b, to_c, to_d):
    planes, rows = modulus.shape[0], modulus.shape[1]
    own = functools.partial(raw_field, forces, modulus, occupancy, bonded)
    pack_rows_from(
        extended_rows(own, from_a, from_b, planes, odd("len")), planes, rows, to_c, to_d
    )


def pack_rows_coarse(own, from_a, from_b, to_c, to_d):
    planes, rows = own.shape[1], own.shape[2]
    get = extended_rows(lambda k, p, r: own[k, p, r, :], from_a, from_b, planes, odd("len"))
    pack_rows_from(get, planes, rows, to_c, to_d)


def spread_rows(get, from_c, from_d, planes, rows, put):
    is_odd = odd("brick")
    for p in range(planes + 2 * HALO):
        for k in range(5):
            low = jnp.where(is_odd, from_c[k, p], from_d[k, p])
            high = jnp.where(is_odd, from_d[k, p], from_c[k, p])
            put(k, p, slice(0, HALO), low)
            put(k, p, slice(HALO, HALO + rows), get(k, p, slice(0, rows)))
            put(k, p, slice(HALO + rows, 2 * HALO + rows), high)


def fine_before(
    forces, modulus, occupancy, bonded, from_a, from_b, from_c, from_d,
    own_coarse, cells, v2, source, quarter, weight, step,
    shift, v1, work, coarse_q,
):
    planes, rows = modulus.shape[0], modulus.shape[1]
    ext_planes, ext_rows = planes + 2 * HALO, rows + 2 * HALO
    lane = Lane(ext_rows, 1)
    own = functools.partial(raw_field, forces, modulus, occupancy, bonded)

    def put(k, p, r, value):
        if k < 3:
            source[k, p, r, :] = value
        elif k == 3:
            quarter[p, r, :] = 0.25 * value
        else:
            shift[p, r, :] = value

    get = extended_rows(own, from_a, from_b, planes, odd("len"))
    spread_rows(get, from_c, from_d, planes, rows, put)

    bounds = (0, ext_planes)
    for p, w in stiffness_sum(quarter, range(1, ext_planes - 1), bounds, lane):
        q, s = quarter[p], shift[p]
        total = w + s
        weight[p] = total + 8.0 * q
        st = step_of(s, total + (4.0 * COUPLING) * q)
        step[p] = st
        for k in range(3):
            v1[k, p] = st * source[k, p]

    def put_v2(k, p, value):
        v2[k, p] = value

    sweep(
        lambda k, p: v1[k, p], quarter, weight, step, source,
        range(2, ext_planes - 2), bounds, lane, put_v2,
    )

    held = {}
    half = rows // 2
    for p, _, r in defects(
        lambda k, p: v2[k, p], quarter, weight, source,
        range(HALO, HALO + planes), bounds, lane,
    ):
        if p % 2 == 0:
            held = r
            continue
        i = (p - HALO) // 2
        for k in range(3):
            work[k, i] = held[k] + r[k]
    for i in range(planes // 2):
        for k in range(3):
            work[k, i] = lane.pair(work[k, i])
    for i in range(planes // 2):
        for k in range(3):
            own_coarse[k, i] = 0.125 * (
                work[k, i, pl.ds(HALO, half, stride=2), :]
                + work[k, i, pl.ds(HALO + 1, half, stride=2), :]
            )

    reach = planes // 2 + 2
    for j in range(reach):
        p = 2 * j + 2
        work[0, j] = lane.pair(quarter[p] + quarter[p + 1])
        coarse_q[j, pl.ds(6, ext_rows // 2), :] = (0.25 * 0.125) * (
            work[0, j, pl.ds(0, ext_rows // 2, stride=2), :]
            + work[0, j, pl.ds(1, ext_rows // 2, stride=2), :]
        )
    for i in range(planes // 2):
        p = HALO + 2 * i
        work[1, i] = lane.pair(shift[p] + shift[p + 1])
    lane1 = Lane(half, 2)
    shift1, q1 = [], []
    for i in range(planes // 2):
        s = 0.125 * (
            work[1, i, pl.ds(HALO, half, stride=2), :]
            + work[1, i, pl.ds(HALO + 1, half, stride=2), :]
        )
        sides = smooth_planes(lambda j: coarse_q[j, pl.ds(7, half), :], i + 1)
        here = smooth_planes(lambda j: coarse_q[j, pl.ds(8, half), :], i + 1)
        others = smooth_planes(lambda j: coarse_q[j, pl.ds(9, half), :], i + 1)
        q = coarse_q[i + 1, pl.ds(8, half), :]
        w = 24.0 * q + lane1.smooth(sides + 2.0 * here + others)
        own_coarse[3, i] = q
        own_coarse[4, i] = w + s
        shift1.append(s)
        q1.append(q)

    quarter_rows = half // 2
    for i in range(planes // 4):
        work[2, 0, pl.ds(0, half), :] = lane1.pair(q1[2 * i] + q1[2 * i + 1])
        work[2, 1, pl.ds(0, half), :] = lane1.pair(shift1[2 * i] + shift1[2 * i + 1])
        cells[0, i] = (0.25 * 0.125) * (
            work[2, 0, pl.ds(0, quarter_rows, stride=2), :]
            + work[2, 0, pl.ds(1, quarter_rows, stride=2), :]
        )
        cells[1, i] = 0.125 * (
            work[2, 1, pl.ds(0, quarter_rows, stride=2), :]
            + work[2, 1, pl.ds(1, quarter_rows, stride=2), :]
        )


def middle_before(
    own, cells, from_a, from_b, from_c, from_d,
    to_all, v2, source, quarter, weight, step,
    v1, work,
):
    planes, rows = own.shape[1], own.shape[2]
    ext_planes, ext_rows = planes + 2 * HALO, rows + 2 * HALO
    lane = Lane(ext_rows, 2)

    def put(k, p, r, value):
        if k < 3:
            source[k, p, r, :] = value
        elif k == 3:
            quarter[p, r, :] = value
        else:
            weight[p, r, :] = value

    get = extended_rows(lambda k, p, r: own[k, p, r, :], from_a, from_b, planes, odd("len"))
    spread_rows(get, from_c, from_d, planes, rows, put)

    for p in range(ext_planes):
        q, total = quarter[p], weight[p]
        st = step_of(total, total + (4.0 * COUPLING) * q)
        step[p] = st
        weight[p] = total + 8.0 * q
        for k in range(3):
            v1[k, p] = st * source[k, p]

    def put_v2(k, p, value):
        v2[k, p] = value

    bounds = (0, ext_planes)
    sweep(
        lambda k, p: v1[k, p], quarter, weight, step, source,
        range(1, ext_planes - 1), bounds, lane, put_v2,
    )
    held = {}
    half = rows // 2
    ids = lane_ids((half, LANES))
    mine = (ids & 3) == lax.broadcasted_iota(jnp.int32, (half, LANES), 0)
    slots = 2 * to_all.shape[0] // (5 * (planes // 2))

    def send(row, value):
        packed = jnp.sum(jnp.where(mine, value, 0.0), axis=0, keepdims=True)
        for s in range(slots):
            at = s * (5 * (planes // 2)) + row
            to_all[at // 2, at % 2 : at % 2 + 1, :] = packed

    for p, _, r in defects(
        lambda k, p: v2[k, p], quarter, weight, source,
        range(HALO, HALO + planes), bounds, lane,
    ):
        if p % 2 == 0:
            held = r
            continue
        i = (p - HALO) // 2
        for k in range(3):
            work[k, i] = held[k] + r[k]
    for i in range(planes // 2):
        for k in range(3):
            work[k, i] = lane.pair(work[k, i])
    for i in range(planes // 2):
        for k in range(3):
            send(
                k * (planes // 2) + i,
                0.125
                * (
                    work[k, i, pl.ds(HALO, half, stride=2), :]
                    + work[k, i, pl.ds(HALO + 1, half, stride=2), :]
                ),
            )
        for k in range(2):
            send((3 + k) * (planes // 2) + i, cells[k, i])


def coarse_and_after(
    bricks_before,
    table, v2_mid, source_mid, quarter_mid, weight_mid, step_mid,
    v2_fine, source_fine, quarter_fine, weight_fine, step_fine,
    out,
    wide2, u_mid, x_mid, u_fine, x_fine,
):
    brick = lax.axis_index("brick")
    slab = lax.axis_index("len")
    slabs, bricks, lines = table.shape[0], table.shape[1], table.shape[2]
    depth = lines // 5
    planes2 = slabs * depth

    def field(f):
        return jnp.stack(
            [table[i // depth, :, f * depth + i % depth, :] for i in range(planes2)], axis=0
        )

    lane2, lane3 = Packed(bricks, 1), Packed(bricks, 2)
    b2, q2, s2 = [field(k) for k in range(3)], field(3), field(4)
    e2, x2 = lane2.terms(q2, s2)
    u2 = lane2.sweep([x2 * b for b in b2], q2, e2, x2, b2)

    rest = lane2.defects(u2, q2, e2, b2)
    joint = lane2.restrict(jnp.concatenate(rest + [0.25 * q2, s2], axis=0))
    count = planes2 // 2
    *b3, q3, s3 = [joint[i * count : (i + 1) * count] for i in range(5)]
    e3, x3 = lane3.terms(q3, s3)
    u3 = [x3 * b for b in b3]
    for _ in range(3):
        u3 = lane3.sweep(u3, q3, e3, x3, b3)

    u2 = [u2[k] + twice_planes(u3[k]) for k in range(3)]
    for _ in range(2):
        u2 = lane2.sweep(u2, q2, e2, x2, b2)
    wide2[...] = jnp.zeros_like(wide2)
    for k in range(3):
        wide2[k, pl.ds(2, planes2), pl.ds(8, bricks), :] = u2[k]

    planes1 = v2_mid.shape[1]
    rows1 = v2_mid.shape[2]
    lane1 = Lane(rows1, 2)
    bounds1 = (0, planes1)
    line_at = brick - bricks_before(brick) + 8
    half_shape = (rows1 // 2, LANES)
    ids, row = lane_ids(half_shape), lax.broadcasted_iota(jnp.int32, half_shape, 0)
    mine = (ids & 3) == ((row + 2) & 3)
    pieces = []
    for k in range(3):
        for i in range(planes1 // 2):
            low, own, high = [
                jnp.broadcast_to(
                    wide2[k, depth * slab + i, pl.ds(line_at + at, 1), :], half_shape
                )
                for at in (-1, 0, 1)
            ]
            piece = jnp.where(row < 2, low, jnp.where(row < 6, own, high))
            pieces.append(jnp.where(mine, piece, 0.0))
    for by in (1, 2):
        first = (ids & by) == 0
        pieces = [x + swap_lanes(x, by, first) for x in pieces]
    for k in range(3):
        for i in range(planes1 // 2):
            piece = pieces[k * (planes1 // 2) + i]
            for half in range(2):
                x_mid[k, i, pl.ds(half, rows1 // 2, stride=2), :] = piece
            both = x_mid[k, i]
            for p in (2 * i, 2 * i + 1):
                if 1 <= p < planes1 - 1:
                    u_mid[k, p] = v2_mid[k, p] + both

    def put_mid(k, p, value):
        x_mid[k, p] = value

    sweep(
        lambda k, p: u_mid[k, p], quarter_mid, weight_mid, step_mid, source_mid,
        range(2, planes1 - 2), bounds1, lane1, put_mid,
    )

    def put_mid_last(k, p, value):
        u_mid[k, p] = value

    sweep(
        lambda k, p: x_mid[k, p], quarter_mid, weight_mid, step_mid, source_mid,
        range(3, planes1 - 3), bounds1, lane1, put_mid_last,
    )

    planes0, rows0 = v2_fine.shape[1], v2_fine.shape[2]
    lane0 = Lane(rows0, 1)
    bounds0 = (0, planes0)
    half_rows = rows0 // 2
    for k in range(3):
        for i in range(3, planes1 - 3):
            piece = u_mid[k, i, pl.ds(2, half_rows), :]
            p = 2 * i - HALO
            for half in range(2):
                x_fine[k, p, pl.ds(half, half_rows, stride=2), :] = piece
            both = x_fine[k, p]
            for at in (p, p + 1):
                u_fine[k, at] = v2_fine[k, at] + both

    def put_fine(k, p, value):
        x_fine[k, p] = value

    sweep(
        lambda k, p: u_fine[k, p], quarter_fine, weight_fine, step_fine, source_fine,
        range(3, planes0 - 3), bounds0, lane0, put_fine,
    )

    def put_out(k, p, value):
        out[k, p - HALO] = value[HALO : rows0 - HALO]

    sweep(
        lambda k, p: x_fine[k, p], quarter_fine, weight_fine, step_fine, source_fine,
        range(HALO, planes0 - HALO), bounds0, lane0, put_out,
    )


def call(kernel, outs, scratch=(), name=None):
    return pl.pallas_call(
        kernel,
        out_shape=[jax.ShapeDtypeStruct(shape, F32) for shape in outs],
        scratch_shapes=[vmem(shape) for shape in scratch],
        compiler_params=pltpu.CompilerParams(vmem_limit_bytes=48 * 1024 * 1024),
        name=name,
    )


def swap(x, axis, first):
    count = lax.axis_size(axis)
    pairs = []
    for i in range(first, count - 1, 2):
        pairs += [(i, i + 1), (i + 1, i)]
    return lax.ppermute(x, axis, pairs)


def body(forces, modulus, occupancy, bonded):
    planes, rows = modulus.shape[0], modulus.shape[1]
    slabs, bricks = lax.axis_size("len"), lax.axis_size("brick")
    raw = (forces, modulus, occupancy, bonded)
    ext, ext_rows = planes + 2 * HALO, rows + 2 * HALO
    half, half_rows = planes // 2, rows // 2
    mid, mid_rows = half + 2 * HALO, half_rows + 2 * HALO

    side = (5, HALO, rows, LANES)
    to_a, to_b = call(pack_planes, [side, side], name="pack_planes")(*raw)
    from_a, from_b = swap(to_a, "len", 0), swap(to_b, "len", 1)
    side = (5, ext, HALO, LANES)
    to_c, to_d = call(pack_rows_fine, [side, side], name="pack_rows_fine")(*raw, from_a, from_b)
    from_c, from_d = swap(to_c, "brick", 0), swap(to_d, "brick", 1)

    field, cell = (3, ext, ext_rows, LANES), (ext, ext_rows, LANES)
    own, cells, *fine = call(
        fine_before,
        [(5, half, half_rows, LANES), (2, half // 2, half_rows // 2, LANES)]
        + [field, field, cell, cell, cell],
        [cell, field, (3, half + 2, ext_rows, LANES), (half + 2, ext_rows, LANES)],
        name="fine_before",
    )(*raw, from_a, from_b, from_c, from_d)

    from_a, from_b = swap(own, "len", 0), swap(own, "len", 1)
    side = (5, mid, HALO, LANES)
    to_c, to_d = call(pack_rows_coarse, [side, side], name="pack_rows_coarse")(
        own, from_a, from_b
    )
    from_c, from_d = swap(to_c, "brick", 0), swap(to_d, "brick", 1)

    field1, cell1 = (3, mid, mid_rows, LANES), (mid, mid_rows, LANES)
    depth = half // 2
    lines = 5 * depth
    to_all, *middle = call(
        middle_before,
        [(slabs * bricks * lines // 2, 2, LANES)] + [field1, field1, cell1, cell1, cell1],
        [field1, (3, depth, mid_rows, LANES)],
        name="middle_before",
    )(own, cells, from_a, from_b, from_c, from_d)

    table = lax.all_to_all(to_all, BOTH, 0, 0, tiled=True)
    table = table.reshape(slabs, bricks, lines, LANES)
    window = bricks if bricks <= 8 else 16

    def first_brick(brick):
        return jnp.clip(brick - 4, 0, bricks - window)

    if window < bricks:
        table = lax.dynamic_slice_in_dim(
            table, first_brick(lax.axis_index("brick")), window, axis=1
        )
    planes2 = slabs * depth
    (out,) = call(
        functools.partial(coarse_and_after, first_brick),
        [forces.shape],
        [(3, planes2 + 4, window + 16, LANES), field1, field1, field, field],
        name="coarse_and_after",
    )(table, *middle, *fine)
    return out


def solution(mesh):
    cells = P("len", "brick", None)
    forces = P(None, "len", "brick", None)
    return jax.shard_map(
        body, mesh=mesh, in_specs=(forces, cells, cells, cells), out_specs=forces, check_vma=False
    )
```

```python
import functools

import jax
import jax.numpy as jnp
from jax import lax
from jax.experimental import pallas as pl
from jax.experimental.pallas import tpu as pltpu
from jax.sharding import PartitionSpec as P

DAMPING = 0.6
COUPLING = 0.2
MASS_TERM = 0.1
PENALTY = 20.0

HALO = 4
WIDE = 12
ROWS = (10, 10, 10, 11, 10)
PLANES = (3, 3, 3, 4, 3)
LANES = 128
F32 = jnp.float32
BOTH = ("len", "brick")


def lane_ids(shape):
    return lax.broadcasted_iota(jnp.int32, shape, len(shape) - 1)


def turn(x, by, axis):
    return pltpu.roll(x, by % x.shape[axis], axis)


class Lane:
    def __init__(self, rows, wide):
        ids = lane_ids((rows, LANES))
        self.wide = wide
        self.low = jnp.where(ids >= wide, 0.5, 0.0).astype(F32)
        self.high = jnp.where(ids < LANES - wide, 0.5, 0.0).astype(F32)
        self.first = (ids & wide) == 0

    def smooth(self, x):
        return x + self.low * turn(x, self.wide, 1) + self.high * turn(x, -self.wide, 1)

    def pair(self, x):
        return x + swap_lanes(x, self.wide, self.first)

    def rows(self, x):
        pair = x + turn(x, 1, 0)
        return pair + turn(pair, -1, 0)


def swap_lanes(x, by, first):
    return jnp.where(first, turn(x, -by, 1), turn(x, by, 1))


class Packed:
    def __init__(self, bricks, wide):
        shape = (1, bricks, LANES)
        ids = lane_ids(shape)
        line = lax.broadcasted_iota(jnp.int32, shape, 1)
        self.wide, self.across = wide, 4 * wide
        row = ids & (4 - wide)
        top, bottom = row == 0, row == 4 - wide

        def number(mask, value):
            return jnp.where(mask, value, 0.0).astype(F32)

        self.low = number(ids >= self.across, 0.5)
        self.high = number(ids < LANES - self.across, 0.5)
        self.not_top, self.not_bottom = number(~top, 1.0), number(~bottom, 1.0)
        self.top = number(top & (line > 0), 1.0)
        self.bottom = number(bottom & (line < bricks - 1), 1.0)
        self.odd_row, self.odd_lane = number((ids & 1) > 0, 1.0), number((ids & 4) > 0, 1.0)

    def smooth(self, x):
        return x + (self.low * turn(x, self.across, 2) + self.high * turn(x, -self.across, 2))

    def rows(self, x):
        back, ahead = turn(x, self.wide, 2), turn(x, -self.wide, 2)
        if self.wide == 2:
            far_back, far_ahead = ahead, back
        else:
            far_back, far_ahead = turn(x, -3, 2), turn(x, 3, 2)
        before = self.not_top * back + self.top * turn(far_back, 1, 1)
        after = self.not_bottom * ahead + self.bottom * turn(far_ahead, -1, 1)
        return (x + x) + (before + after)

    def pair(self, x):
        for by, is_odd in ((1, self.odd_row), (4, self.odd_lane)):
            x = x + (is_odd * turn(x, by, 2) + (1.0 - is_odd) * turn(x, -by, 2))
        return x

    def planes(self, x):
        none = jnp.zeros_like(x[:1])
        above = jnp.concatenate([x[1:], none], axis=0)
        below = jnp.concatenate([none, x[:-1]], axis=0)
        return (x + x) + (above + below)

    def full(self, x):
        return self.smooth(self.rows(self.planes(x)))

    def terms(self, q, s):
        total = 24.0 * q + self.full(q) + s
        return total + 8.0 * q, DAMPING / (total + (4.0 * COUPLING) * q)

    def defects(self, v, q, weight, source):
        count = q.shape[0]
        stack = [self.planes(x) for x in v] + [self.planes(q * x) for x in v]
        both = self.smooth(self.rows(jnp.concatenate(stack, axis=0)))
        part = [both[i * count : (i + 1) * count] for i in range(6)]
        coupled = (4.0 * COUPLING) * q * (v[0] + v[1] + v[2])
        return [
            source[k] - weight * v[k] + (q * part[k] + part[3 + k]) - coupled for k in range(3)
        ]

    def sweep(self, v, q, weight, step, source):
        r = self.defects(v, q, weight, source)
        return [v[k] + step * r[k] for k in range(3)]

    def restrict(self, x):
        x = x.reshape((x.shape[0] // 2, 2) + x.shape[1:])
        return 0.125 * self.pair(x[:, 0] + x[:, 1])


def twice_planes(x):
    return jnp.concatenate([x[i // 2 : i // 2 + 1] for i in range(2 * x.shape[0])], axis=0)


def smooth_planes(get, p):
    below, here, above = get(p - 1), get(p), get(p + 1)
    total = here + here
    if below is not None:
        total = total + below
    if above is not None:
        total = total + above
    return total


def remember(get):
    seen = {}

    def cached(p):
        if p not in seen:
            seen[p] = get(p)
        return seen[p]

    return cached


def within(get, low, high):
    return lambda p: get(p) if low <= p < high else None


def gathered(field, quarter, planes, bounds, lane):
    low, high = bounds
    q_at = remember(within(lambda p: quarter[p], low, high))
    v_at = [remember(within(lambda p, k=k: field(k, p), low, high)) for k in range(3)]
    w_at = [
        remember(within(lambda p, k=k: q_at(p) * v_at[k](p), low, high)) for k in range(3)
    ]
    for p in planes:
        q = q_at(p)
        sums = []
        for k in range(3):
            x = lane.rows(smooth_planes(v_at[k], p))
            y = lane.rows(smooth_planes(w_at[k], p))
            sums.append(q * lane.smooth(x) + lane.smooth(y))
        yield p, [v_at[k](p) for k in range(3)], q, sums


def defects(field, quarter, weight, source, planes, bounds, lane):
    for p, v, q, sums in gathered(field, quarter, planes, bounds, lane):
        coupled = (4.0 * COUPLING) * q * (v[0] + v[1] + v[2])
        e = weight[p]
        yield p, v, [source[k, p] - e * v[k] + sums[k] - coupled for k in range(3)]


def sweep(field, quarter, weight, step, source, planes, bounds, lane, put):
    for p, v, r in defects(field, quarter, weight, source, planes, bounds, lane):
        s = step[p]
        for k in range(3):
            put(k, p, v[k] + s * r[k])


def stiffness_sum(quarter, planes, bounds, lane):
    q_at = remember(within(lambda p: quarter[p], *bounds))
    for p in planes:
        yield p, 24.0 * q_at(p) + lane.smooth(lane.rows(smooth_planes(q_at, p)))


def step_of(inside, diagonal):
    return jnp.where(inside > 0.0, DAMPING / diagonal, 0.0)


def odd(axis):
    return lax.rem(lax.axis_index(axis), 2) == 1


class From:
    def __init__(self, ref, first):
        self.ref, self.first = ref, first

    def __getitem__(self, at):
        if isinstance(at, tuple):
            return self.ref[at[0], at[1] - self.first]
        return self.ref[at - self.first]


def vmem(shape):
    return pltpu.VMEM(shape, F32)


def row_spots(planes):
    spots, at = {}, 0
    for k, reach in enumerate(ROWS):
        for p in range(planes):
            spots[k, p] = slice(at, at + reach)
            at += reach
    return spots, at


def plane_spots(heights):
    spots, at = {}, 0
    for k, count in enumerate(PLANES):
        for i in range(count):
            spots[k, i] = slice(at, at + heights[k])
            at += heights[k]
    return spots, at


def middle_spots(rows):
    return plane_spots([rows] * 5)


def corner_spots():
    return plane_spots([2 * reach for reach in ROWS])


def pack_rows(
    forces, modulus, occupancy, bonded, own, to_c, to_d, to_a, to_b,
    modulus_here, occupancy_here, bonded_here, arrived,
):
    copies = [
        pltpu.make_async_copy(source, target, arrived.at[i])
        for i, (source, target) in enumerate(
            [
                (modulus, modulus_here),
                (occupancy, occupancy_here),
                (bonded, bonded_here),
                (forces, own.at[pl.ds(0, 3)]),
            ]
        )
    ]
    for copy in copies:
        copy.start()
    for copy in copies:
        copy.wait()
    planes, rows = own.shape[1], own.shape[2]
    for p in range(planes):
        own[3, p] = modulus_here[p] * occupancy_here[p].astype(F32)
        own[4, p] = MASS_TERM + PENALTY * bonded_here[p].astype(F32)
    is_odd = odd("brick")
    spots, _ = row_spots(planes)
    for (k, p), spot in spots.items():
        first = own[k, p, 0 : ROWS[k], :]
        last = own[k, p, rows - ROWS[k] : rows, :]
        to_c[spot, :] = jnp.where(is_odd, first, last)
        to_d[spot, :] = jnp.where(is_odd, last, first)
    is_odd = odd("len")
    for (k, i), spot in middle_spots(rows)[0].items():
        first, last = own[k, i], own[k, planes - PLANES[k] + i]
        to_a[spot, :] = jnp.where(is_odd, first, last)
        to_b[spot, :] = jnp.where(is_odd, last, first)


def rows_beside(from_c, from_d):
    is_odd = odd("brick")

    def get(spot):
        c, d = from_c[spot, :], from_d[spot, :]
        return jnp.where(is_odd, c, d), jnp.where(is_odd, d, c)

    return get


def pack_corners(planes, from_c, from_d, middle_a, middle_b, to_a, to_b):
    del middle_a, middle_b
    is_odd = odd("len")
    from_rows, _ = row_spots(planes)
    beside = rows_beside(from_c, from_d)
    for (k, i), spot in corner_spots()[0].items():
        firsts = beside(from_rows[k, i])
        lasts = beside(from_rows[k, planes - PLANES[k] + i])
        for half, (first, last) in enumerate(zip(firsts, lasts)):
            start = spot.start + half * ROWS[k]
            span = slice(start, start + ROWS[k])
            to_a[span, :] = jnp.where(is_odd, first, last)
            to_b[span, :] = jnp.where(is_odd, last, first)


def fine_before(
    own, from_c, from_d, middle_a, middle_b, corner_a, corner_b,
    own_coarse, to_len, cells, v2_kept, source_kept, quarter_kept, weight_kept, step_kept,
    v2, source, quarter, weight, step, shift, v1, work, coarse_q,
):
    planes, rows = own.shape[1], own.shape[2]
    ext_planes, ext_rows = planes + 2 * HALO, rows + 2 * WIDE
    lane = Lane(ext_rows, 1)

    def put(k, p, r, value):
        if k < 3:
            source[k, p, r, :] = value
        elif k == 3:
            quarter[p, r, :] = 0.25 * value
        else:
            shift[p, r, :] = value

    beside = rows_beside(from_c, from_d)
    for (k, p), spot in row_spots(planes)[0].items():
        low, high = beside(spot)
        put(k, HALO + p, slice(WIDE - ROWS[k], WIDE), low)
        put(k, HALO + p, slice(WIDE, WIDE + rows), own[k, p])
        put(k, HALO + p, slice(WIDE + rows, WIDE + rows + ROWS[k]), high)
    is_odd = odd("len")
    kept = slice(WIDE - HALO, WIDE + rows + HALO)
    corners = corner_spots()[0]
    for (k, i), spot in middle_spots(rows)[0].items():
        reach, corner = ROWS[k], corners[k, i].start
        for start, a, b in (
            (WIDE - reach, corner_a[corner : corner + reach, :], corner_b[corner : corner + reach, :]),
            (WIDE, middle_a[spot, :], middle_b[spot, :]),
            (
                WIDE + rows,
                corner_a[corner + reach : corner + 2 * reach, :],
                corner_b[corner + reach : corner + 2 * reach, :],
            ),
        ):
            r = slice(start, start + a.shape[0])
            put(k, HALO - PLANES[k] + i, r, jnp.where(is_odd, a, b))
            put(k, HALO + planes + i, r, jnp.where(is_odd, b, a))

    bounds = (0, ext_planes)
    for p, w in stiffness_sum(quarter, range(1, ext_planes - 1), bounds, lane):
        q, s = quarter[p], shift[p]
        total = w + s
        weight[p] = total + 8.0 * q
        st = step_of(s, total + (4.0 * COUPLING) * q)
        step[p] = st
        for k in range(3):
            v1[k, p] = st * source[k, p]
        if 2 <= p < ext_planes - 2:
            quarter_kept[p - 2] = q[kept]
        if 3 <= p < ext_planes - 3:
            weight_kept[p - 3] = weight[p, kept, :]
            step_kept[p - 3] = st[kept]
            for k in range(3):
                source_kept[k, p - 3] = source[k, p, kept, :]

    def put_v2(k, p, value):
        v2[k, p] = value
        v2_kept[k, p - 2] = value[kept]

    sweep(
        lambda k, p: v1[k, p], quarter, weight, step, source,
        range(2, ext_planes - 2), bounds, lane, put_v2,
    )

    held = {}
    half = rows // 2 + 2 * HALO
    first_row = WIDE - 2 * HALO
    coarse_planes = planes // 2
    for p, _, r in defects(
        lambda k, p: v2[k, p], quarter, weight, source,
        range(HALO, HALO + planes), bounds, lane,
    ):
        if p % 2 == 0:
            held = r
            continue
        i = (p - HALO) // 2
        for k in range(3):
            work[k, i] = held[k] + r[k]
    for i in range(coarse_planes):
        work[4, i] = shift[HALO + 2 * i] + shift[HALO + 2 * i + 1]
    reach = coarse_planes + 2
    for j in range(reach):
        work[3, j] = quarter[2 * j + 2] + quarter[2 * j + 3]
    for k in range(5):
        for i in range(reach if k == 3 else coarse_planes):
            work[k, i] = lane.pair(work[k, i])

    def halved(k, i, start, count):
        return (
            work[k, i, pl.ds(start, count, stride=2), :]
            + work[k, i, pl.ds(start + 1, count, stride=2), :]
        )

    for i in range(coarse_planes):
        for k in range(3):
            own_coarse[k, i] = 0.125 * halved(k, i, first_row, half)

    for j in range(reach):
        coarse_q[j, pl.ds(7, half + 2), :] = (0.25 * 0.125) * halved(3, j, first_row - 2, half + 2)
    lane1 = Lane(half, 2)
    shift1, q1 = [], []
    for i in range(coarse_planes):
        s = 0.125 * halved(4, i, first_row, half)
        sides = smooth_planes(lambda j: coarse_q[j, pl.ds(7, half), :], i + 1)
        here = smooth_planes(lambda j: coarse_q[j, pl.ds(8, half), :], i + 1)
        others = smooth_planes(lambda j: coarse_q[j, pl.ds(9, half), :], i + 1)
        q = coarse_q[i + 1, pl.ds(8, half), :]
        w = 24.0 * q + lane1.smooth(sides + 2.0 * here + others)
        own_coarse[3, i] = q
        own_coarse[4, i] = jnp.where(s > 0.0, w + s, 0.0)
        shift1.append(s)
        q1.append(q)

    even = (lane_ids((half, LANES)) & 1) == 0
    for k in range(5):
        for i in range(coarse_planes // 2):
            to_len[k, i] = jnp.where(even, own_coarse[k, 2 * i], own_coarse[k, 2 * i + 1])

    for i in range(coarse_planes // 2):
        for f, (values, scale) in enumerate(((q1, 0.25 * 0.125), (shift1, 0.125))):
            work[f, i, pl.ds(0, half), :] = lane1.pair(values[2 * i] + values[2 * i + 1])
            cells[f, i] = scale * (
                work[f, i, pl.ds(HALO, rows // 4, stride=2), :]
                + work[f, i, pl.ds(HALO + 1, rows // 4, stride=2), :]
            )


def middle_before(
    own, cells, from_a, from_b,
    to_all, v2, source, quarter, weight, step,
    v1, work,
):
    planes, ext_rows = own.shape[1], own.shape[2]
    rows = ext_rows - 2 * HALO
    ext_planes = planes + 2 * HALO
    lane = Lane(ext_rows, 2)

    def put(k, p, value):
        if k < 3:
            source[k, p] = value
        elif k == 3:
            quarter[p] = value
        else:
            weight[p] = value

    is_odd = odd("len")
    even = (lane_ids((ext_rows, LANES)) & 1) == 0
    for k in range(5):
        for p in range(planes):
            put(k, HALO + p, own[k, p])
        for i in range(HALO // 2):
            a, b = from_a[k, i], from_b[k, i]
            for start, x in (
                (0, jnp.where(is_odd, a, b)),
                (HALO + planes, jnp.where(is_odd, b, a)),
            ):
                put(k, start + 2 * i, jnp.where(even, x, turn(x, 1, 1)))
                put(k, start + 2 * i + 1, jnp.where(even, turn(x, -1, 1), x))

    for p in range(ext_planes):
        q, total = quarter[p], weight[p]
        st = step_of(total, total + (4.0 * COUPLING) * q)
        step[p] = st
        weight[p] = total + 8.0 * q
        for k in range(3):
            v1[k, p] = st * source[k, p]

    def put_v2(k, p, value):
        v2[k, p] = value

    bounds = (0, ext_planes)
    sweep(
        lambda k, p: v1[k, p], quarter, weight, step, source,
        range(1, ext_planes - 1), bounds, lane, put_v2,
    )
    held = {}
    half = rows // 2
    ids = lane_ids((half, LANES))
    mine = (ids & 3) == lax.broadcasted_iota(jnp.int32, (half, LANES), 0)
    lines = 5 * (planes // 2)
    slots = to_all.shape[0] // lines

    def send(row, value):
        packed = jnp.sum(jnp.where(mine, value, 0.0), axis=0, keepdims=True)
        for s in range(slots):
            to_all[s * lines + row : s * lines + row + 1, :] = packed

    for p, _, r in defects(
        lambda k, p: v2[k, p], quarter, weight, source,
        range(HALO, HALO + planes), bounds, lane,
    ):
        if p % 2 == 0:
            held = r
            continue
        i = (p - HALO) // 2
        for k in range(3):
            work[k, i] = held[k] + r[k]
    for i in range(planes // 2):
        for k in range(3):
            work[k, i] = lane.pair(work[k, i])
    for i in range(planes // 2):
        for k in range(3):
            send(
                k * (planes // 2) + i,
                0.125
                * (
                    work[k, i, pl.ds(HALO, half, stride=2), :]
                    + work[k, i, pl.ds(HALO + 1, half, stride=2), :]
                ),
            )
        for k in range(2):
            send((3 + k) * (planes // 2) + i, cells[k, i])


def coarse_and_after(
    bricks_before,
    table, v2_mid, source_mid, quarter_mid, weight_mid, step_mid,
    v2_fine, source_fine, quarter_fine, weight_fine, step_fine,
    out,
    wide2, u_mid, x_mid, u_fine, x_fine,
):
    brick = lax.axis_index("brick")
    slab = lax.axis_index("len")
    bricks, planes2 = wide2.shape[2] - 16, wide2.shape[1] - 4
    depth = (v2_mid.shape[1] - 2 * HALO) // 2
    lines = 5 * depth

    def field(f):
        return jnp.stack(
            [
                table[pl.ds((i // depth) * bricks * lines + f * depth + i % depth, bricks, stride=lines), :]
                for i in range(planes2)
            ],
            axis=0,
        )

    lane2, lane3 = Packed(bricks, 1), Packed(bricks, 2)
    b2, q2, s2 = [field(k) for k in range(3)], field(3), field(4)
    e2, x2 = lane2.terms(q2, s2)
    u2 = lane2.sweep([x2 * b for b in b2], q2, e2, x2, b2)

    rest = lane2.defects(u2, q2, e2, b2)
    joint = lane2.restrict(jnp.concatenate(rest + [0.25 * q2, s2], axis=0))
    count = planes2 // 2
    *b3, q3, s3 = [joint[i * count : (i + 1) * count] for i in range(5)]
    e3, x3 = lane3.terms(q3, s3)
    u3 = [x3 * b for b in b3]
    for _ in range(3):
        u3 = lane3.sweep(u3, q3, e3, x3, b3)

    u2 = [u2[k] + twice_planes(u3[k]) for k in range(3)]
    for _ in range(2):
        u2 = lane2.sweep(u2, q2, e2, x2, b2)
    wide2[...] = jnp.zeros_like(wide2)
    for k in range(3):
        wide2[k, pl.ds(2, planes2), pl.ds(8, bricks), :] = u2[k]

    v2_fine, quarter_fine = From(v2_fine, 2), From(quarter_fine, 2)
    source_fine, weight_fine, step_fine = [
        From(x, 3) for x in (source_fine, weight_fine, step_fine)
    ]
    planes1 = v2_mid.shape[1]
    rows1 = v2_mid.shape[2]
    lane1 = Lane(rows1, 2)
    bounds1 = (0, planes1)
    line_at = brick - bricks_before(brick) + 8
    half_shape = (rows1 // 2, LANES)
    ids, row = lane_ids(half_shape), lax.broadcasted_iota(jnp.int32, half_shape, 0)
    mine = (ids & 3) == ((row + 2) & 3)
    pieces = []
    for k in range(3):
        for i in range(planes1 // 2):
            low, own, high = [
                jnp.broadcast_to(
                    wide2[k, depth * slab + i, pl.ds(line_at + at, 1), :], half_shape
                )
                for at in (-1, 0, 1)
            ]
            piece = jnp.where(row < 2, low, jnp.where(row < 6, own, high))
            pieces.append(jnp.where(mine, piece, 0.0))
    for by in (1, 2):
        first = (ids & by) == 0
        pieces = [x + swap_lanes(x, by, first) for x in pieces]
    for k in range(3):
        for i in range(planes1 // 2):
            piece = pieces[k * (planes1 // 2) + i]
            for half in range(2):
                x_mid[k, i, pl.ds(half, rows1 // 2, stride=2), :] = piece
            both = x_mid[k, i]
            for p in (2 * i, 2 * i + 1):
                if 1 <= p < planes1 - 1:
                    u_mid[k, p] = v2_mid[k, p] + both

    def put_mid(k, p, value):
        x_mid[k, p] = value

    sweep(
        lambda k, p: u_mid[k, p], quarter_mid, weight_mid, step_mid, source_mid,
        range(2, planes1 - 2), bounds1, lane1, put_mid,
    )

    def put_mid_last(k, p, value):
        u_mid[k, p] = value

    sweep(
        lambda k, p: x_mid[k, p], quarter_mid, weight_mid, step_mid, source_mid,
        range(3, planes1 - 3), bounds1, lane1, put_mid_last,
    )

    planes0, rows0 = x_fine.shape[1], x_fine.shape[2]
    lane0 = Lane(rows0, 1)
    bounds0 = (0, planes0)
    half_rows = rows0 // 2
    for k in range(3):
        for i in range(3, planes1 - 3):
            piece = u_mid[k, i, pl.ds(2, half_rows), :]
            p = 2 * i - HALO
            for half in range(2):
                x_fine[k, p, pl.ds(half, half_rows, stride=2), :] = piece
            both = x_fine[k, p]
            for at in (p, p + 1):
                u_fine[k, at] = v2_fine[k, at] + both

    def put_fine(k, p, value):
        x_fine[k, p] = value

    sweep(
        lambda k, p: u_fine[k, p], quarter_fine, weight_fine, step_fine, source_fine,
        range(3, planes0 - 3), bounds0, lane0, put_fine,
    )

    def put_out(k, p, value):
        out[k, p - HALO] = value[HALO : rows0 - HALO]

    sweep(
        lambda k, p: x_fine[k, p], quarter_fine, weight_fine, step_fine, source_fine,
        range(HALO, planes0 - HALO), bounds0, lane0, put_out,
    )


def call(kernel, outs, scratch=(), name=None, **more):
    return pl.pallas_call(
        kernel,
        out_shape=[jax.ShapeDtypeStruct(shape, F32) for shape in outs],
        scratch_shapes=[vmem(x) if isinstance(x, tuple) else x for x in scratch],
        compiler_params=pltpu.CompilerParams(vmem_limit_bytes=40 * 1024 * 1024),
        name=name,
        **more,
    )


def swap(x, axis, first):
    count = lax.axis_size(axis)
    pairs = []
    for i in range(first, count - 1, 2):
        pairs += [(i, i + 1), (i + 1, i)]
    return lax.ppermute(x, axis, pairs)


def body(forces, modulus, occupancy, bonded):
    planes, rows = modulus.shape[0], modulus.shape[1]
    slabs, bricks = lax.axis_size("len"), lax.axis_size("brick")
    ext, ext_rows = planes + 2 * HALO, rows + 2 * WIDE
    half, half_rows = planes // 2, rows // 2
    mid, mid_rows = half + 2 * HALO, half_rows + 2 * HALO

    side, block = (row_spots(planes)[1], LANES), (planes, rows, LANES)
    middle_side, corner = (middle_spots(rows)[1], LANES), (corner_spots()[1], LANES)
    here = [
        pltpu.with_memory_space_constraint(x, pltpu.HBM)
        for x in (forces, modulus, occupancy, bonded)
    ]
    own, to_c, to_d, to_a, to_b = call(
        pack_rows,
        [(5,) + block, side, side, middle_side, middle_side],
        [block, pltpu.VMEM(block, jnp.int32), pltpu.VMEM(block, jnp.int32)]
        + [pltpu.SemaphoreType.DMA((4,))],
        name="pack_rows",
        in_specs=[pl.BlockSpec(memory_space=pltpu.HBM)] * 4,
    )(*here)
    from_c, from_d = swap(to_c, "brick", 0), swap(to_d, "brick", 1)
    middle_a, middle_b = swap(to_a, "len", 0), swap(to_b, "len", 1)
    to_a, to_b = call(
        functools.partial(pack_corners, planes),
        [corner, corner],
        name="pack_corners",
        in_specs=[pl.BlockSpec(memory_space=pltpu.VMEM)] * 2
        + [pl.BlockSpec(memory_space=pl.ANY)] * 2,
    )(from_c, from_d, middle_a, middle_b)
    corner_a, corner_b = swap(to_a, "len", 0), swap(to_b, "len", 1)

    field, cell = (3, ext, ext_rows, LANES), (ext, ext_rows, LANES)
    line = (rows + 2 * HALO, LANES)
    own, to_len, cells, *fine = call(
        fine_before,
        [(5, half, mid_rows, LANES), (5, half // 2, mid_rows, LANES)]
        + [(2, half // 2, half_rows // 2, LANES)]
        + [(3, ext - 4) + line, (3, ext - 6) + line, (ext - 4,) + line]
        + [(ext - 6,) + line] * 2,
        [field, field, cell, cell, cell, cell, field, (5, half + 2, ext_rows, LANES), (half + 2, mid_rows + 16, LANES)],
        name="fine_before",
    )(own, from_c, from_d, middle_a, middle_b, corner_a, corner_b)
    from_a, from_b = swap(to_len, "len", 0), swap(to_len, "len", 1)

    field1, cell1 = (3, mid, mid_rows, LANES), (mid, mid_rows, LANES)
    depth = half // 2
    lines = 5 * depth
    to_all, *middle = call(
        middle_before,
        [(slabs * bricks * lines, LANES)] + [field1, field1, cell1, cell1, cell1],
        [field1, (3, depth, mid_rows, LANES)],
        name="middle_before",
    )(own, cells, from_a, from_b)

    to_all = to_all.reshape(-1, 2, LANES)
    table = lax.all_to_all(to_all, BOTH, 0, 0, tiled=True).reshape(-1, LANES)
    window = bricks if bricks <= 8 else 16

    def first_brick(brick):
        return jnp.clip(brick - 4, 0, bricks - window)

    if window < bricks:
        table = lax.dynamic_slice_in_dim(
            table.reshape(slabs, bricks * lines, LANES),
            first_brick(lax.axis_index("brick")) * lines, window * lines, axis=1,
        ).reshape(slabs * window * lines, LANES)
    planes2 = slabs * depth
    (out,) = call(
        functools.partial(coarse_and_after, first_brick),
        [forces.shape],
        [(3, planes2 + 4, window + 16, LANES), field1, field1]
        + [(3, ext, rows + 2 * HALO, LANES)] * 2,
        name="coarse_and_after",
    )(table, *middle, *fine)
    return out


def solution(mesh):
    cells = P("len", "brick", None)
    forces = P(None, "len", "brick", None)
    return jax.shard_map(
        body, mesh=mesh, in_specs=(forces, cells, cells, cells), out_specs=forces, check_vma=False
    )
```

```python
import functools

import jax
import jax.numpy as jnp
from jax import lax
from jax.experimental import pallas as pl
from jax.experimental.pallas import tpu as pltpu
from jax.sharding import PartitionSpec as P

DAMPING = 0.6
COUPLING = 0.2
MASS_TERM = 0.1
PENALTY = 20.0

HALO = 4
WIDE = 12
ROWS = (10, 10, 10, 11, 10)
PLANES = (3, 3, 3, 4, 3)
LANES = 128
ROW = 32
F32 = jnp.float32
BOTH = ("len", "brick")


def lane_ids(shape):
    return lax.broadcasted_iota(jnp.int32, shape, len(shape) - 1)


def turn(x, by, axis):
    return pltpu.roll(x, by % x.shape[axis], axis)


def pick(x, lanes):
    return jnp.take_along_axis(x, lanes, axis=1, mode="promise_in_bounds")


class Lane:
    def __init__(self, rows, wide):
        ids = lane_ids((rows, LANES))
        self.wide = wide
        self.low = jnp.where(ids >= wide, 0.5, 0.0).astype(F32)
        self.high = jnp.where(ids < LANES - wide, 0.5, 0.0).astype(F32)
        self.first = (ids & wide) == 0

    def smooth(self, x):
        return x + self.low * turn(x, self.wide, 1) + self.high * turn(x, -self.wide, 1)

    def pair(self, x):
        return x + swap_lanes(x, self.wide, self.first)

    def rows(self, x):
        pair = x + turn(x, 1, 0)
        return pair + turn(pair, -1, 0)


def swap_lanes(x, by, first):
    return jnp.where(first, turn(x, -by, 1), turn(x, by, 1))


class Packed:
    def __init__(self, bricks, wide):
        shape = (1, bricks, LANES)
        ids = lane_ids(shape)
        line = lax.broadcasted_iota(jnp.int32, shape, 1)
        self.wide = wide
        top, bottom = ids < ROW * wide, ids >= LANES - ROW * wide

        def number(mask, value):
            return jnp.where(mask, value, 0.0).astype(F32)

        self.low = number((ids & (ROW - 1)) >= wide, 0.5)
        self.high = number((ids & (ROW - 1)) < ROW - wide, 0.5)
        self.not_top, self.not_bottom = number(~top, 1.0), number(~bottom, 1.0)
        self.top = number(top & (line > 0), 1.0)
        self.bottom = number(bottom & (line < bricks - 1), 1.0)
        self.odd_row, self.odd_lane = number((ids & ROW) > 0, 1.0), number((ids & 1) > 0, 1.0)

    def smooth(self, x):
        return x + (self.low * turn(x, self.wide, 2) + self.high * turn(x, -self.wide, 2))

    def rows(self, x):
        back = turn(x, ROW * self.wide, 2)
        ahead = back if self.wide == 2 else turn(x, -ROW, 2)
        before = self.not_top * back + self.top * turn(back, 1, 1)
        after = self.not_bottom * ahead + self.bottom * turn(ahead, -1, 1)
        return (x + x) + (before + after)

    def pair(self, x):
        for by, is_odd in ((ROW, self.odd_row), (1, self.odd_lane)):
            x = x + (is_odd * turn(x, by, 2) + (1.0 - is_odd) * turn(x, -by, 2))
        return x

    def planes(self, x):
        none = jnp.zeros_like(x[:1])
        above = jnp.concatenate([x[1:], none], axis=0)
        below = jnp.concatenate([none, x[:-1]], axis=0)
        return (x + x) + (above + below)

    def full(self, x):
        return self.smooth(self.rows(self.planes(x)))

    def terms(self, q, s):
        total = 24.0 * q + self.full(q) + s
        return total + 8.0 * q, DAMPING / (total + (4.0 * COUPLING) * q)

    def defects(self, v, q, weight, source):
        count = q.shape[0]
        stack = [self.planes(x) for x in v] + [self.planes(q * x) for x in v]
        both = self.smooth(self.rows(jnp.concatenate(stack, axis=0)))
        part = [both[i * count : (i + 1) * count] for i in range(6)]
        coupled = (4.0 * COUPLING) * q * (v[0] + v[1] + v[2])
        return [
            source[k] - weight * v[k] + (q * part[k] + part[3 + k]) - coupled for k in range(3)
        ]

    def sweep(self, v, q, weight, step, source):
        r = self.defects(v, q, weight, source)
        return [v[k] + step * r[k] for k in range(3)]

    def restrict(self, x):
        x = x.reshape((x.shape[0] // 2, 2) + x.shape[1:])
        return 0.125 * self.pair(x[:, 0] + x[:, 1])


def twice_planes(x):
    return jnp.concatenate([x[i // 2 : i // 2 + 1] for i in range(2 * x.shape[0])], axis=0)


def smooth_planes(get, p):
    below, here, above = get(p - 1), get(p), get(p + 1)
    total = here + here
    if below is not None:
        total = total + below
    if above is not None:
        total = total + above
    return total


def remember(get):
    seen = {}

    def cached(p):
        if p not in seen:
            seen[p] = get(p)
        return seen[p]

    return cached


def within(get, low, high):
    return lambda p: get(p) if low <= p < high else None


def gathered(field, quarter, planes, bounds, lane):
    low, high = bounds
    q_at = remember(within(lambda p: quarter[p], low, high))
    v_at = [remember(within(lambda p, k=k: field(k, p), low, high)) for k in range(3)]
    w_at = [
        remember(within(lambda p, k=k: q_at(p) * v_at[k](p), low, high)) for k in range(3)
    ]
    for p in planes:
        q = q_at(p)
        sums = []
        for k in range(3):
            x = lane.rows(smooth_planes(v_at[k], p))
            y = lane.rows(smooth_planes(w_at[k], p))
            sums.append(q * lane.smooth(x) + lane.smooth(y))
        yield p, [v_at[k](p) for k in range(3)], q, sums


def defects(field, quarter, weight, source, planes, bounds, lane):
    for p, v, q, sums in gathered(field, quarter, planes, bounds, lane):
        coupled = (4.0 * COUPLING) * q * (v[0] + v[1] + v[2])
        e = weight[p]
        yield p, v, [source[k, p] - e * v[k] + sums[k] - coupled for k in range(3)]


def sweep(field, quarter, weight, step, source, planes, bounds, lane, put):
    for p, v, r in defects(field, quarter, weight, source, planes, bounds, lane):
        s = step[p]
        for k in range(3):
            put(k, p, v[k] + s * r[k])


def stiffness_sum(quarter, planes, bounds, lane):
    q_at = remember(within(lambda p: quarter[p], *bounds))
    for p in planes:
        yield p, 24.0 * q_at(p) + lane.smooth(lane.rows(smooth_planes(q_at, p)))


def step_of(inside, diagonal):
    return jnp.where(inside > 0.0, DAMPING / diagonal, 0.0)


def odd(axis):
    return lax.rem(lax.axis_index(axis), 2) == 1


class From:
    def __init__(self, ref, first):
        self.ref, self.first = ref, first

    def __getitem__(self, at):
        if isinstance(at, tuple):
            return self.ref[at[0], at[1] - self.first]
        return self.ref[at - self.first]


class Either:
    def __init__(self, inner, span, outer):
        self.inner, self.span, self.outer = From(inner, span[0]), span, outer

    def __getitem__(self, at):
        p = at[1] if isinstance(at, tuple) else at
        return self.inner[at] if p in self.span else self.outer[at]


def vmem(shape):
    return pltpu.VMEM(shape, F32)


def row_spots(planes):
    spots, at = {}, 0
    for k, reach in enumerate(ROWS):
        for p in range(planes):
            spots[k, p] = slice(at, at + reach)
            at += reach
    return spots, at


def plane_spots(heights):
    spots, at = {}, 0
    for k, count in enumerate(PLANES):
        for i in range(count):
            spots[k, i] = slice(at, at + heights[k])
            at += heights[k]
    return spots, at


def middle_spots(rows):
    return plane_spots([rows] * 5)


def corner_spots():
    spots, at = {}, 0
    for k, count in enumerate(PLANES):
        for distance in range(1, count + 1):
            reach = ROWS[k] if distance < count else count
            spots[k, distance] = at, reach
            at += 2 * reach
    return spots, at


def pack_rows(
    forces, modulus, occupancy, bonded, own, to_c, to_d, to_a, to_b,
    modulus_here, occupancy_here, bonded_here, arrived,
):
    copies = [
        pltpu.make_async_copy(source, target, arrived.at[i])
        for i, (source, target) in enumerate(
            [
                (modulus, modulus_here),
                (occupancy, occupancy_here),
                (bonded, bonded_here),
                (forces, own.at[pl.ds(0, 3)]),
            ]
        )
    ]
    for copy in copies:
        copy.start()
    for copy in copies:
        copy.wait()
    planes, rows = own.shape[1], own.shape[2]
    for p in range(planes):
        own[3, p] = modulus_here[p] * occupancy_here[p].astype(F32)
        own[4, p] = MASS_TERM + PENALTY * bonded_here[p].astype(F32)
    is_odd = odd("brick")
    spots, _ = row_spots(planes)
    for (k, p), spot in spots.items():
        first = own[k, p, 0 : ROWS[k], :]
        last = own[k, p, rows - ROWS[k] : rows, :]
        to_c[spot, :] = jnp.where(is_odd, first, last)
        to_d[spot, :] = jnp.where(is_odd, last, first)
    is_odd = odd("len")
    for (k, i), spot in middle_spots(rows)[0].items():
        first, last = own[k, i], own[k, planes - PLANES[k] + i]
        to_a[spot, :] = jnp.where(is_odd, first, last)
        to_b[spot, :] = jnp.where(is_odd, last, first)


def rows_beside(from_c, from_d):
    is_odd = odd("brick")

    def get(spot, reach):
        low, high = slice(spot.stop - reach, spot.stop), slice(spot.start, spot.start + reach)
        return (
            jnp.where(is_odd, from_c[low, :], from_d[low, :]),
            jnp.where(is_odd, from_d[high, :], from_c[high, :]),
        )

    return get


def pack_corners(planes, from_c, middle_b, from_d, middle_a, to_a, to_b):
    del middle_a, middle_b
    is_odd = odd("len")
    from_rows, _ = row_spots(planes)
    beside = rows_beside(from_c, from_d)
    for (k, distance), (at, reach) in corner_spots()[0].items():
        firsts = beside(from_rows[k, distance - 1], reach)
        lasts = beside(from_rows[k, planes - distance], reach)
        for half, (first, last) in enumerate(zip(firsts, lasts)):
            span = slice(at + half * reach, at + (half + 1) * reach)
            to_a[span, :] = jnp.where(is_odd, first, last)
            to_b[span, :] = jnp.where(is_odd, last, first)


def inner_planes(planes):
    return [range(HALO + i, HALO + planes - i) for i in (1, 2, 3)]


def fine_inner(
    own, from_c, from_d, to_a,
    source, quarter, shift, weight, step, v1, v2, rest,
):
    del to_a
    planes, rows = own.shape[1], own.shape[2]
    lane = Lane(rows + 2 * WIDE, 1)
    beside = rows_beside(from_c, from_d)

    def put(k, p, r, value):
        if k < 3:
            source[k, p, r, :] = value
        elif k == 3:
            quarter[p, r, :] = 0.25 * value
        else:
            shift[p, r, :] = value

    for (k, p), spot in row_spots(planes)[0].items():
        low, high = beside(spot, ROWS[k])
        put(k, p, slice(WIDE - ROWS[k], WIDE), low)
        put(k, p, slice(WIDE, WIDE + rows), own[k, p])
        put(k, p, slice(WIDE + rows, WIDE + rows + ROWS[k]), high)

    weighed, swept, left = inner_planes(planes)
    bounds = (HALO, HALO + planes)
    source_at, quarter_at = From(source, HALO), From(quarter, HALO)
    for p, w in stiffness_sum(quarter_at, weighed, bounds, lane):
        q, s, i = quarter_at[p], shift[p - HALO], p - weighed[0]
        total = w + s
        weight[i] = total + 8.0 * q
        st = step_of(s, total + (4.0 * COUPLING) * q)
        step[i] = st
        for k in range(3):
            v1[k, i] = st * source_at[k, p]
    weight_at, step_at = From(weight, weighed[0]), From(step, weighed[0])

    def put_v2(k, p, value):
        v2[k, p - swept[0]] = value

    v1_at, v2_at = From(v1, weighed[0]), From(v2, swept[0])
    sweep(
        lambda k, p: v1_at[k, p], quarter_at, weight_at, step_at, source_at,
        swept, (weighed[0], weighed[-1] + 1), lane, put_v2,
    )
    for p, _, r in defects(
        lambda k, p: v2_at[k, p], quarter_at, weight_at, source_at,
        left, (swept[0], swept[-1] + 1), lane,
    ):
        for k in range(3):
            rest[k, p - left[0]] = r[k]


def fine_before(
    source_in, quarter_in, shift_in, weight_in, step_in, v1_in, v2_in, rest_in,
    middle_b, middle_a, corner_b, corner_a,
    own_coarse, to_len, cells, v2_kept, source_kept, quarter_kept, weight_kept, step_kept,
    v2_out, source_out, quarter_out, weight_out, step_out, shift_out, v1_out, work, coarse_q,
):
    planes, ext_rows = quarter_in.shape[0], quarter_in.shape[1]
    ext_planes, rows = planes + 2 * HALO, ext_rows - 2 * WIDE
    lane = Lane(ext_rows, 1)

    def put(k, p, r, value):
        if k < 3:
            source_out[k, p, r, :] = value
        elif k == 3:
            quarter_out[p, r, :] = 0.25 * value
        else:
            shift_out[p, r, :] = value

    is_odd = odd("len")
    def put_both(k, distance, start, low, high):
        r = slice(start, start + low.shape[0])
        put(k, HALO - distance, r, low)
        put(k, HALO + planes - 1 + distance, r, high)

    def sides(a, b):
        return jnp.where(is_odd, a, b), jnp.where(is_odd, b, a)

    spots = middle_spots(rows)[0]
    for k, count in enumerate(PLANES):
        for distance in range(1, count + 1):
            low = sides(*[x[spots[k, count - distance], :] for x in (middle_a, middle_b)])[0]
            high = sides(*[x[spots[k, distance - 1], :] for x in (middle_a, middle_b)])[1]
            put_both(k, distance, WIDE, low, high)
    for (k, distance), (at, reach) in corner_spots()[0].items():
        for half, start in enumerate((WIDE - reach, WIDE + rows)):
            span = slice(at + half * reach, at + (half + 1) * reach)
            put_both(k, distance, start, *sides(corner_a[span, :], corner_b[span, :]))

    weighed, swept, left = inner_planes(planes)
    here = range(HALO, HALO + planes)
    source, quarter, shift = [
        Either(x, here, y)
        for x, y in ((source_in, source_out), (quarter_in, quarter_out), (shift_in, shift_out))
    ]
    weight, step, v1 = [
        Either(x, weighed, y)
        for x, y in ((weight_in, weight_out), (step_in, step_out), (v1_in, v1_out))
    ]
    v2 = Either(v2_in, swept, v2_out)
    kept = slice(WIDE - HALO, WIDE + rows + HALO)

    bounds = (0, ext_planes)
    others = [p for p in range(1, ext_planes - 1) if p not in weighed]
    for p, w in stiffness_sum(quarter, others, bounds, lane):
        q, s = quarter[p], shift[p]
        total = w + s
        weight_out[p] = total + 8.0 * q
        st = step_of(s, total + (4.0 * COUPLING) * q)
        step_out[p] = st
        for k in range(3):
            v1_out[k, p] = st * source[k, p]

    def put_v2(k, p, value):
        v2_out[k, p] = value

    sweep(
        lambda k, p: v1[k, p], quarter, weight, step, source,
        [p for p in range(2, ext_planes - 2) if p not in swept], bounds, lane, put_v2,
    )

    half = rows // 2 + 2 * HALO
    first_row = WIDE - 2 * HALO
    coarse_planes = planes // 2
    rest = {p: [rest_in[k, p - left[0]] for k in range(3)] for p in left}
    for p, _, r in defects(
        lambda k, p: v2[k, p], quarter, weight, source,
        [p for p in here if p not in left], bounds, lane,
    ):
        rest[p] = r
    for i in range(coarse_planes):
        p = HALO + 2 * i
        for k in range(3):
            work[k, i] = rest[p][k] + rest[p + 1][k]
    for i in range(coarse_planes):
        work[4, i] = shift[HALO + 2 * i] + shift[HALO + 2 * i + 1]
    reach = coarse_planes + 2
    for j in range(reach):
        work[3, j] = quarter[2 * j + 2] + quarter[2 * j + 3]
    for k in range(5):
        for i in range(reach if k == 3 else coarse_planes):
            work[k, i] = lane.pair(work[k, i])

    def halved(k, i, start, count):
        return (
            work[k, i, pl.ds(start, count, stride=2), :]
            + work[k, i, pl.ds(start + 1, count, stride=2), :]
        )

    for i in range(coarse_planes):
        for k in range(3):
            own_coarse[k, i] = 0.125 * halved(k, i, first_row, half)

    for j in range(reach):
        coarse_q[j, pl.ds(7, half + 2), :] = (0.25 * 0.125) * halved(3, j, first_row - 2, half + 2)
    lane1 = Lane(half, 2)
    shift1, q1 = [], []
    for i in range(coarse_planes):
        s = 0.125 * halved(4, i, first_row, half)
        sides = smooth_planes(lambda j: coarse_q[j, pl.ds(7, half), :], i + 1)
        here = smooth_planes(lambda j: coarse_q[j, pl.ds(8, half), :], i + 1)
        others = smooth_planes(lambda j: coarse_q[j, pl.ds(9, half), :], i + 1)
        q = coarse_q[i + 1, pl.ds(8, half), :]
        w = 24.0 * q + lane1.smooth(sides + 2.0 * here + others)
        own_coarse[3, i] = q
        own_coarse[4, i] = jnp.where(s > 0.0, w + s, 0.0)
        shift1.append(s)
        q1.append(q)

    even = (lane_ids((half, LANES)) & 1) == 0
    for k in range(5):
        for i in range(coarse_planes // 2):
            to_len[k, i] = jnp.where(even, own_coarse[k, 2 * i], own_coarse[k, 2 * i + 1])

    for i in range(coarse_planes // 2):
        for f, (values, scale) in enumerate(((q1, 0.25 * 0.125), (shift1, 0.125))):
            work[f, i, pl.ds(0, half), :] = lane1.pair(values[2 * i] + values[2 * i + 1])
            cells[f, i] = scale * (
                work[f, i, pl.ds(HALO, rows // 4, stride=2), :]
                + work[f, i, pl.ds(HALO + 1, rows // 4, stride=2), :]
            )

    for p in range(2, ext_planes - 2):
        quarter_kept[p - 2] = quarter[p][kept]
        for k in range(3):
            v2_kept[k, p - 2] = v2[k, p][kept]
    for p in range(3, ext_planes - 3):
        weight_kept[p - 3], step_kept[p - 3] = weight[p][kept], step[p][kept]
        for k in range(3):
            source_kept[k, p - 3] = source[k, p][kept]


def middle_before(
    own, cells, from_a, from_b,
    to_all, v2, source, quarter, weight, step,
    v1, work,
):
    planes, ext_rows = own.shape[1], own.shape[2]
    rows = ext_rows - 2 * HALO
    ext_planes = planes + 2 * HALO
    lane = Lane(ext_rows, 2)

    def put(k, p, value):
        if k < 3:
            source[k, p] = value
        elif k == 3:
            quarter[p] = value
        else:
            weight[p] = value

    is_odd = odd("len")
    even = (lane_ids((ext_rows, LANES)) & 1) == 0
    for k in range(5):
        for p in range(planes):
            put(k, HALO + p, own[k, p])
        for i in range(HALO // 2):
            a, b = from_a[k, i], from_b[k, i]
            for start, x in (
                (0, jnp.where(is_odd, a, b)),
                (HALO + planes, jnp.where(is_odd, b, a)),
            ):
                put(k, start + 2 * i, jnp.where(even, x, turn(x, 1, 1)))
                put(k, start + 2 * i + 1, jnp.where(even, turn(x, -1, 1), x))

    for p in range(ext_planes):
        q, total = quarter[p], weight[p]
        st = step_of(total, total + (4.0 * COUPLING) * q)
        step[p] = st
        weight[p] = total + 8.0 * q
        for k in range(3):
            v1[k, p] = st * source[k, p]

    def put_v2(k, p, value):
        v2[k, p] = value

    bounds = (0, ext_planes)
    sweep(
        lambda k, p: v1[k, p], quarter, weight, step, source,
        range(1, ext_planes - 1), bounds, lane, put_v2,
    )
    held = {}
    half = rows // 2
    for p, _, r in defects(
        lambda k, p: v2[k, p], quarter, weight, source,
        range(HALO, HALO + planes), bounds, lane,
    ):
        if p % 2 == 0:
            held = r
            continue
        i = (p - HALO) // 2
        for k in range(3):
            work[k, i] = held[k] + r[k]
    for i in range(planes // 2):
        for k in range(3):
            work[k, i] = lane.pair(work[k, i])
    depth = planes // 2
    ids = lane_ids((depth * half, LANES))
    row = lax.broadcasted_iota(jnp.int32, ids.shape, 0)
    mine = ids // ROW == row % half
    lines = []
    for k in range(5):
        parts = [
            cells[k - 3, i]
            if k >= 3
            else 0.125
            * (
                work[k, i, pl.ds(HALO, half, stride=2), :]
                + work[k, i, pl.ds(HALO + 1, half, stride=2), :]
            )
            for i in range(depth)
        ]
        x = pick(jnp.concatenate(parts, axis=0), (ids % ROW) * (LANES // ROW))
        x = jnp.where(mine, x, 0.0)
        x = x + turn(x, -1, 0)
        x = x + turn(x, -2, 0)
        lines += [x[i * half : i * half + 1] for i in range(depth)]
    block = jnp.concatenate(lines * 4, axis=0)
    count = block.shape[0]
    for at in range(0, to_all.shape[0], count):
        to_all[at : at + count, :] = block


def coarse_and_after(
    bricks_before,
    table, v2_mid, source_mid, quarter_mid, weight_mid, step_mid,
    v2_fine, source_fine, quarter_fine, weight_fine, step_fine,
    out,
    wide2, u_mid, x_mid, u_fine, x_fine,
):
    brick = lax.axis_index("brick")
    slab = lax.axis_index("len")
    bricks, planes2 = wide2.shape[2] - 16, wide2.shape[1] - 4
    depth = (v2_mid.shape[1] - 2 * HALO) // 2
    lines = 5 * depth

    def field(f):
        return jnp.stack(
            [
                table[pl.ds((i // depth) * bricks * lines + f * depth + i % depth, bricks, stride=lines), :]
                for i in range(planes2)
            ],
            axis=0,
        )

    lane2, lane3 = Packed(bricks, 1), Packed(bricks, 2)
    b2, q2, s2 = [field(k) for k in range(3)], field(3), field(4)
    e2, x2 = lane2.terms(q2, s2)
    u2 = lane2.sweep([x2 * b for b in b2], q2, e2, x2, b2)

    rest = lane2.defects(u2, q2, e2, b2)
    joint = lane2.restrict(jnp.concatenate(rest + [0.25 * q2, s2], axis=0))
    count = planes2 // 2
    *b3, q3, s3 = [joint[i * count : (i + 1) * count] for i in range(5)]
    e3, x3 = lane3.terms(q3, s3)
    u3 = [x3 * b for b in b3]
    for _ in range(3):
        u3 = lane3.sweep(u3, q3, e3, x3, b3)

    u2 = [u2[k] + twice_planes(u3[k]) for k in range(3)]
    for _ in range(2):
        u2 = lane2.sweep(u2, q2, e2, x2, b2)
    wide2[...] = jnp.zeros_like(wide2)
    for k in range(3):
        wide2[k, pl.ds(2, planes2), pl.ds(8, bricks), :] = u2[k]

    v2_fine, quarter_fine = From(v2_fine, 2), From(quarter_fine, 2)
    source_fine, weight_fine, step_fine = [
        From(x, 3) for x in (source_fine, weight_fine, step_fine)
    ]
    planes1 = v2_mid.shape[1]
    rows1 = v2_mid.shape[2]
    lane1 = Lane(rows1, 2)
    bounds1 = (0, planes1)
    line_at = brick - bricks_before(brick) + 8
    half_shape = (rows1 // 2, LANES)
    ids, row = lane_ids(half_shape), lax.broadcasted_iota(jnp.int32, half_shape, 0)
    lanes = ROW * ((row + 2) % 4) + ids // (LANES // ROW)
    for k in range(3):
        for i in range(planes1 // 2):
            low, own, high = [
                jnp.broadcast_to(
                    wide2[k, depth * slab + i, pl.ds(line_at + at, 1), :], half_shape
                )
                for at in (-1, 0, 1)
            ]
            piece = pick(jnp.where(row < 2, low, jnp.where(row < 6, own, high)), lanes)
            for half in range(2):
                x_mid[k, i, pl.ds(half, rows1 // 2, stride=2), :] = piece
            both = x_mid[k, i]
            for p in (2 * i, 2 * i + 1):
                if 1 <= p < planes1 - 1:
                    u_mid[k, p] = v2_mid[k, p] + both

    def put_mid(k, p, value):
        x_mid[k, p] = value

    sweep(
        lambda k, p: u_mid[k, p], quarter_mid, weight_mid, step_mid, source_mid,
        range(2, planes1 - 2), bounds1, lane1, put_mid,
    )

    def put_mid_last(k, p, value):
        u_mid[k, p] = value

    sweep(
        lambda k, p: x_mid[k, p], quarter_mid, weight_mid, step_mid, source_mid,
        range(3, planes1 - 3), bounds1, lane1, put_mid_last,
    )

    planes0, rows0 = x_fine.shape[1], x_fine.shape[2]
    lane0 = Lane(rows0, 1)
    bounds0 = (0, planes0)
    half_rows = rows0 // 2
    for k in range(3):
        for i in range(3, planes1 - 3):
            piece = u_mid[k, i, pl.ds(2, half_rows), :]
            p = 2 * i - HALO
            for half in range(2):
                x_fine[k, p, pl.ds(half, half_rows, stride=2), :] = piece
            both = x_fine[k, p]
            for at in (p, p + 1):
                u_fine[k, at] = v2_fine[k, at] + both

    def put_fine(k, p, value):
        x_fine[k, p] = value

    sweep(
        lambda k, p: u_fine[k, p], quarter_fine, weight_fine, step_fine, source_fine,
        range(3, planes0 - 3), bounds0, lane0, put_fine,
    )

    def put_out(k, p, value):
        out[k, p - HALO] = value[HALO : rows0 - HALO]

    sweep(
        lambda k, p: x_fine[k, p], quarter_fine, weight_fine, step_fine, source_fine,
        range(HALO, planes0 - HALO), bounds0, lane0, put_out,
    )


def call(kernel, outs, scratch=(), name=None, **more):
    return pl.pallas_call(
        kernel,
        out_shape=[jax.ShapeDtypeStruct(shape, F32) for shape in outs],
        scratch_shapes=[vmem(x) if isinstance(x, tuple) else x for x in scratch],
        compiler_params=pltpu.CompilerParams(vmem_limit_bytes=40 * 1024 * 1024),
        name=name,
        **more,
    )


def swap(x, axis, first):
    count = lax.axis_size(axis)
    pairs = []
    for i in range(first, count - 1, 2):
        pairs += [(i, i + 1), (i + 1, i)]
    return lax.ppermute(x, axis, pairs)


def body(forces, modulus, occupancy, bonded):
    planes, rows = modulus.shape[0], modulus.shape[1]
    slabs, bricks = lax.axis_size("len"), lax.axis_size("brick")
    ext, ext_rows = planes + 2 * HALO, rows + 2 * WIDE
    half, half_rows = planes // 2, rows // 2
    mid, mid_rows = half + 2 * HALO, half_rows + 2 * HALO

    side, block = (row_spots(planes)[1], LANES), (planes, rows, LANES)
    middle_side, corner = (middle_spots(rows)[1], LANES), (corner_spots()[1], LANES)
    here = [
        pltpu.with_memory_space_constraint(x, pltpu.HBM)
        for x in (forces, modulus, occupancy, bonded)
    ]
    own, to_c, to_d, to_a, to_b = call(
        pack_rows,
        [(5,) + block, side, side, middle_side, middle_side],
        [block, pltpu.VMEM(block, jnp.int32), pltpu.VMEM(block, jnp.int32)]
        + [pltpu.SemaphoreType.DMA((4,))],
        name="pack_rows",
        in_specs=[pl.BlockSpec(memory_space=pltpu.HBM)] * 4,
    )(*here)
    from_c = swap(to_c, "brick", 0)
    middle_b = swap(to_b, "len", 1)
    from_d = swap(to_d, "brick", 1)
    middle_a = swap(to_a, "len", 0)
    to_a, to_b = call(
        functools.partial(pack_corners, planes),
        [corner, corner],
        name="pack_corners",
        in_specs=[pl.BlockSpec(memory_space=x) for x in (pltpu.VMEM, pl.ANY) * 2],
    )(from_c, middle_b, from_d, middle_a)
    corner_b = swap(to_b, "len", 1)
    corner_a = swap(to_a, "len", 0)

    field, cell = (3, ext, ext_rows, LANES), (ext, ext_rows, LANES)
    line = (rows + 2 * HALO, LANES)
    block = (planes, ext_rows, LANES)
    weighed, swept, left = [(len(x), ext_rows, LANES) for x in inner_planes(planes)]
    inner = call(
        fine_inner,
        [(3,) + block, block, block, weighed, weighed]
        + [(3,) + weighed, (3,) + swept, (3,) + left],
        name="fine_inner",
        in_specs=[pl.BlockSpec(memory_space=pltpu.VMEM)] * 3
        + [pl.BlockSpec(memory_space=pl.ANY)],
        cost_estimate=pl.CostEstimate(flops=10**7, bytes_accessed=4 * 10**6, transcendentals=0),
    )(own, from_c, from_d, to_a)
    own, to_len, cells, *fine = call(
        fine_before,
        [(5, half, mid_rows, LANES), (5, half // 2, mid_rows, LANES)]
        + [(2, half // 2, half_rows // 2, LANES)]
        + [(3, ext - 4) + line, (3, ext - 6) + line, (ext - 4,) + line]
        + [(ext - 6,) + line] * 2,
        [field, field, cell, cell, cell, cell, field]
        + [(5, half + 2, ext_rows, LANES), (half + 2, mid_rows + 16, LANES)],
        name="fine_before",
    )(*inner, middle_b, middle_a, corner_b, corner_a)
    from_b = swap(to_len, "len", 1)
    from_a = swap(to_len, "len", 0)

    field1, cell1 = (3, mid, mid_rows, LANES), (mid, mid_rows, LANES)
    depth = half // 2
    lines = 5 * depth
    to_all, *middle = call(
        middle_before,
        [(slabs * bricks * lines, LANES)] + [field1, field1, cell1, cell1, cell1],
        [field1, (3, depth, mid_rows, LANES)],
        name="middle_before",
    )(own, cells, from_a, from_b)

    to_all = to_all.reshape(-1, 2, LANES)
    table = lax.all_to_all(to_all, BOTH, 0, 0, tiled=True).reshape(-1, LANES)
    window = bricks if bricks <= 8 else 16

    def first_brick(brick):
        return jnp.clip(brick - 4, 0, bricks - window)

    if window < bricks:
        table = lax.dynamic_slice_in_dim(
            table.reshape(slabs, bricks * lines, LANES),
            first_brick(lax.axis_index("brick")) * lines, window * lines, axis=1,
        ).reshape(slabs * window * lines, LANES)
    planes2 = slabs * depth
    (out,) = call(
        functools.partial(coarse_and_after, first_brick),
        [forces.shape],
        [(3, planes2 + 4, window + 16, LANES), field1, field1]
        + [(3, ext, rows + 2 * HALO, LANES)] * 2,
        name="coarse_and_after",
    )(table, *middle, *fine)
    return out


def solution(mesh):
    cells = P("len", "brick", None)
    forces = P(None, "len", "brick", None)
    return jax.shard_map(
        body, mesh=mesh, in_specs=(forces, cells, cells, cells), out_specs=forces, check_vma=False
    )
```

```python
import functools

import jax
import jax.numpy as jnp
from jax import lax
from jax.experimental import pallas as pl
from jax.experimental.pallas import tpu as pltpu
from jax.sharding import PartitionSpec as P

DAMPING = 0.6
COUPLING = 0.2
MASS_TERM = 0.1
PENALTY = 20.0

HALO = 4
WIDE = 12
ROWS = (10, 10, 10, 11, 10)
PLANES = (3, 3, 3, 4, 3)
LANES = 128
ROW = 32
F32 = jnp.float32
BOTH = ("len", "brick")


def lane_ids(shape):
    return lax.broadcasted_iota(jnp.int32, shape, len(shape) - 1)


def turn(x, by, axis):
    return pltpu.roll(x, by % x.shape[axis], axis)


def pick(x, lanes):
    return jnp.take_along_axis(x, lanes, axis=1, mode="promise_in_bounds")


class Lane:
    def __init__(self, rows, wide):
        ids = lane_ids((rows, LANES))
        self.wide = wide
        self.low = jnp.where(ids >= wide, 0.5, 0.0).astype(F32)
        self.high = jnp.where(ids < LANES - wide, 0.5, 0.0).astype(F32)
        self.first = (ids & wide) == 0

    def smooth(self, x):
        return x + self.low * turn(x, self.wide, 1) + self.high * turn(x, -self.wide, 1)

    def beside(self, q):
        return turn(q, self.wide, 1), turn(q, -self.wide, 1)

    def blend(self, x, y, q, before, after):
        return (q * x + y) + (
            self.low * turn(after * x + y, self.wide, 1)
            + self.high * turn(before * x + y, -self.wide, 1)
        )

    def pair(self, x):
        return x + swap_lanes(x, self.wide, self.first)

    def rows(self, x):
        pair = x + turn(x, 1, 0)
        return pair + turn(pair, -1, 0)


def swap_lanes(x, by, first):
    return jnp.where(first, turn(x, -by, 1), turn(x, by, 1))


class Packed:
    def __init__(self, bricks, wide):
        shape = (1, bricks, LANES)
        ids = lane_ids(shape)
        line = lax.broadcasted_iota(jnp.int32, shape, 1)
        self.wide = wide
        top, bottom = ids < ROW * wide, ids >= LANES - ROW * wide

        def number(mask, value):
            return jnp.where(mask, value, 0.0).astype(F32)

        self.low = number((ids & (ROW - 1)) >= wide, 0.5)
        self.high = number((ids & (ROW - 1)) < ROW - wide, 0.5)
        self.not_top, self.not_bottom = number(~top, 1.0), number(~bottom, 1.0)
        self.top = number(top & (line > 0), 1.0)
        self.bottom = number(bottom & (line < bricks - 1), 1.0)
        self.odd_row, self.odd_lane = number((ids & ROW) > 0, 1.0), number((ids & 1) > 0, 1.0)

    def smooth(self, x):
        return x + (self.low * turn(x, self.wide, 2) + self.high * turn(x, -self.wide, 2))

    def rows(self, x):
        back = turn(x, ROW * self.wide, 2)
        ahead = back if self.wide == 2 else turn(x, -ROW, 2)
        before = self.not_top * back + self.top * turn(back, 1, 1)
        after = self.not_bottom * ahead + self.bottom * turn(ahead, -1, 1)
        return (x + x) + (before + after)

    def pair(self, x):
        for by, is_odd in ((ROW, self.odd_row), (1, self.odd_lane)):
            x = x + (is_odd * turn(x, by, 2) + (1.0 - is_odd) * turn(x, -by, 2))
        return x

    def planes(self, x):
        none = jnp.zeros_like(x[:1])
        above = jnp.concatenate([x[1:], none], axis=0)
        below = jnp.concatenate([none, x[:-1]], axis=0)
        return (x + x) + (above + below)

    def full(self, x):
        return self.smooth(self.rows(self.planes(x)))

    def terms(self, q, s):
        total = 24.0 * q + self.full(q) + s
        q = [jnp.concatenate([x] * 3, axis=0) for x in (q, turn(q, self.wide, 2), turn(q, -self.wide, 2))]
        weight = total + 8.0 * q[0][: total.shape[0]]
        return (q, weight), DAMPING / (total + (4.0 * COUPLING) * q[0][: total.shape[0]])

    def defects(self, v, terms, source):
        (q3, before, after), weight = terms
        count = weight.shape[0]
        q = q3[:count]
        stack = [self.planes(x) for x in v] + [self.planes(q * x) for x in v]
        both = self.rows(jnp.concatenate(stack, axis=0))
        x, y = both[: 3 * count], both[3 * count :]
        sums = (q3 * x + y) + (
            self.low * turn(after * x + y, self.wide, 2)
            + self.high * turn(before * x + y, -self.wide, 2)
        )
        coupled = (4.0 * COUPLING) * q * (v[0] + v[1] + v[2])
        return [
            source[k] - weight * v[k] + sums[k * count : (k + 1) * count] - coupled
            for k in range(3)
        ]

    def sweep(self, v, terms, step, source):
        r = self.defects(v, terms, source)
        return [v[k] + step * r[k] for k in range(3)]

    def restrict(self, x):
        x = x.reshape((x.shape[0] // 2, 2) + x.shape[1:])
        return 0.125 * self.pair(x[:, 0] + x[:, 1])


def twice_planes(x):
    return jnp.concatenate([x[i // 2 : i // 2 + 1] for i in range(2 * x.shape[0])], axis=0)


def smooth_planes(get, p):
    below, here, above = get(p - 1), get(p), get(p + 1)
    total = here + here
    if below is not None:
        total = total + below
    if above is not None:
        total = total + above
    return total


def remember(get):
    seen = {}

    def cached(p):
        if p not in seen:
            seen[p] = get(p)
        return seen[p]

    return cached


def within(get, low, high):
    return lambda p: get(p) if low <= p < high else None


APART = {}


def gathered(field, quarter, planes, bounds, lane, beside=None):
    beside = {} if beside is None else beside
    q_at = remember(lambda p: quarter[p])
    v_at = [remember(lambda p, k=k: field(k, p)) for k in range(3)]
    w_at = [remember(lambda p, k=k: q_at(p) * v_at[k](p)) for k in range(3)]
    pairs = [
        [remember(lambda p, x=x: x(p) + x(p + 1)) for x in group] for group in (v_at, w_at)
    ]
    for p in planes:
        q = q_at(p)
        if p not in beside and beside is not APART:
            beside[p] = lane.beside(q)
        sums = []
        for k in range(3):
            x, y = [lane.rows(group[k](p - 1) + group[k](p)) for group in pairs]
            if beside is APART:
                sums.append(q * lane.smooth(x) + lane.smooth(y))
            else:
                sums.append(lane.blend(x, y, q, *beside[p]))
        yield p, [v_at[k](p) for k in range(3)], q, sums


def defects(field, quarter, weight, source, planes, bounds, lane, beside=None):
    for p, v, q, sums in gathered(field, quarter, planes, bounds, lane, beside):
        coupled = (4.0 * COUPLING) * q * (v[0] + v[1] + v[2])
        e = weight[p]
        yield p, v, [source[k, p] - e * v[k] + sums[k] - coupled for k in range(3)]


def sweep(field, quarter, weight, step, source, planes, bounds, lane, put, beside=None):
    for p, v, r in defects(field, quarter, weight, source, planes, bounds, lane, beside):
        s = step[p]
        for k in range(3):
            put(k, p, v[k] + s * r[k])


def stiffness_sum(quarter, planes, bounds, lane):
    q_at = remember(within(lambda p: quarter[p], *bounds))
    for p in planes:
        yield p, 24.0 * q_at(p) + lane.smooth(lane.rows(smooth_planes(q_at, p)))


def step_of(inside, diagonal):
    return jnp.where(inside > 0.0, DAMPING / diagonal, 0.0)


def odd(axis):
    return lax.rem(lax.axis_index(axis), 2) == 1


class From:
    def __init__(self, ref, first):
        self.ref, self.first = ref, first

    def __getitem__(self, at):
        if isinstance(at, tuple):
            return self.ref[at[0], at[1] - self.first]
        return self.ref[at - self.first]


class Either:
    def __init__(self, inner, span, outer):
        self.inner, self.span, self.outer = From(inner, span[0]), span, outer

    def __getitem__(self, at):
        p = at[1] if isinstance(at, tuple) else at
        return self.inner[at] if p in self.span else self.outer[at]


class Stack:
    def __init__(self, *parts):
        self.spots = {p: (ref, i) for ref, planes in parts for i, p in enumerate(planes)}

    def __getitem__(self, at):
        if isinstance(at, tuple):
            ref, i = self.spots[at[1]]
            return ref[at[0], i]
        ref, i = self.spots[at]
        return ref[i]


def vmem(shape):
    return pltpu.VMEM(shape, F32)


def row_spots(planes):
    spots, at = {}, 0
    for k, reach in enumerate(ROWS):
        for p in range(planes):
            spots[k, p] = slice(at, at + reach)
            at += reach
    return spots, at


def plane_spots(heights):
    spots, at = {}, 0
    for k, count in enumerate(PLANES):
        for i in range(count):
            spots[k, i] = slice(at, at + heights[k])
            at += heights[k]
    return spots, at


def middle_spots(rows):
    return plane_spots([rows] * 5)


def corner_spots():
    spots, at = {}, 0
    for k, count in enumerate(PLANES):
        for distance in range(1, count + 1):
            reach = ROWS[k] if distance < count else count
            spots[k, distance] = at, reach
            at += 2 * reach
    return spots, at


def pack_rows(
    forces, modulus, occupancy, bonded, own, to_c, to_d, to_a, to_b,
    modulus_here, occupancy_here, bonded_here, arrived,
):
    pairs = [(modulus, modulus_here), (occupancy, occupancy_here), (bonded, bonded_here)]
    pairs += [(forces.at[k], own.at[k]) for k in range(3)]
    copies = [pltpu.make_async_copy(*pair, arrived.at[i]) for i, pair in enumerate(pairs)]
    for copy in copies:
        copy.start()
    planes, rows = own.shape[1], own.shape[2]
    for copy in copies[:2]:
        copy.wait()
    for p in range(planes):
        own[3, p] = modulus_here[p] * occupancy_here[p].astype(F32)
    copies[2].wait()
    for p in range(planes):
        own[4, p] = MASS_TERM + PENALTY * bonded_here[p].astype(F32)
    for copy in copies[3:]:
        copy.wait()
    is_odd = odd("brick")
    spots, _ = row_spots(planes)
    for (k, p), spot in spots.items():
        first = own[k, p, 0 : ROWS[k], :]
        last = own[k, p, rows - ROWS[k] : rows, :]
        to_c[spot, :] = jnp.where(is_odd, first, last)
        to_d[spot, :] = jnp.where(is_odd, last, first)
    is_odd = odd("len")
    for (k, i), spot in middle_spots(rows)[0].items():
        first, last = own[k, i], own[k, planes - PLANES[k] + i]
        to_a[spot, :] = jnp.where(is_odd, first, last)
        to_b[spot, :] = jnp.where(is_odd, last, first)


def rows_beside(from_c, from_d):
    is_odd = odd("brick")

    def get(spot, reach):
        low, high = slice(spot.stop - reach, spot.stop), slice(spot.start, spot.start + reach)
        return (
            jnp.where(is_odd, from_c[low, :], from_d[low, :]),
            jnp.where(is_odd, from_d[high, :], from_c[high, :]),
        )

    return get


def pack_corners(planes, from_c, middle_b, from_d, middle_a, to_a, to_b):
    del middle_a, middle_b
    is_odd = odd("len")
    from_rows, _ = row_spots(planes)
    beside = rows_beside(from_c, from_d)
    for (k, distance), (at, reach) in corner_spots()[0].items():
        firsts = beside(from_rows[k, distance - 1], reach)
        lasts = beside(from_rows[k, planes - distance], reach)
        for half, (first, last) in enumerate(zip(firsts, lasts)):
            span = slice(at + half * reach, at + (half + 1) * reach)
            to_a[span, :] = jnp.where(is_odd, first, last)
            to_b[span, :] = jnp.where(is_odd, last, first)


def inner_planes(planes):
    return [range(HALO + i, HALO + planes - i) for i in (1, 2, 3)]


def kept_planes(planes):
    weighed, swept, _ = inner_planes(planes)
    own = range(HALO, HALO + planes)
    end = planes + 2 * HALO
    wide, close = range(2, end - 2), range(3, end - 3)
    pairs = ((swept, wide), (own, close), (own, wide), (weighed, close), (weighed, close))
    return [(inner, [p for p in every if p not in inner]) for inner, every in pairs]


def keep(kept_rows, targets, arrays, numbers):
    for k in range(2):
        for i, p in enumerate(numbers[k]):
            for c in range(3):
                targets[k][c, i] = arrays[k][c, p][kept_rows]
    for k in range(2, 5):
        for i, p in enumerate(numbers[k]):
            targets[k][i] = arrays[k][p][kept_rows]


def halves(x, rows):
    count = (rows.stop - rows.start) // 2
    return x[pl.ds(rows.start, count, stride=2), :] + x[pl.ds(rows.start + 1, count, stride=2), :]


def coarse_weight(lane, quarter_at, i, rows):
    sides, here, others = [
        smooth_planes(lambda j, at=at: quarter_at(j)[pl.ds(at, rows), :], i) for at in (7, 8, 9)
    ]
    return 24.0 * quarter_at(i)[pl.ds(8, rows), :] + lane.smooth(sides + 2.0 * here + others)


def fine_inner(
    own, from_c, from_d, to_a,
    source, quarter, shift, weight, step, v1, v2, rest, coarse_q, shift1, sums, cells, *more,
):
    del to_a
    planes, rows = own.shape[1], own.shape[2]
    lane = Lane(rows + 2 * WIDE, 1)
    beside = rows_beside(from_c, from_d)

    def put(k, p, r, value):
        if k < 3:
            source[k, p, r, :] = value
        elif k == 3:
            quarter[p, r, :] = 0.25 * value
        else:
            shift[p, r, :] = value

    for (k, p), spot in row_spots(planes)[0].items():
        low, high = beside(spot, ROWS[k])
        put(k, p, slice(WIDE - ROWS[k], WIDE), low)
        put(k, p, slice(WIDE, WIDE + rows), own[k, p])
        put(k, p, slice(WIDE + rows, WIDE + rows + ROWS[k]), high)

    weighed, swept, left = inner_planes(planes)
    bounds = (HALO, HALO + planes)
    source_at, quarter_at = From(source, HALO), From(quarter, HALO)
    for p, w in stiffness_sum(quarter_at, weighed, bounds, lane):
        q, s, i = quarter_at[p], shift[p - HALO], p - weighed[0]
        total = w + s
        weight[i] = total + 8.0 * q
        st = step_of(s, total + (4.0 * COUPLING) * q)
        step[i] = st
        for k in range(3):
            v1[k, i] = st * source_at[k, p]
    weight_at, step_at = From(weight, weighed[0]), From(step, weighed[0])

    def put_v2(k, p, value):
        v2[k, p - swept[0]] = value

    v1_at, v2_at, near = From(v1, weighed[0]), From(v2, swept[0]), APART
    sweep(
        lambda k, p: v1_at[k, p], quarter_at, weight_at, step_at, source_at,
        swept, (weighed[0], weighed[-1] + 1), lane, put_v2, near,
    )
    for p, _, r in defects(
        lambda k, p: v2_at[k, p], quarter_at, weight_at, source_at,
        left, (swept[0], swept[-1] + 1), lane, near,
    ):
        for k in range(3):
            rest[k, p - left[0]] = r[k]

    *kept, work = more
    half = rows // 2 + 2 * HALO
    outer = slice(WIDE - 2 * HALO, WIDE + rows + 2 * HALO)
    beyond = slice(outer.start - 2, outer.stop + 2)
    count = planes // 2
    for i in range(count):
        work[0, i] = quarter[2 * i] + quarter[2 * i + 1]
        work[1, i] = shift[2 * i] + shift[2 * i + 1]
    for f in range(2):
        for i in range(count):
            work[f, i] = lane.pair(work[f, i])
    for i in range(count):
        coarse_q[i, pl.ds(7, half + 2), :] = (0.25 * 0.125) * halves(work.at[0, i], beyond)
        shift1[i] = 0.125 * halves(work.at[1, i], outer)
    lane1 = Lane(half, 2)
    for i in range(1, count - 1):
        s = shift1[i]
        w = coarse_weight(lane1, lambda j: coarse_q.at[j], i, half)
        sums[i - 1] = jnp.where(s > 0.0, w + s, 0.0)

    inner = slice(HALO, HALO + rows // 2)
    for i in range(count // 2):
        pair = [coarse_q[2 * i + j, pl.ds(8, half), :] for j in range(2)]
        work[0, i, pl.ds(0, half), :] = lane1.pair(pair[0] + pair[1])
        work[1, i, pl.ds(0, half), :] = lane1.pair(shift1[2 * i] + shift1[2 * i + 1])
        for f, scale in enumerate((0.25 * 0.125, 0.125)):
            cells[f, i] = scale * halves(work.at[f, i], inner)
    keep(
        slice(WIDE - HALO, WIDE + rows + HALO), kept,
        (v2_at, source_at, quarter_at, weight_at, step_at),
        [x for x, _ in kept_planes(planes)],
    )


def fine_before(
    source_in, quarter_in, shift_in, weight_in, step_in, v1_in, v2_in, rest_in,
    coarse_q_in, shift1, sums_in, middle_b, middle_a, corner_a, corner_b,
    own_coarse, to_len, *more,
):
    *kept, v2_out, source_out, quarter_out, weight_out, step_out, shift_out, v1_out, work, coarse_q = more
    planes, ext_rows = quarter_in.shape[0], quarter_in.shape[1]
    ext_planes, rows = planes + 2 * HALO, ext_rows - 2 * WIDE
    lane = Lane(ext_rows, 1)

    def put(k, p, r, value):
        if k < 3:
            source_out[k, p, r, :] = value
        elif k == 3:
            quarter_out[p, r, :] = 0.25 * value
        else:
            shift_out[p, r, :] = value

    is_odd = odd("len")
    def put_both(k, distance, start, low, high):
        r = slice(start, start + low.shape[0])
        put(k, HALO - distance, r, low)
        put(k, HALO + planes - 1 + distance, r, high)

    def sides(a, b):
        return jnp.where(is_odd, a, b), jnp.where(is_odd, b, a)

    spots = middle_spots(rows)[0]
    for k, count in enumerate(PLANES):
        for distance in range(1, count + 1):
            low = sides(*[x[spots[k, count - distance], :] for x in (middle_a, middle_b)])[0]
            high = sides(*[x[spots[k, distance - 1], :] for x in (middle_a, middle_b)])[1]
            put_both(k, distance, WIDE, low, high)
    for (k, distance), (at, reach) in corner_spots()[0].items():
        for half, start in enumerate((WIDE - reach, WIDE + rows)):
            span = slice(at + half * reach, at + (half + 1) * reach)
            put_both(k, distance, start, *sides(corner_a[span, :], corner_b[span, :]))

    weighed, swept, left = inner_planes(planes)
    here = range(HALO, HALO + planes)
    source, quarter, shift = [
        Either(x, here, y)
        for x, y in ((source_in, source_out), (quarter_in, quarter_out), (shift_in, shift_out))
    ]
    weight, step, v1 = [
        Either(x, weighed, y)
        for x, y in ((weight_in, weight_out), (step_in, step_out), (v1_in, v1_out))
    ]
    v2 = Either(v2_in, swept, v2_out)

    bounds, near = (0, ext_planes), APART
    others = [p for p in range(1, ext_planes - 1) if p not in weighed]
    for p, w in stiffness_sum(quarter, others, bounds, lane):
        q, s = quarter[p], shift[p]
        total = w + s
        weight_out[p] = total + 8.0 * q
        st = step_of(s, total + (4.0 * COUPLING) * q)
        step_out[p] = st
        for k in range(3):
            v1_out[k, p] = st * source[k, p]

    def put_v2(k, p, value):
        v2_out[k, p] = value

    sweep(
        lambda k, p: v1[k, p], quarter, weight, step, source,
        [p for p in range(2, ext_planes - 2) if p not in swept], bounds, lane, put_v2, near,
    )

    half = rows // 2 + 2 * HALO
    outer = slice(WIDE - 2 * HALO, WIDE + rows + 2 * HALO)
    beyond = slice(outer.start - 2, outer.stop + 2)
    coarse_planes = planes // 2
    rest = {p: [rest_in[k, p - left[0]] for k in range(3)] for p in left}
    for p, _, r in defects(
        lambda k, p: v2[k, p], quarter, weight, source,
        [p for p in here if p not in left], bounds, lane, near,
    ):
        rest[p] = r
    for i in range(coarse_planes):
        p = HALO + 2 * i
        for k in range(3):
            work[k, i] = rest[p][k] + rest[p + 1][k]
    for j, p in enumerate((HALO - 2, HALO + planes)):
        work[3, j] = quarter[p] + quarter[p + 1]
    for k in range(4):
        for i in range(2 if k == 3 else coarse_planes):
            work[k, i] = lane.pair(work[k, i])
    for i in range(coarse_planes):
        for k in range(3):
            own_coarse[k, i] = 0.125 * halves(work.at[k, i], outer)

    for j in range(2):
        coarse_q[j, pl.ds(7, half + 2), :] = (0.25 * 0.125) * halves(work.at[3, j], beyond)

    def quarter1(i):
        if i < 0:
            return coarse_q.at[0]
        return coarse_q.at[1] if i == coarse_planes else coarse_q_in.at[i]

    lane1 = Lane(half, 2)
    for i in range(coarse_planes):
        own_coarse[3, i] = coarse_q_in[i, pl.ds(8, half), :]
        if 0 < i < coarse_planes - 1:
            own_coarse[4, i] = sums_in[i - 1]
        else:
            s = shift1[i]
            w = coarse_weight(lane1, quarter1, i, half)
            own_coarse[4, i] = jnp.where(s > 0.0, w + s, 0.0)

    even = (lane_ids((half, LANES)) & 1) == 0
    for k in range(5):
        for i in range(coarse_planes // 2):
            to_len[k, i] = jnp.where(even, own_coarse[k, 2 * i], own_coarse[k, 2 * i + 1])

    keep(
        slice(WIDE - HALO, WIDE + rows + HALO), kept,
        (v2, source, quarter, weight, step),
        [x for _, x in kept_planes(planes)],
    )


def middle_before(
    own, cells, from_b, from_a,
    to_all, v2, source, quarter, weight, step,
    v1, work,
):
    planes, ext_rows = own.shape[1], own.shape[2]
    rows = ext_rows - 2 * HALO
    ext_planes = planes + 2 * HALO
    lane = Lane(ext_rows, 2)

    def put(k, p, value):
        if k < 3:
            source[k, p] = value
        elif k == 3:
            quarter[p] = value
        else:
            weight[p] = value

    is_odd = odd("len")
    even = (lane_ids((ext_rows, LANES)) & 1) == 0
    for k in range(5):
        for p in range(planes):
            put(k, HALO + p, own[k, p])
        for i in range(HALO // 2):
            a, b = from_a[k, i], from_b[k, i]
            for start, x in (
                (0, jnp.where(is_odd, a, b)),
                (HALO + planes, jnp.where(is_odd, b, a)),
            ):
                put(k, start + 2 * i, jnp.where(even, x, turn(x, 1, 1)))
                put(k, start + 2 * i + 1, jnp.where(even, turn(x, -1, 1), x))

    for p in range(ext_planes):
        q, total = quarter[p], weight[p]
        st = step_of(total, total + (4.0 * COUPLING) * q)
        step[p] = st
        weight[p] = total + 8.0 * q
        for k in range(3):
            v1[k, p] = st * source[k, p]

    def put_v2(k, p, value):
        v2[k, p] = value

    bounds, near = (0, ext_planes), {}
    sweep(
        lambda k, p: v1[k, p], quarter, weight, step, source,
        range(1, ext_planes - 1), bounds, lane, put_v2, near,
    )
    held = {}
    half = rows // 2
    for p, _, r in defects(
        lambda k, p: v2[k, p], quarter, weight, source,
        range(HALO, HALO + planes), bounds, lane, near,
    ):
        if p % 2 == 0:
            held = r
            continue
        i = (p - HALO) // 2
        for k in range(3):
            work[k, i] = held[k] + r[k]
    for i in range(planes // 2):
        for k in range(3):
            work[k, i] = lane.pair(work[k, i])
    depth = planes // 2
    ids = lane_ids((depth * half, LANES))
    row = lax.broadcasted_iota(jnp.int32, ids.shape, 0)
    mine = ids // ROW == row % half
    lines = []
    for k in range(5):
        parts = [
            cells[k - 3, i]
            if k >= 3
            else 0.125
            * (
                work[k, i, pl.ds(HALO, half, stride=2), :]
                + work[k, i, pl.ds(HALO + 1, half, stride=2), :]
            )
            for i in range(depth)
        ]
        x = pick(jnp.concatenate(parts, axis=0), (ids % ROW) * (LANES // ROW))
        x = jnp.where(mine, x, 0.0)
        x = x + turn(x, -1, 0)
        x = x + turn(x, -2, 0)
        lines += [x[i * half : i * half + 1] for i in range(depth)]
    block = jnp.concatenate(lines * 4, axis=0)
    count = block.shape[0]
    for at in range(0, to_all.shape[0], count):
        to_all[at : at + count, :] = block


def coarse_and_after(
    bricks_before,
    table, v2_mid, source_mid, quarter_mid, weight_mid, step_mid, *more,
):
    kept_inner, kept_outer = more[:5], more[5:10]
    out, wide2, u_mid, x_mid, u_fine, x_fine = more[10:]
    brick = lax.axis_index("brick")
    slab = lax.axis_index("len")
    bricks, planes2 = wide2.shape[2] - 16, wide2.shape[1] - 4
    depth = (v2_mid.shape[1] - 2 * HALO) // 2
    lines = 5 * depth

    def field(f):
        return jnp.stack(
            [
                table[pl.ds((i // depth) * bricks * lines + f * depth + i % depth, bricks, stride=lines), :]
                for i in range(planes2)
            ],
            axis=0,
        )

    lane2, lane3 = Packed(bricks, 1), Packed(bricks, 2)
    b2, q2, s2 = [field(k) for k in range(3)], field(3), field(4)
    e2, x2 = lane2.terms(q2, s2)
    u2 = lane2.sweep([x2 * b for b in b2], e2, x2, b2)

    rest = lane2.defects(u2, e2, b2)
    joint = lane2.restrict(jnp.concatenate(rest + [0.25 * q2, s2], axis=0))
    count = planes2 // 2
    *b3, q3, s3 = [joint[i * count : (i + 1) * count] for i in range(5)]
    e3, x3 = lane3.terms(q3, s3)
    u3 = [x3 * b for b in b3]
    for _ in range(3):
        u3 = lane3.sweep(u3, e3, x3, b3)

    u2 = [u2[k] + twice_planes(u3[k]) for k in range(3)]
    for _ in range(2):
        u2 = lane2.sweep(u2, e2, x2, b2)
    wide2[...] = jnp.zeros_like(wide2)
    for k in range(3):
        wide2[k, pl.ds(2, planes2), pl.ds(8, bricks), :] = u2[k]

    v2_fine, source_fine, quarter_fine, weight_fine, step_fine = [
        Stack((inner, numbers[0]), (outer, numbers[1]))
        for inner, outer, numbers in zip(
            kept_inner, kept_outer, kept_planes(x_fine.shape[1] - 2 * HALO)
        )
    ]
    planes1 = v2_mid.shape[1]
    rows1 = v2_mid.shape[2]
    lane1 = Lane(rows1, 2)
    bounds1, beside1 = (0, planes1), {}
    line_at = brick - bricks_before(brick) + 8
    half_shape = (rows1 // 2, LANES)
    ids, row = lane_ids(half_shape), lax.broadcasted_iota(jnp.int32, half_shape, 0)
    lanes = ROW * ((row + 2) % 4) + ids // (LANES // ROW)
    for k in range(3):
        for i in range(planes1 // 2):
            low, own, high = [
                jnp.broadcast_to(
                    wide2[k, depth * slab + i, pl.ds(line_at + at, 1), :], half_shape
                )
                for at in (-1, 0, 1)
            ]
            piece = pick(jnp.where(row < 2, low, jnp.where(row < 6, own, high)), lanes)
            for half in range(2):
                x_mid[k, i, pl.ds(half, rows1 // 2, stride=2), :] = piece
            both = x_mid[k, i]
            for p in (2 * i, 2 * i + 1):
                if 1 <= p < planes1 - 1:
                    u_mid[k, p] = v2_mid[k, p] + both

    def put_mid(k, p, value):
        x_mid[k, p] = value

    sweep(
        lambda k, p: u_mid[k, p], quarter_mid, weight_mid, step_mid, source_mid,
        range(2, planes1 - 2), bounds1, lane1, put_mid, beside1,
    )

    def put_mid_last(k, p, value):
        u_mid[k, p] = value

    sweep(
        lambda k, p: x_mid[k, p], quarter_mid, weight_mid, step_mid, source_mid,
        range(3, planes1 - 3), bounds1, lane1, put_mid_last, beside1,
    )

    planes0, rows0 = x_fine.shape[1], x_fine.shape[2]
    lane0 = Lane(rows0, 1)
    bounds0, beside0 = (0, planes0), {}
    half_rows = rows0 // 2
    for k in range(3):
        for i in range(3, planes1 - 3):
            piece = u_mid[k, i, pl.ds(2, half_rows), :]
            p = 2 * i - HALO
            for half in range(2):
                x_fine[k, p, pl.ds(half, half_rows, stride=2), :] = piece
            both = x_fine[k, p]
            for at in (p, p + 1):
                u_fine[k, at] = v2_fine[k, at] + both

    def put_fine(k, p, value):
        x_fine[k, p] = value

    sweep(
        lambda k, p: u_fine[k, p], quarter_fine, weight_fine, step_fine, source_fine,
        range(3, planes0 - 3), bounds0, lane0, put_fine, beside0,
    )

    def put_out(k, p, value):
        out[k, p - HALO] = value[HALO : rows0 - HALO]

    sweep(
        lambda k, p: x_fine[k, p], quarter_fine, weight_fine, step_fine, source_fine,
        range(HALO, planes0 - HALO), bounds0, lane0, put_out, beside0,
    )


def call(kernel, outs, scratch=(), name=None, **more):
    return pl.pallas_call(
        kernel,
        out_shape=[jax.ShapeDtypeStruct(shape, F32) for shape in outs],
        scratch_shapes=[vmem(x) if isinstance(x, tuple) else x for x in scratch],
        compiler_params=pltpu.CompilerParams(vmem_limit_bytes=40 * 1024 * 1024),
        name=name,
        **more,
    )


def swap(x, axis, first):
    count = lax.axis_size(axis)
    pairs = []
    for i in range(first, count - 1, 2):
        pairs += [(i, i + 1), (i + 1, i)]
    return lax.ppermute(x, axis, pairs)


def body(forces, modulus, occupancy, bonded):
    planes, rows = modulus.shape[0], modulus.shape[1]
    slabs, bricks = lax.axis_size("len"), lax.axis_size("brick")
    ext, ext_rows = planes + 2 * HALO, rows + 2 * WIDE
    half, half_rows = planes // 2, rows // 2
    mid, mid_rows = half + 2 * HALO, half_rows + 2 * HALO

    side, block = (row_spots(planes)[1], LANES), (planes, rows, LANES)
    middle_side, corner = (middle_spots(rows)[1], LANES), (corner_spots()[1], LANES)
    here = [
        pltpu.with_memory_space_constraint(x, pltpu.HBM)
        for x in (forces, modulus, occupancy, bonded)
    ]
    own, to_c, to_d, to_a, to_b = call(
        pack_rows,
        [(5,) + block, side, side, middle_side, middle_side],
        [block, pltpu.VMEM(block, jnp.int32), pltpu.VMEM(block, jnp.int32)]
        + [pltpu.SemaphoreType.DMA((6,))],
        name="pack_rows",
        in_specs=[pl.BlockSpec(memory_space=pltpu.HBM)] * 4,
    )(*here)
    from_c = swap(to_c, "brick", 0)
    middle_b = swap(to_b, "len", 1)
    from_d = swap(to_d, "brick", 1)
    middle_a = swap(to_a, "len", 0)
    to_a, to_b = call(
        functools.partial(pack_corners, planes),
        [corner, corner],
        name="pack_corners",
        in_specs=[pl.BlockSpec(memory_space=x) for x in (pltpu.VMEM, pl.ANY) * 2],
    )(from_c, middle_b, from_d, middle_a)
    corner_a = swap(to_a, "len", 0)
    corner_b = swap(to_b, "len", 1)

    field, cell = (3, ext, ext_rows, LANES), (ext, ext_rows, LANES)
    line = (rows + 2 * HALO, LANES)
    block = (planes, ext_rows, LANES)
    weighed, swept, left = [(len(x), ext_rows, LANES) for x in inner_planes(planes)]
    kept_inner, kept_outer = [
        [
            ((3,) if k < 2 else ()) + (len(numbers[part]),) + line
            for k, numbers in enumerate(kept_planes(planes))
        ]
        for part in range(2)
    ]
    coarse = (half, mid_rows + 16, LANES)
    inner = call(
        fine_inner,
        [(3,) + block, block, block, weighed, weighed]
        + [(3,) + weighed, (3,) + swept, (3,) + left]
        + [coarse, (half, mid_rows, LANES), (half - 2, mid_rows, LANES)]
        + [(2, half // 2, half_rows // 2, LANES)]
        + kept_inner,
        [(2, half, ext_rows, LANES)],
        name="fine_inner",
        in_specs=[pl.BlockSpec(memory_space=pltpu.VMEM)] * 3
        + [pl.BlockSpec(memory_space=pl.ANY)],
        cost_estimate=pl.CostEstimate(flops=10**7, bytes_accessed=4 * 10**6, transcendentals=0),
    )(own, from_c, from_d, to_a)
    inner, cells, kept_inner = inner[:11], inner[11], inner[12:]
    own, to_len, *kept_outer = call(
        fine_before,
        [(5, half, mid_rows, LANES), (5, half // 2, mid_rows, LANES)] + kept_outer,
        [field, field, cell, cell, cell, cell, field]
        + [(4, half, ext_rows, LANES), (2,) + coarse[1:]],
        name="fine_before",
    )(*inner, middle_b, middle_a, corner_a, corner_b)
    from_a = swap(to_len, "len", 0)
    from_b = swap(to_len, "len", 1)

    field1, cell1 = (3, mid, mid_rows, LANES), (mid, mid_rows, LANES)
    depth = half // 2
    lines = 5 * depth
    to_all, *middle = call(
        middle_before,
        [(slabs * bricks * lines, LANES)] + [field1, field1, cell1, cell1, cell1],
        [field1, (3, depth, mid_rows, LANES)],
        name="middle_before",
    )(own, cells, from_b, from_a)

    to_all = to_all.reshape(-1, 2, LANES)
    table = lax.all_to_all(to_all, BOTH, 0, 0, tiled=True).reshape(-1, LANES)
    window = bricks if bricks <= 8 else 16

    def first_brick(brick):
        return jnp.clip(brick - 4, 0, bricks - window)

    if window < bricks:
        table = lax.dynamic_slice_in_dim(
            table.reshape(slabs, bricks * lines, LANES),
            first_brick(lax.axis_index("brick")) * lines, window * lines, axis=1,
        ).reshape(slabs * window * lines, LANES)
    planes2 = slabs * depth
    (out,) = call(
        functools.partial(coarse_and_after, first_brick),
        [forces.shape],
        [(3, planes2 + 4, window + 16, LANES), field1, field1]
        + [(3, ext, rows + 2 * HALO, LANES)] * 2,
        name="coarse_and_after",
    )(table, *middle, *kept_inner, *kept_outer)
    return out


def solution(mesh):
    cells = P("len", "brick", None)
    forces = P(None, "len", "brick", None)
    return jax.shard_map(
        body, mesh=mesh, in_specs=(forces, cells, cells, cells), out_specs=forces, check_vma=False
    )
```

```python
import functools

import jax
import jax.numpy as jnp
from jax import lax
from jax.experimental import pallas as pl
from jax.experimental.pallas import tpu as pltpu
from jax.sharding import PartitionSpec as P

DAMPING = 0.6
COUPLING = 0.2
MASS_TERM = 0.1
PENALTY = 20.0

HALO = 4
WIDE = 12
ROWS = (10, 10, 10, 11, 10)
PLANES = (3, 3, 3, 4, 3)
LANES = 128
ROW = 32
F32 = jnp.float32
BOTH = ("len", "brick")


def lane_ids(shape):
    return lax.broadcasted_iota(jnp.int32, shape, len(shape) - 1)


def turn(x, by, axis):
    return pltpu.roll(x, by % x.shape[axis], axis)


def pick(x, lanes):
    return jnp.take_along_axis(x, lanes, axis=1, mode="promise_in_bounds")


class Lane:
    def __init__(self, rows, wide):
        ids = lane_ids((rows, LANES))
        self.wide = wide
        self.low = jnp.where(ids >= wide, 0.5, 0.0).astype(F32)
        self.high = jnp.where(ids < LANES - wide, 0.5, 0.0).astype(F32)
        self.first = (ids & wide) == 0

    def smooth(self, x):
        return x + self.low * turn(x, self.wide, 1) + self.high * turn(x, -self.wide, 1)

    def beside(self, q):
        return turn(q, self.wide, 1), turn(q, -self.wide, 1)

    def blend(self, x, y, q, before, after):
        return (q * x + y) + (
            self.low * turn(after * x + y, self.wide, 1)
            + self.high * turn(before * x + y, -self.wide, 1)
        )

    def pair(self, x):
        return x + swap_lanes(x, self.wide, self.first)

    def rows(self, x):
        pair = x + turn(x, 1, 0)
        return pair + turn(pair, -1, 0)


def swap_lanes(x, by, first):
    return jnp.where(first, turn(x, -by, 1), turn(x, by, 1))


class Packed:
    def __init__(self, bricks, wide):
        shape = (1, bricks, LANES)
        ids = lane_ids(shape)
        line = lax.broadcasted_iota(jnp.int32, shape, 1)
        self.wide = wide
        top, bottom = ids < ROW * wide, ids >= LANES - ROW * wide

        def number(mask, value):
            return jnp.where(mask, value, 0.0).astype(F32)

        self.low = number((ids & (ROW - 1)) >= wide, 0.5)
        self.high = number((ids & (ROW - 1)) < ROW - wide, 0.5)
        self.not_top, self.not_bottom = number(~top, 1.0), number(~bottom, 1.0)
        self.top = number(top & (line > 0), 1.0)
        self.bottom = number(bottom & (line < bricks - 1), 1.0)
        self.odd_row, self.odd_lane = number((ids & ROW) > 0, 1.0), number((ids & 1) > 0, 1.0)

    def smooth(self, x):
        return x + (self.low * turn(x, self.wide, 2) + self.high * turn(x, -self.wide, 2))

    def rows(self, x):
        back = turn(x, ROW * self.wide, 2)
        ahead = back if self.wide == 2 else turn(x, -ROW, 2)
        before = self.not_top * back + self.top * turn(back, 1, 1)
        after = self.not_bottom * ahead + self.bottom * turn(ahead, -1, 1)
        return (x + x) + (before + after)

    def pair(self, x):
        for by, is_odd in ((ROW, self.odd_row), (1, self.odd_lane)):
            x = x + (is_odd * turn(x, by, 2) + (1.0 - is_odd) * turn(x, -by, 2))
        return x

    def planes(self, x):
        none = jnp.zeros_like(x[:1])
        above = jnp.concatenate([x[1:], none], axis=0)
        below = jnp.concatenate([none, x[:-1]], axis=0)
        return (x + x) + (above + below)

    def full(self, x):
        return self.smooth(self.rows(self.planes(x)))

    def terms(self, q, s):
        total = 24.0 * q + self.full(q) + s
        q = [jnp.concatenate([x] * 3, axis=0) for x in (q, turn(q, self.wide, 2), turn(q, -self.wide, 2))]
        weight = total + 8.0 * q[0][: total.shape[0]]
        return (q, weight), DAMPING / (total + (4.0 * COUPLING) * q[0][: total.shape[0]])

    def defects(self, v, terms, source):
        (q3, before, after), weight = terms
        count = weight.shape[0]
        q = q3[:count]
        stack = [self.planes(x) for x in v] + [self.planes(q * x) for x in v]
        both = self.rows(jnp.concatenate(stack, axis=0))
        x, y = both[: 3 * count], both[3 * count :]
        sums = (q3 * x + y) + (
            self.low * turn(after * x + y, self.wide, 2)
            + self.high * turn(before * x + y, -self.wide, 2)
        )
        coupled = (4.0 * COUPLING) * q * (v[0] + v[1] + v[2])
        return [
            source[k] - weight * v[k] + sums[k * count : (k + 1) * count] - coupled
            for k in range(3)
        ]

    def sweep(self, v, terms, step, source):
        r = self.defects(v, terms, source)
        return [v[k] + step * r[k] for k in range(3)]

    def restrict(self, x):
        x = x.reshape((x.shape[0] // 2, 2) + x.shape[1:])
        return 0.125 * self.pair(x[:, 0] + x[:, 1])


def twice_planes(x):
    return jnp.concatenate([x[i // 2 : i // 2 + 1] for i in range(2 * x.shape[0])], axis=0)


def smooth_planes(get, p):
    below, here, above = get(p - 1), get(p), get(p + 1)
    total = here + here
    if below is not None:
        total = total + below
    if above is not None:
        total = total + above
    return total


def remember(get):
    seen = {}

    def cached(p):
        if p not in seen:
            seen[p] = get(p)
        return seen[p]

    return cached


def within(get, low, high):
    return lambda p: get(p) if low <= p < high else None


APART = {}


def gathered(field, quarter, planes, bounds, lane, beside=None):
    beside = {} if beside is None else beside
    q_at = remember(lambda p: quarter[p])
    v_at = [remember(lambda p, k=k: field(k, p)) for k in range(3)]
    w_at = [remember(lambda p, k=k: q_at(p) * v_at[k](p)) for k in range(3)]
    pairs = [
        [remember(lambda p, x=x: x(p) + x(p + 1)) for x in group] for group in (v_at, w_at)
    ]
    for p in planes:
        q = q_at(p)
        if p not in beside and beside is not APART:
            beside[p] = lane.beside(q)
        sums = []
        for k in range(3):
            x, y = [lane.rows(group[k](p - 1) + group[k](p)) for group in pairs]
            if beside is APART:
                sums.append(q * lane.smooth(x) + lane.smooth(y))
            else:
                sums.append(lane.blend(x, y, q, *beside[p]))
        yield p, [v_at[k](p) for k in range(3)], q, sums


def defects(field, quarter, weight, source, planes, bounds, lane, beside=None):
    for p, v, q, sums in gathered(field, quarter, planes, bounds, lane, beside):
        coupled = (4.0 * COUPLING) * q * (v[0] + v[1] + v[2])
        e = weight[p]
        yield p, v, [source[k, p] - e * v[k] + sums[k] - coupled for k in range(3)]


def sweep(field, quarter, weight, step, source, planes, bounds, lane, put, beside=None):
    for p, v, r in defects(field, quarter, weight, source, planes, bounds, lane, beside):
        s = step[p]
        for k in range(3):
            put(k, p, v[k] + s * r[k])


def sweep_rows(field, quarter, weight, step, source, planes, rows, lane, put):
    near = [slice(rows.start + by, rows.stop + by) for by in (-1, 0, 1)]
    q_at = remember(lambda p: [quarter.cut(p, r) for r in near])
    v_at = [remember(lambda p, k=k: [field(k, p, r) for r in near]) for k in range(3)]

    def over_rows(x):
        return (x[0] + x[2]) + (x[1] + x[1])

    rows_v = [remember(lambda p, k=k: over_rows(v_at[k](p))) for k in range(3)]
    rows_w = [
        remember(lambda p, k=k: over_rows([q * v for q, v in zip(q_at(p), v_at[k](p))]))
        for k in range(3)
    ]
    pairs = [
        [remember(lambda p, x=x: x(p) + x(p + 1)) for x in group] for group in (rows_v, rows_w)
    ]
    for p in planes:
        q = q_at(p)[1]
        beside = lane.beside(q)
        v = [x(p)[1] for x in v_at]
        coupled = (4.0 * COUPLING) * q * (v[0] + v[1] + v[2])
        e, s = weight.cut(p, rows), step.cut(p, rows)
        for k in range(3):
            x, y = [group[k](p - 1) + group[k](p) for group in pairs]
            sums = lane.blend(x, y, q, *beside)
            put(k, p, v[k] + s * (source.cut((k, p), rows) - e * v[k] + sums - coupled))


def stiffness_sum(quarter, planes, bounds, lane):
    q_at = remember(within(lambda p: quarter[p], *bounds))
    for p in planes:
        yield p, 24.0 * q_at(p) + lane.smooth(lane.rows(smooth_planes(q_at, p)))


def step_of(inside, diagonal):
    return jnp.where(inside > 0.0, DAMPING / diagonal, 0.0)


def odd(axis):
    return lax.rem(lax.axis_index(axis), 2) == 1


class From:
    def __init__(self, ref, first):
        self.ref, self.first = ref, first

    def __getitem__(self, at):
        if isinstance(at, tuple):
            return self.ref[at[0], at[1] - self.first]
        return self.ref[at - self.first]


class Either:
    def __init__(self, inner, span, outer):
        self.inner, self.span, self.outer = From(inner, span[0]), span, outer

    def __getitem__(self, at):
        p = at[1] if isinstance(at, tuple) else at
        return self.inner[at] if p in self.span else self.outer[at]


class Stack:
    def __init__(self, *parts):
        self.spots = {p: (ref, i) for ref, planes in parts for i, p in enumerate(planes)}

    def __getitem__(self, at):
        if isinstance(at, tuple):
            ref, i = self.spots[at[1]]
            return ref[at[0], i]
        ref, i = self.spots[at]
        return ref[i]

    def cut(self, at, rows):
        if isinstance(at, tuple):
            ref, i = self.spots[at[1]]
            return ref[at[0], i, rows, :]
        ref, i = self.spots[at]
        return ref[i, rows, :]


def vmem(shape):
    return pltpu.VMEM(shape, F32)


def row_spots(planes):
    spots, at = {}, 0
    for k, reach in enumerate(ROWS):
        for p in range(planes):
            spots[k, p] = slice(at, at + reach)
            at += reach
    return spots, at


def plane_spots(heights):
    spots, at = {}, 0
    for k, count in enumerate(PLANES):
        for i in range(count):
            spots[k, i] = slice(at, at + heights[k])
            at += heights[k]
    return spots, at


def middle_spots(rows):
    return plane_spots([rows] * 5)


def corner_spots():
    spots, at = {}, 0
    for k, count in enumerate(PLANES):
        for distance in range(1, count + 1):
            reach = ROWS[k] if distance < count else count
            spots[k, distance] = at, reach
            at += 2 * reach
    return spots, at


def pack_rows(
    forces, modulus, occupancy, bonded, own, to_c, to_d, to_a, to_b,
    modulus_here, occupancy_here, bonded_here, arrived,
):
    pairs = [(modulus, modulus_here), (occupancy, occupancy_here), (bonded, bonded_here)]
    pairs += [(forces.at[k], own.at[k]) for k in range(3)]
    copies = [pltpu.make_async_copy(*pair, arrived.at[i]) for i, pair in enumerate(pairs)]
    for copy in copies:
        copy.start()
    planes, rows = own.shape[1], own.shape[2]
    for copy in copies[:2]:
        copy.wait()
    for p in range(planes):
        own[3, p] = modulus_here[p] * occupancy_here[p].astype(F32)
    copies[2].wait()
    for p in range(planes):
        own[4, p] = MASS_TERM + PENALTY * bonded_here[p].astype(F32)
    for copy in copies[3:]:
        copy.wait()
    is_odd = odd("brick")
    spots, _ = row_spots(planes)
    for (k, p), spot in spots.items():
        first = own[k, p, 0 : ROWS[k], :]
        last = own[k, p, rows - ROWS[k] : rows, :]
        to_c[spot, :] = jnp.where(is_odd, first, last)
        to_d[spot, :] = jnp.where(is_odd, last, first)
    is_odd = odd("len")
    for (k, i), spot in middle_spots(rows)[0].items():
        first, last = own[k, i], own[k, planes - PLANES[k] + i]
        to_a[spot, :] = jnp.where(is_odd, first, last)
        to_b[spot, :] = jnp.where(is_odd, last, first)


def rows_beside(from_c, from_d):
    is_odd = odd("brick")

    def get(spot, reach):
        low, high = slice(spot.stop - reach, spot.stop), slice(spot.start, spot.start + reach)
        return (
            jnp.where(is_odd, from_c[low, :], from_d[low, :]),
            jnp.where(is_odd, from_d[high, :], from_c[high, :]),
        )

    return get


def pack_corners(planes, from_c, middle_b, from_d, middle_a, to_a, to_b):
    del middle_a, middle_b
    is_odd = odd("len")
    from_rows, _ = row_spots(planes)
    beside = rows_beside(from_c, from_d)
    for (k, distance), (at, reach) in corner_spots()[0].items():
        firsts = beside(from_rows[k, distance - 1], reach)
        lasts = beside(from_rows[k, planes - distance], reach)
        for half, (first, last) in enumerate(zip(firsts, lasts)):
            span = slice(at + half * reach, at + (half + 1) * reach)
            to_a[span, :] = jnp.where(is_odd, first, last)
            to_b[span, :] = jnp.where(is_odd, last, first)


def inner_planes(planes):
    return [range(HALO + i, HALO + planes - i) for i in (1, 2, 3)]


def kept_planes(planes):
    weighed, swept, _ = inner_planes(planes)
    own = range(HALO, HALO + planes)
    end = planes + 2 * HALO
    wide, close = range(2, end - 2), range(3, end - 3)
    pairs = ((swept, wide), (own, close), (own, wide), (weighed, close), (weighed, close))
    return [(inner, [p for p in every if p not in inner]) for inner, every in pairs]


def keep(kept_rows, targets, arrays, numbers):
    for k in range(2):
        for i, p in enumerate(numbers[k]):
            for c in range(3):
                targets[k][c, i] = arrays[k][c, p][kept_rows]
    for k in range(2, 5):
        for i, p in enumerate(numbers[k]):
            targets[k][i] = arrays[k][p][kept_rows]


def halves(x, rows):
    count = (rows.stop - rows.start) // 2
    return x[pl.ds(rows.start, count, stride=2), :] + x[pl.ds(rows.start + 1, count, stride=2), :]


def coarse_weight(lane, quarter_at, i, rows):
    sides, here, others = [
        smooth_planes(lambda j, at=at: quarter_at(j)[pl.ds(at, rows), :], i) for at in (7, 8, 9)
    ]
    return 24.0 * quarter_at(i)[pl.ds(8, rows), :] + lane.smooth(sides + 2.0 * here + others)


def fine_inner(
    own, from_c, from_d, to_a,
    source, quarter, shift, weight, step, v1, v2, rest, coarse_q, shift1, sums, cells, *more,
):
    del to_a
    planes, rows = own.shape[1], own.shape[2]
    lane = Lane(rows + 2 * WIDE, 1)
    beside = rows_beside(from_c, from_d)

    def put(k, p, r, value):
        if k < 3:
            source[k, p, r, :] = value
        elif k == 3:
            quarter[p, r, :] = 0.25 * value
        else:
            shift[p, r, :] = value

    for (k, p), spot in row_spots(planes)[0].items():
        low, high = beside(spot, ROWS[k])
        put(k, p, slice(WIDE - ROWS[k], WIDE), low)
        put(k, p, slice(WIDE, WIDE + rows), own[k, p])
        put(k, p, slice(WIDE + rows, WIDE + rows + ROWS[k]), high)

    weighed, swept, left = inner_planes(planes)
    bounds = (HALO, HALO + planes)
    source_at, quarter_at = From(source, HALO), From(quarter, HALO)
    for p, w in stiffness_sum(quarter_at, weighed, bounds, lane):
        q, s, i = quarter_at[p], shift[p - HALO], p - weighed[0]
        total = w + s
        weight[i] = total + 8.0 * q
        st = step_of(s, total + (4.0 * COUPLING) * q)
        step[i] = st
        for k in range(3):
            v1[k, i] = st * source_at[k, p]
    weight_at, step_at = From(weight, weighed[0]), From(step, weighed[0])

    def put_v2(k, p, value):
        v2[k, p - swept[0]] = value

    v1_at, v2_at, near = From(v1, weighed[0]), From(v2, swept[0]), APART
    sweep(
        lambda k, p: v1_at[k, p], quarter_at, weight_at, step_at, source_at,
        swept, (weighed[0], weighed[-1] + 1), lane, put_v2, near,
    )
    for p, _, r in defects(
        lambda k, p: v2_at[k, p], quarter_at, weight_at, source_at,
        left, (swept[0], swept[-1] + 1), lane, near,
    ):
        for k in range(3):
            rest[k, p - left[0]] = r[k]

    *kept, work = more
    half = rows // 2 + 2 * HALO
    outer = slice(WIDE - 2 * HALO, WIDE + rows + 2 * HALO)
    beyond = slice(outer.start - 2, outer.stop + 2)
    count = planes // 2
    for i in range(count):
        work[0, i] = quarter[2 * i] + quarter[2 * i + 1]
        work[1, i] = shift[2 * i] + shift[2 * i + 1]
    for f in range(2):
        for i in range(count):
            work[f, i] = lane.pair(work[f, i])
    for i in range(count):
        coarse_q[i, pl.ds(7, half + 2), :] = (0.25 * 0.125) * halves(work.at[0, i], beyond)
        shift1[i] = 0.125 * halves(work.at[1, i], outer)
    lane1 = Lane(half, 2)
    for i in range(1, count - 1):
        s = shift1[i]
        w = coarse_weight(lane1, lambda j: coarse_q.at[j], i, half)
        sums[i - 1] = jnp.where(s > 0.0, w + s, 0.0)

    inner = slice(HALO, HALO + rows // 2)
    for i in range(count // 2):
        pair = [coarse_q[2 * i + j, pl.ds(8, half), :] for j in range(2)]
        work[0, i, pl.ds(0, half), :] = lane1.pair(pair[0] + pair[1])
        work[1, i, pl.ds(0, half), :] = lane1.pair(shift1[2 * i] + shift1[2 * i + 1])
        for f, scale in enumerate((0.25 * 0.125, 0.125)):
            cells[f, i] = scale * halves(work.at[f, i], inner)
    keep(
        slice(WIDE - HALO, WIDE + rows + HALO), kept,
        (v2_at, source_at, quarter_at, weight_at, step_at),
        [x for x, _ in kept_planes(planes)],
    )


def fine_before(
    source_in, quarter_in, shift_in, weight_in, step_in, v1_in, v2_in, rest_in,
    coarse_q_in, shift1, sums_in, middle_b, middle_a, corner_b, corner_a,
    own_coarse, to_len, *more,
):
    *kept, v2_out, source_out, quarter_out, weight_out, step_out, shift_out, v1_out, work, coarse_q = more
    planes, ext_rows = quarter_in.shape[0], quarter_in.shape[1]
    ext_planes, rows = planes + 2 * HALO, ext_rows - 2 * WIDE
    lane = Lane(ext_rows, 1)

    def put(k, p, r, value):
        if k < 3:
            source_out[k, p, r, :] = value
        elif k == 3:
            quarter_out[p, r, :] = 0.25 * value
        else:
            shift_out[p, r, :] = value

    is_odd = odd("len")
    def put_both(k, distance, start, low, high):
        r = slice(start, start + low.shape[0])
        put(k, HALO - distance, r, low)
        put(k, HALO + planes - 1 + distance, r, high)

    def sides(a, b):
        return jnp.where(is_odd, a, b), jnp.where(is_odd, b, a)

    spots = middle_spots(rows)[0]
    for k, count in enumerate(PLANES):
        for distance in range(1, count + 1):
            low = sides(*[x[spots[k, count - distance], :] for x in (middle_a, middle_b)])[0]
            high = sides(*[x[spots[k, distance - 1], :] for x in (middle_a, middle_b)])[1]
            put_both(k, distance, WIDE, low, high)
    for (k, distance), (at, reach) in corner_spots()[0].items():
        for half, start in enumerate((WIDE - reach, WIDE + rows)):
            span = slice(at + half * reach, at + (half + 1) * reach)
            put_both(k, distance, start, *sides(corner_a[span, :], corner_b[span, :]))

    weighed, swept, left = inner_planes(planes)
    here = range(HALO, HALO + planes)
    source, quarter, shift = [
        Either(x, here, y)
        for x, y in ((source_in, source_out), (quarter_in, quarter_out), (shift_in, shift_out))
    ]
    weight, step, v1 = [
        Either(x, weighed, y)
        for x, y in ((weight_in, weight_out), (step_in, step_out), (v1_in, v1_out))
    ]
    v2 = Either(v2_in, swept, v2_out)

    bounds, near = (0, ext_planes), APART
    others = [p for p in range(1, ext_planes - 1) if p not in weighed]
    for p, w in stiffness_sum(quarter, others, bounds, lane):
        q, s = quarter[p], shift[p]
        total = w + s
        weight_out[p] = total + 8.0 * q
        st = step_of(s, total + (4.0 * COUPLING) * q)
        step_out[p] = st
        for k in range(3):
            v1_out[k, p] = st * source[k, p]

    numbers = [x for _, x in kept_planes(planes)]
    kept_rows = slice(WIDE - HALO, WIDE + rows + HALO)

    def put_v2(k, p, value):
        v2_out[k, p] = value
        kept[0][k, numbers[0].index(p)] = value[kept_rows]

    sweep(
        lambda k, p: v1[k, p], quarter, weight, step, source,
        [p for p in range(2, ext_planes - 2) if p not in swept], bounds, lane, put_v2, near,
    )

    half = rows // 2 + 2 * HALO
    outer = slice(WIDE - 2 * HALO, WIDE + rows + 2 * HALO)
    beyond = slice(outer.start - 2, outer.stop + 2)
    coarse_planes = planes // 2
    rest = {p: [rest_in[k, p - left[0]] for k in range(3)] for p in left}
    for p, _, r in defects(
        lambda k, p: v2[k, p], quarter, weight, source,
        [p for p in here if p not in left], bounds, lane, near,
    ):
        rest[p] = r
    for i in range(coarse_planes):
        p = HALO + 2 * i
        for k in range(3):
            work[k, i] = rest[p][k] + rest[p + 1][k]
    for j, p in enumerate((HALO - 2, HALO + planes)):
        work[3, j] = quarter[p] + quarter[p + 1]
    for k in range(4):
        for i in range(2 if k == 3 else coarse_planes):
            work[k, i] = lane.pair(work[k, i])
    for i in range(coarse_planes):
        for k in range(3):
            own_coarse[k, i] = 0.125 * halves(work.at[k, i], outer)

    for j in range(2):
        coarse_q[j, pl.ds(7, half + 2), :] = (0.25 * 0.125) * halves(work.at[3, j], beyond)

    def quarter1(i):
        if i < 0:
            return coarse_q.at[0]
        return coarse_q.at[1] if i == coarse_planes else coarse_q_in.at[i]

    lane1 = Lane(half, 2)
    for i in range(coarse_planes):
        own_coarse[3, i] = coarse_q_in[i, pl.ds(8, half), :]
        if 0 < i < coarse_planes - 1:
            own_coarse[4, i] = sums_in[i - 1]
        else:
            s = shift1[i]
            w = coarse_weight(lane1, quarter1, i, half)
            own_coarse[4, i] = jnp.where(s > 0.0, w + s, 0.0)

    even = (lane_ids((half, LANES)) & 1) == 0
    for k in range(5):
        for i in range(coarse_planes // 2):
            to_len[k, i] = jnp.where(even, own_coarse[k, 2 * i], own_coarse[k, 2 * i + 1])

    keep(kept_rows, kept, (v2, source, quarter, weight, step), [[]] + numbers[1:])


def middle_before(
    own, cells, from_b, from_a,
    to_all, v2, source, quarter, weight, step,
    v1, work,
):
    planes, ext_rows = own.shape[1], own.shape[2]
    rows = ext_rows - 2 * HALO
    ext_planes = planes + 2 * HALO
    lane = Lane(ext_rows, 2)

    def put(k, p, value):
        if k < 3:
            source[k, p] = value
        elif k == 3:
            quarter[p] = value
        else:
            weight[p] = value

    is_odd = odd("len")
    even = (lane_ids((ext_rows, LANES)) & 1) == 0
    for k in range(5):
        for p in range(planes):
            put(k, HALO + p, own[k, p])
        for i in range(HALO // 2):
            a, b = from_a[k, i], from_b[k, i]
            for start, x in (
                (0, jnp.where(is_odd, a, b)),
                (HALO + planes, jnp.where(is_odd, b, a)),
            ):
                put(k, start + 2 * i, jnp.where(even, x, turn(x, 1, 1)))
                put(k, start + 2 * i + 1, jnp.where(even, turn(x, -1, 1), x))

    for p in range(ext_planes):
        q, total = quarter[p], weight[p]
        st = step_of(total, total + (4.0 * COUPLING) * q)
        step[p] = st
        weight[p] = total + 8.0 * q
        for k in range(3):
            v1[k, p] = st * source[k, p]

    def put_v2(k, p, value):
        v2[k, p] = value

    bounds, near = (0, ext_planes), {}
    sweep(
        lambda k, p: v1[k, p], quarter, weight, step, source,
        range(1, ext_planes - 1), bounds, lane, put_v2, near,
    )
    held = {}
    half = rows // 2
    for p, _, r in defects(
        lambda k, p: v2[k, p], quarter, weight, source,
        range(HALO, HALO + planes), bounds, lane, near,
    ):
        if p % 2 == 0:
            held = r
            continue
        i = (p - HALO) // 2
        for k in range(3):
            work[k, i] = held[k] + r[k]
    for i in range(planes // 2):
        for k in range(3):
            work[k, i] = lane.pair(work[k, i])
    depth = planes // 2
    ids = lane_ids((depth * half, LANES))
    row = lax.broadcasted_iota(jnp.int32, ids.shape, 0)
    mine = ids // ROW == row % half
    lines = []
    for k in range(5):
        parts = [
            cells[k - 3, i]
            if k >= 3
            else 0.125
            * (
                work[k, i, pl.ds(HALO, half, stride=2), :]
                + work[k, i, pl.ds(HALO + 1, half, stride=2), :]
            )
            for i in range(depth)
        ]
        x = pick(jnp.concatenate(parts, axis=0), (ids % ROW) * (LANES // ROW))
        x = jnp.where(mine, x, 0.0)
        x = x + turn(x, -1, 0)
        x = x + turn(x, -2, 0)
        lines += [x[i * half : i * half + 1] for i in range(depth)]
    block = jnp.concatenate(lines * 4, axis=0)
    count = block.shape[0]
    for at in range(0, to_all.shape[0], count):
        to_all[at : at + count, :] = block


def coarse_and_after(
    bricks_before,
    table, v2_mid, source_mid, quarter_mid, weight_mid, step_mid, *more,
):
    kept_inner, kept_outer = more[:5], more[5:10]
    out, wide2, u_mid, x_mid, u_fine, x_fine = more[10:]
    brick = lax.axis_index("brick")
    slab = lax.axis_index("len")
    bricks, planes2 = wide2.shape[2] - 16, wide2.shape[1] - 4
    depth = (v2_mid.shape[1] - 2 * HALO) // 2
    lines = 5 * depth

    def field(f):
        return jnp.stack(
            [
                table[pl.ds((i // depth) * bricks * lines + f * depth + i % depth, bricks, stride=lines), :]
                for i in range(planes2)
            ],
            axis=0,
        )

    lane2, lane3 = Packed(bricks, 1), Packed(bricks, 2)
    b2, q2, s2 = [field(k) for k in range(3)], field(3), field(4)
    e2, x2 = lane2.terms(q2, s2)
    u2 = lane2.sweep([x2 * b for b in b2], e2, x2, b2)

    rest = lane2.defects(u2, e2, b2)
    joint = lane2.restrict(jnp.concatenate(rest + [0.25 * q2, s2], axis=0))
    count = planes2 // 2
    *b3, q3, s3 = [joint[i * count : (i + 1) * count] for i in range(5)]
    e3, x3 = lane3.terms(q3, s3)
    u3 = [x3 * b for b in b3]
    for _ in range(3):
        u3 = lane3.sweep(u3, e3, x3, b3)

    u2 = [u2[k] + twice_planes(u3[k]) for k in range(3)]
    for _ in range(2):
        u2 = lane2.sweep(u2, e2, x2, b2)
    wide2[...] = jnp.zeros_like(wide2)
    for k in range(3):
        wide2[k, pl.ds(2, planes2), pl.ds(8, bricks), :] = u2[k]

    v2_fine, source_fine, quarter_fine, weight_fine, step_fine = [
        Stack((inner, numbers[0]), (outer, numbers[1]))
        for inner, outer, numbers in zip(
            kept_inner, kept_outer, kept_planes(x_fine.shape[1] - 2 * HALO)
        )
    ]
    planes1 = v2_mid.shape[1]
    rows1 = v2_mid.shape[2]
    lane1 = Lane(rows1, 2)
    bounds1, beside1 = (0, planes1), {}
    line_at = brick - bricks_before(brick) + 8
    half_shape = (rows1 // 2, LANES)
    ids, row = lane_ids(half_shape), lax.broadcasted_iota(jnp.int32, half_shape, 0)
    lanes = ROW * ((row + 2) % 4) + ids // (LANES // ROW)
    for k in range(3):
        for i in range(planes1 // 2):
            low, own, high = [
                jnp.broadcast_to(
                    wide2[k, depth * slab + i, pl.ds(line_at + at, 1), :], half_shape
                )
                for at in (-1, 0, 1)
            ]
            piece = pick(jnp.where(row < 2, low, jnp.where(row < 6, own, high)), lanes)
            for half in range(2):
                x_mid[k, i, pl.ds(half, rows1 // 2, stride=2), :] = piece
            both = x_mid[k, i]
            for p in (2 * i, 2 * i + 1):
                if 1 <= p < planes1 - 1:
                    u_mid[k, p] = v2_mid[k, p] + both

    def put_mid(k, p, value):
        x_mid[k, p] = value

    sweep(
        lambda k, p: u_mid[k, p], quarter_mid, weight_mid, step_mid, source_mid,
        range(2, planes1 - 2), bounds1, lane1, put_mid, beside1,
    )

    def put_mid_last(k, p, value):
        u_mid[k, p] = value

    sweep(
        lambda k, p: x_mid[k, p], quarter_mid, weight_mid, step_mid, source_mid,
        range(3, planes1 - 3), bounds1, lane1, put_mid_last, beside1,
    )

    planes0, rows0 = x_fine.shape[1], x_fine.shape[2]
    lane0 = Lane(rows0, 1)
    bounds0, beside0 = (0, planes0), {}
    half_rows = rows0 // 2
    for k in range(3):
        for i in range(3, planes1 - 3):
            piece = u_mid[k, i, pl.ds(2, half_rows), :]
            p = 2 * i - HALO
            for half in range(2):
                x_fine[k, p, pl.ds(half, half_rows, stride=2), :] = piece
            both = x_fine[k, p]
            for at in (p, p + 1):
                u_fine[k, at] = v2_fine[k, at] + both

    def put_fine(k, p, value):
        x_fine[k, p] = value

    sweep(
        lambda k, p: u_fine[k, p], quarter_fine, weight_fine, step_fine, source_fine,
        range(3, planes0 - 3), bounds0, lane0, put_fine, beside0,
    )

    def put_out(k, p, value):
        out[k, p - HALO] = value

    own_rows = slice(HALO, rows0 - HALO)
    sweep_rows(
        lambda k, p, r: x_fine[k, p, r, :], quarter_fine, weight_fine, step_fine, source_fine,
        range(HALO, planes0 - HALO), own_rows, Lane(rows0 - 2 * HALO, 1), put_out,
    )


def call(kernel, outs, scratch=(), name=None, **more):
    return pl.pallas_call(
        kernel,
        out_shape=[jax.ShapeDtypeStruct(shape, F32) for shape in outs],
        scratch_shapes=[vmem(x) if isinstance(x, tuple) else x for x in scratch],
        compiler_params=pltpu.CompilerParams(vmem_limit_bytes=40 * 1024 * 1024),
        name=name,
        **more,
    )


def swap(x, axis, first):
    count = lax.axis_size(axis)
    pairs = []
    for i in range(first, count - 1, 2):
        pairs += [(i, i + 1), (i + 1, i)]
    return lax.ppermute(x, axis, pairs)


def body(forces, modulus, occupancy, bonded):
    planes, rows = modulus.shape[0], modulus.shape[1]
    slabs, bricks = lax.axis_size("len"), lax.axis_size("brick")
    ext, ext_rows = planes + 2 * HALO, rows + 2 * WIDE
    half, half_rows = planes // 2, rows // 2
    mid, mid_rows = half + 2 * HALO, half_rows + 2 * HALO

    side, block = (row_spots(planes)[1], LANES), (planes, rows, LANES)
    middle_side, corner = (middle_spots(rows)[1], LANES), (corner_spots()[1], LANES)
    here = [
        pltpu.with_memory_space_constraint(x, pltpu.HBM)
        for x in (forces, modulus, occupancy, bonded)
    ]
    own, to_c, to_d, to_a, to_b = call(
        pack_rows,
        [(5,) + block, side, side, middle_side, middle_side],
        [block, pltpu.VMEM(block, jnp.int32), pltpu.VMEM(block, jnp.int32)]
        + [pltpu.SemaphoreType.DMA((6,))],
        name="pack_rows",
        in_specs=[pl.BlockSpec(memory_space=pltpu.HBM)] * 4,
    )(*here)
    from_c = swap(to_c, "brick", 0)
    middle_b = swap(to_b, "len", 1)
    from_d = swap(to_d, "brick", 1)
    middle_a = swap(to_a, "len", 0)
    to_a, to_b = call(
        functools.partial(pack_corners, planes),
        [corner, corner],
        name="pack_corners",
        in_specs=[pl.BlockSpec(memory_space=x) for x in (pltpu.VMEM, pl.ANY) * 2],
    )(from_c, middle_b, from_d, middle_a)
    corner_a = swap(to_a, "len", 0)
    corner_b = swap(to_b, "len", 1)

    field, cell = (3, ext, ext_rows, LANES), (ext, ext_rows, LANES)
    line = (rows + 2 * HALO, LANES)
    block = (planes, ext_rows, LANES)
    weighed, swept, left = [(len(x), ext_rows, LANES) for x in inner_planes(planes)]
    kept_inner, kept_outer = [
        [
            ((3,) if k < 2 else ()) + (len(numbers[part]),) + line
            for k, numbers in enumerate(kept_planes(planes))
        ]
        for part in range(2)
    ]
    coarse = (half, mid_rows + 16, LANES)
    inner = call(
        fine_inner,
        [(3,) + block, block, block, weighed, weighed]
        + [(3,) + weighed, (3,) + swept, (3,) + left]
        + [coarse, (half, mid_rows, LANES), (half - 2, mid_rows, LANES)]
        + [(2, half // 2, half_rows // 2, LANES)]
        + kept_inner,
        [(2, half, ext_rows, LANES)],
        name="fine_inner",
        in_specs=[pl.BlockSpec(memory_space=pltpu.VMEM)] * 3
        + [pl.BlockSpec(memory_space=pl.ANY)],
        cost_estimate=pl.CostEstimate(flops=10**7, bytes_accessed=4 * 10**6, transcendentals=0),
    )(own, from_c, from_d, to_b)
    inner, cells, kept_inner = inner[:11], inner[11], inner[12:]
    own, to_len, *kept_outer = call(
        fine_before,
        [(5, half, mid_rows, LANES), (5, half // 2, mid_rows, LANES)] + kept_outer,
        [field, field, cell, cell, cell, cell, field]
        + [(4, half, ext_rows, LANES), (2,) + coarse[1:]],
        name="fine_before",
    )(*inner, middle_b, middle_a, corner_b, corner_a)
    from_a = swap(to_len, "len", 0)
    from_b = swap(to_len, "len", 1)

    field1, cell1 = (3, mid, mid_rows, LANES), (mid, mid_rows, LANES)
    depth = half // 2
    lines = 5 * depth
    to_all, *middle = call(
        middle_before,
        [(slabs * bricks * lines, LANES)] + [field1, field1, cell1, cell1, cell1],
        [field1, (3, depth, mid_rows, LANES)],
        name="middle_before",
    )(own, cells, from_b, from_a)

    to_all = to_all.reshape(-1, 2, LANES)
    table = lax.all_to_all(to_all, BOTH, 0, 0, tiled=True).reshape(-1, LANES)
    window = bricks if bricks <= 8 else 16

    def first_brick(brick):
        return jnp.clip(brick - 4, 0, bricks - window)

    if window < bricks:
        table = lax.dynamic_slice_in_dim(
            table.reshape(slabs, bricks * lines, LANES),
            first_brick(lax.axis_index("brick")) * lines, window * lines, axis=1,
        ).reshape(slabs * window * lines, LANES)
    planes2 = slabs * depth
    (out,) = call(
        functools.partial(coarse_and_after, first_brick),
        [forces.shape],
        [(3, planes2 + 4, window + 16, LANES), field1, field1]
        + [(3, ext, rows + 2 * HALO, LANES)] * 2,
        name="coarse_and_after",
    )(table, *middle, *kept_inner, *kept_outer)
    return out


def solution(mesh):
    cells = P("len", "brick", None)
    forces = P(None, "len", "brick", None)
    return jax.shard_map(
        body, mesh=mesh, in_specs=(forces, cells, cells, cells), out_specs=forces, check_vma=False
    )
```

```python
import functools

import jax
import jax.numpy as jnp
from jax import lax
from jax.experimental import pallas as pl
from jax.experimental.pallas import tpu as pltpu
from jax.sharding import PartitionSpec as P

DAMPING = 0.6
COUPLING = 0.2
MASS_TERM = 0.1
PENALTY = 20.0

HALO = 4
WIDE = 12
ROWS = (10, 10, 10, 11, 10)
PLANES = (3, 3, 3, 4, 3)
LANES = 128
ROW = 32
F32 = jnp.float32
BOTH = ("len", "brick")


def lane_ids(shape):
    return lax.broadcasted_iota(jnp.int32, shape, len(shape) - 1)


def turn(x, by, axis):
    return pltpu.roll(x, by % x.shape[axis], axis)


def pick(x, lanes):
    return jnp.take_along_axis(x, lanes, axis=1, mode="promise_in_bounds")


class Lane:
    def __init__(self, rows, wide):
        ids = lane_ids((rows, LANES))
        self.wide = wide
        self.low = jnp.where(ids >= wide, 0.5, 0.0).astype(F32)
        self.high = jnp.where(ids < LANES - wide, 0.5, 0.0).astype(F32)
        self.first = (ids & wide) == 0

    def smooth(self, x):
        return x + self.low * turn(x, self.wide, 1) + self.high * turn(x, -self.wide, 1)

    def beside(self, q):
        return turn(q, self.wide, 1), turn(q, -self.wide, 1)

    def blend(self, x, y, q, before, after):
        return (q * x + y) + (
            self.low * turn(after * x + y, self.wide, 1)
            + self.high * turn(before * x + y, -self.wide, 1)
        )

    def pair(self, x):
        return x + swap_lanes(x, self.wide, self.first)

    def rows(self, x):
        pair = x + turn(x, 1, 0)
        return pair + turn(pair, -1, 0)


def swap_lanes(x, by, first):
    return jnp.where(first, turn(x, -by, 1), turn(x, by, 1))


class Packed:
    def __init__(self, bricks, wide):
        shape = (1, bricks, LANES)
        ids = lane_ids(shape)
        line = lax.broadcasted_iota(jnp.int32, shape, 1)
        self.wide = wide
        top, bottom = ids < ROW * wide, ids >= LANES - ROW * wide

        def number(mask, value):
            return jnp.where(mask, value, 0.0).astype(F32)

        self.low = number((ids & (ROW - 1)) >= wide, 0.5)
        self.high = number((ids & (ROW - 1)) < ROW - wide, 0.5)
        self.not_top, self.not_bottom = number(~top, 1.0), number(~bottom, 1.0)
        self.top = number(top & (line > 0), 1.0)
        self.bottom = number(bottom & (line < bricks - 1), 1.0)
        self.odd_row, self.odd_lane = number((ids & ROW) > 0, 1.0), number((ids & 1) > 0, 1.0)

    def smooth(self, x):
        return x + (self.low * turn(x, self.wide, 2) + self.high * turn(x, -self.wide, 2))

    def rows(self, x):
        back = turn(x, ROW * self.wide, 2)
        ahead = back if self.wide == 2 else turn(x, -ROW, 2)
        before = self.not_top * back + self.top * turn(back, 1, 1)
        after = self.not_bottom * ahead + self.bottom * turn(ahead, -1, 1)
        return (x + x) + (before + after)

    def pair(self, x):
        for by, is_odd in ((ROW, self.odd_row), (1, self.odd_lane)):
            x = x + (is_odd * turn(x, by, 2) + (1.0 - is_odd) * turn(x, -by, 2))
        return x

    def planes(self, x):
        none = jnp.zeros_like(x[:1])
        above = jnp.concatenate([x[1:], none], axis=0)
        below = jnp.concatenate([none, x[:-1]], axis=0)
        return (x + x) + (above + below)

    def full(self, x):
        return self.smooth(self.rows(self.planes(x)))

    def terms(self, q, s):
        total = 24.0 * q + self.full(q) + s
        q = [jnp.concatenate([x] * 3, axis=0) for x in (q, turn(q, self.wide, 2), turn(q, -self.wide, 2))]
        weight = total + 8.0 * q[0][: total.shape[0]]
        return (q, weight), DAMPING / (total + (4.0 * COUPLING) * q[0][: total.shape[0]])

    def defects(self, v, terms, source):
        (q3, before, after), weight = terms
        count = weight.shape[0]
        q = q3[:count]
        stack = [self.planes(x) for x in v] + [self.planes(q * x) for x in v]
        both = self.rows(jnp.concatenate(stack, axis=0))
        x, y = both[: 3 * count], both[3 * count :]
        sums = (q3 * x + y) + (
            self.low * turn(after * x + y, self.wide, 2)
            + self.high * turn(before * x + y, -self.wide, 2)
        )
        coupled = (4.0 * COUPLING) * q * (v[0] + v[1] + v[2])
        return [
            source[k] - weight * v[k] + sums[k * count : (k + 1) * count] - coupled
            for k in range(3)
        ]

    def sweep(self, v, terms, step, source):
        r = self.defects(v, terms, source)
        return [v[k] + step * r[k] for k in range(3)]

    def restrict(self, x):
        x = x.reshape((x.shape[0] // 2, 2) + x.shape[1:])
        return 0.125 * self.pair(x[:, 0] + x[:, 1])


def twice_planes(x):
    return jnp.concatenate([x[i // 2 : i // 2 + 1] for i in range(2 * x.shape[0])], axis=0)


def smooth_planes(get, p):
    below, here, above = get(p - 1), get(p), get(p + 1)
    total = here + here
    if below is not None:
        total = total + below
    if above is not None:
        total = total + above
    return total


def remember(get):
    seen = {}

    def cached(p):
        if p not in seen:
            seen[p] = get(p)
        return seen[p]

    return cached


def within(get, low, high):
    return lambda p: get(p) if low <= p < high else None


APART = {}


def gathered(field, quarter, planes, bounds, lane, beside=None):
    beside = {} if beside is None else beside
    q_at = remember(lambda p: quarter[p])
    v_at = [remember(lambda p, k=k: field(k, p)) for k in range(3)]
    w_at = [remember(lambda p, k=k: q_at(p) * v_at[k](p)) for k in range(3)]
    pairs = [
        [remember(lambda p, x=x: x(p) + x(p + 1)) for x in group] for group in (v_at, w_at)
    ]
    for p in planes:
        q = q_at(p)
        if p not in beside and beside is not APART:
            beside[p] = lane.beside(q)
        sums = []
        for k in range(3):
            x, y = [lane.rows(group[k](p - 1) + group[k](p)) for group in pairs]
            if beside is APART:
                sums.append(q * lane.smooth(x) + lane.smooth(y))
            else:
                sums.append(lane.blend(x, y, q, *beside[p]))
        yield p, [v_at[k](p) for k in range(3)], q, sums


def defects(field, quarter, weight, source, planes, bounds, lane, beside=None):
    for p, v, q, sums in gathered(field, quarter, planes, bounds, lane, beside):
        coupled = (4.0 * COUPLING) * q * (v[0] + v[1] + v[2])
        e = weight[p]
        yield p, v, [source[k, p] - e * v[k] + sums[k] - coupled for k in range(3)]


def sweep(field, quarter, weight, step, source, planes, bounds, lane, put, beside=None):
    for p, v, r in defects(field, quarter, weight, source, planes, bounds, lane, beside):
        s = step[p]
        for k in range(3):
            put(k, p, v[k] + s * r[k])


def defects_rows(field, quarter, weight, source, planes, rows, lane, apart=False):
    near = [slice(rows.start + by, rows.stop + by) for by in (-1, 0, 1)]
    q_at = remember(lambda p: [quarter.cut(p, r) for r in near])
    v_at = [remember(lambda p, k=k: [field(k, p, r) for r in near]) for k in range(3)]

    def over_rows(x):
        return (x[0] + x[2]) + (x[1] + x[1])

    rows_v = [remember(lambda p, k=k: over_rows(v_at[k](p))) for k in range(3)]
    rows_w = [
        remember(lambda p, k=k: over_rows([q * v for q, v in zip(q_at(p), v_at[k](p))]))
        for k in range(3)
    ]
    pairs = [
        [remember(lambda p, x=x: x(p) + x(p + 1)) for x in group] for group in (rows_v, rows_w)
    ]
    for p in planes:
        q = q_at(p)[1]
        beside = None if apart else lane.beside(q)
        v = [x(p)[1] for x in v_at]
        coupled = (4.0 * COUPLING) * q * (v[0] + v[1] + v[2])
        e = weight.cut(p, rows)
        for k in range(3):
            x, y = [group[k](p - 1) + group[k](p) for group in pairs]
            sums = q * lane.smooth(x) + lane.smooth(y) if apart else lane.blend(x, y, q, *beside)
            yield k, p, v[k], source.cut((k, p), rows) - e * v[k] + sums - coupled


def stiffness_sum(quarter, planes, bounds, lane):
    q_at = remember(within(lambda p: quarter[p], *bounds))
    for p in planes:
        yield p, 24.0 * q_at(p) + lane.smooth(lane.rows(smooth_planes(q_at, p)))


def step_of(inside, diagonal):
    return jnp.where(inside > 0.0, DAMPING / diagonal, 0.0)


def odd(axis):
    return lax.rem(lax.axis_index(axis), 2) == 1


class Stack:
    def __init__(self, *parts):
        self.spots = {p: (ref, i) for ref, planes in parts for i, p in enumerate(planes)}

    def __getitem__(self, at):
        if isinstance(at, tuple):
            ref, i = self.spots[at[1]]
            return ref[at[0], i]
        ref, i = self.spots[at]
        return ref[i]

    def cut(self, at, rows):
        if isinstance(at, tuple):
            ref, i = self.spots[at[1]]
            return ref[at[0], i, rows, :]
        ref, i = self.spots[at]
        return ref[i, rows, :]


def vmem(shape):
    return pltpu.VMEM(shape, F32)


def row_spots(planes):
    spots, at = {}, 0
    for k, reach in enumerate(ROWS):
        for p in range(planes):
            spots[k, p] = slice(at, at + reach)
            at += reach
    return spots, at


def plane_spots(heights):
    spots, at = {}, 0
    for k, count in enumerate(PLANES):
        for i in range(count):
            spots[k, i] = slice(at, at + heights[k])
            at += heights[k]
    return spots, at


def middle_spots(rows):
    return plane_spots([rows] * 5)


def corner_spots():
    spots, at = {}, 0
    for k, count in enumerate(PLANES):
        for distance in range(1, count + 1):
            reach = ROWS[k] if distance < count else count
            spots[k, distance] = at, reach
            at += 2 * reach
    return spots, at


def pack_rows(
    forces, modulus, occupancy, bonded, own, to_c, to_d, to_a, to_b,
    modulus_here, occupancy_here, bonded_here, arrived,
):
    pairs = [(modulus, modulus_here), (occupancy, occupancy_here), (bonded, bonded_here)]
    pairs += [(forces.at[k], own.at[k]) for k in range(3)]
    copies = [pltpu.make_async_copy(*pair, arrived.at[i]) for i, pair in enumerate(pairs)]
    for copy in copies:
        copy.start()
    planes, rows = own.shape[1], own.shape[2]
    for copy in copies[:2]:
        copy.wait()
    for p in range(planes):
        own[3, p] = modulus_here[p] * occupancy_here[p].astype(F32)
    copies[2].wait()
    for p in range(planes):
        own[4, p] = MASS_TERM + PENALTY * bonded_here[p].astype(F32)
    for copy in copies[3:]:
        copy.wait()
    is_odd = odd("brick")
    spots, _ = row_spots(planes)
    for (k, p), spot in spots.items():
        first = own[k, p, 0 : ROWS[k], :]
        last = own[k, p, rows - ROWS[k] : rows, :]
        to_c[spot, :] = jnp.where(is_odd, first, last)
        to_d[spot, :] = jnp.where(is_odd, last, first)
    is_odd = odd("len")
    for (k, i), spot in middle_spots(rows)[0].items():
        first, last = own[k, i], own[k, planes - PLANES[k] + i]
        to_a[spot, :] = jnp.where(is_odd, first, last)
        to_b[spot, :] = jnp.where(is_odd, last, first)


def rows_beside(from_c, from_d):
    is_odd = odd("brick")

    def get(spot, reach):
        low, high = slice(spot.stop - reach, spot.stop), slice(spot.start, spot.start + reach)
        return (
            jnp.where(is_odd, from_c[low, :], from_d[low, :]),
            jnp.where(is_odd, from_d[high, :], from_c[high, :]),
        )

    return get


def pack_corners(planes, from_c, middle_b, from_d, middle_a, to_a, to_b):
    del middle_a, middle_b
    is_odd = odd("len")
    from_rows, _ = row_spots(planes)
    beside = rows_beside(from_c, from_d)
    for (k, distance), (at, reach) in corner_spots()[0].items():
        firsts = beside(from_rows[k, distance - 1], reach)
        lasts = beside(from_rows[k, planes - distance], reach)
        for half, (first, last) in enumerate(zip(firsts, lasts)):
            span = slice(at + half * reach, at + (half + 1) * reach)
            to_a[span, :] = jnp.where(is_odd, first, last)
            to_b[span, :] = jnp.where(is_odd, last, first)


def inner_planes(planes):
    return [range(HALO + i, HALO + planes - i) for i in (1, 2, 3)]


def kept_planes(planes):
    weighed, swept, _ = inner_planes(planes)
    own = range(HALO, HALO + planes)
    end = planes + 2 * HALO
    wide, close = range(2, end - 2), range(3, end - 3)
    pairs = ((swept, wide), (own, close), (own, wide), (weighed, close), (weighed, close))
    return [(inner, [p for p in every if p not in inner]) for inner, every in pairs]


def keep(kept_rows, targets, arrays, numbers):
    for k in range(2):
        for i, p in enumerate(numbers[k]):
            for c in range(3):
                targets[k][c, i] = arrays[k][c, p][kept_rows]
    for k in range(2, 5):
        for i, p in enumerate(numbers[k]):
            targets[k][i] = arrays[k][p][kept_rows]


def halves(x, rows):
    count = (rows.stop - rows.start) // 2
    return x[pl.ds(rows.start, count, stride=2), :] + x[pl.ds(rows.start + 1, count, stride=2), :]


def coarse_weight(lane, quarter_at, i, rows):
    sides, here, others = [
        smooth_planes(lambda j, at=at: quarter_at(j)[pl.ds(at, rows), :], i) for at in (7, 8, 9)
    ]
    return 24.0 * quarter_at(i)[pl.ds(8, rows), :] + lane.smooth(sides + 2.0 * here + others)


def fine_inner(
    own, from_c, from_d, to_a,
    source, quarter, shift, weight, step, v1, v2, rest, coarse_q, shift1, sums, cells, *more,
):
    del to_a
    planes, rows = own.shape[1], own.shape[2]
    lane = Lane(rows + 2 * WIDE, 1)
    beside = rows_beside(from_c, from_d)

    def put(k, p, r, value):
        if k < 3:
            source[k, p, r, :] = value
        elif k == 3:
            quarter[p, r, :] = 0.25 * value
        else:
            shift[p, r, :] = value

    for (k, p), spot in row_spots(planes)[0].items():
        low, high = beside(spot, ROWS[k])
        put(k, p, slice(WIDE - ROWS[k], WIDE), low)
        put(k, p, slice(WIDE, WIDE + rows), own[k, p])
        put(k, p, slice(WIDE + rows, WIDE + rows + ROWS[k]), high)

    weighed, swept, left = inner_planes(planes)
    bounds = (HALO, HALO + planes)
    own_planes = range(HALO, HALO + planes)
    source_at, quarter_at = Stack((source, own_planes)), Stack((quarter, own_planes))
    for p, w in stiffness_sum(quarter_at, weighed, bounds, lane):
        q, s, i = quarter_at[p], shift[p - HALO], p - weighed[0]
        total = w + s
        weight[i] = total + 8.0 * q
        st = step_of(s, total + (4.0 * COUPLING) * q)
        step[i] = st
        for k in range(3):
            v1[k, i] = st * source_at[k, p]
    weight_at, step_at = Stack((weight, weighed)), Stack((step, weighed))

    def put_v2(k, p, value):
        v2[k, p - swept[0]] = value

    v1_at, v2_at, near = Stack((v1, weighed)), Stack((v2, swept)), APART
    sweep(
        lambda k, p: v1_at[k, p], quarter_at, weight_at, step_at, source_at,
        swept, (weighed[0], weighed[-1] + 1), lane, put_v2, near,
    )
    outer = slice(WIDE - 2 * HALO, WIDE + rows + 2 * HALO)
    lane_outer = Lane(outer.stop - outer.start, 1)
    for k, p, _, r in defects_rows(
        lambda k, p, r: v2_at.cut((k, p), r), quarter_at, weight_at, source_at,
        left, outer, lane_outer, apart=True,
    ):
        rest[k, p - left[0]] = r

    *kept, work = more
    half = rows // 2 + 2 * HALO
    beyond = slice(outer.start - 2, outer.stop + 2)
    count = planes // 2
    for i in range(count):
        work[0, i] = quarter[2 * i] + quarter[2 * i + 1]
        work[1, i] = shift[2 * i] + shift[2 * i + 1]
    for f in range(2):
        for i in range(count):
            work[f, i] = lane.pair(work[f, i])
    for i in range(count):
        coarse_q[i, pl.ds(7, half + 2), :] = (0.25 * 0.125) * halves(work.at[0, i], beyond)
        shift1[i] = 0.125 * halves(work.at[1, i], outer)
    lane1 = Lane(half, 2)
    for i in range(1, count - 1):
        s = shift1[i]
        w = coarse_weight(lane1, lambda j: coarse_q.at[j], i, half)
        sums[i - 1] = jnp.where(s > 0.0, w + s, 0.0)

    inner = slice(HALO, HALO + rows // 2)
    for i in range(count // 2):
        pair = [coarse_q[2 * i + j, pl.ds(8, half), :] for j in range(2)]
        work[0, i, pl.ds(0, half), :] = lane1.pair(pair[0] + pair[1])
        work[1, i, pl.ds(0, half), :] = lane1.pair(shift1[2 * i] + shift1[2 * i + 1])
        for f, scale in enumerate((0.25 * 0.125, 0.125)):
            cells[f, i] = scale * halves(work.at[f, i], inner)
    keep(
        slice(WIDE - HALO, WIDE + rows + HALO), kept,
        (v2_at, source_at, quarter_at, weight_at, step_at),
        [x for x, _ in kept_planes(planes)],
    )


def fine_before(
    source_in, quarter_in, shift_in, weight_in, step_in, v1_in, v2_in, rest_in,
    coarse_q_in, shift1, sums_in, middle_b, middle_a, corner_b, corner_a,
    own_coarse, to_len, *more,
):
    *kept, v2_out, source_out, quarter_out, weight_out, step_out, shift_out, v1_out, work, coarse_q = more
    planes, ext_rows = quarter_in.shape[0], quarter_in.shape[1]
    ext_planes, rows = planes + 2 * HALO, ext_rows - 2 * WIDE
    lane = Lane(ext_rows, 1)

    def put(k, p, r, value):
        if k < 3:
            source_out[k, p, r, :] = value
        elif k == 3:
            quarter_out[p, r, :] = 0.25 * value
        else:
            shift_out[p, r, :] = value

    is_odd = odd("len")
    def put_both(k, distance, start, low, high):
        r = slice(start, start + low.shape[0])
        put(k, HALO - distance, r, low)
        put(k, HALO + planes - 1 + distance, r, high)

    def sides(a, b):
        return jnp.where(is_odd, a, b), jnp.where(is_odd, b, a)

    spots = middle_spots(rows)[0]
    for k, count in enumerate(PLANES):
        for distance in range(1, count + 1):
            low = sides(*[x[spots[k, count - distance], :] for x in (middle_a, middle_b)])[0]
            high = sides(*[x[spots[k, distance - 1], :] for x in (middle_a, middle_b)])[1]
            put_both(k, distance, WIDE, low, high)
    for (k, distance), (at, reach) in corner_spots()[0].items():
        for half, start in enumerate((WIDE - reach, WIDE + rows)):
            span = slice(at + half * reach, at + (half + 1) * reach)
            put_both(k, distance, start, *sides(corner_a[span, :], corner_b[span, :]))

    weighed, swept, left = inner_planes(planes)
    here = range(HALO, HALO + planes)
    every = range(ext_planes)
    source, quarter, shift, weight, step, v1, v2 = [
        Stack((outer, every), (inner, numbers))
        for inner, numbers, outer in (
            (source_in, here, source_out),
            (quarter_in, here, quarter_out),
            (shift_in, here, shift_out),
            (weight_in, weighed, weight_out),
            (step_in, weighed, step_out),
            (v1_in, weighed, v1_out),
            (v2_in, swept, v2_out),
        )
    ]

    bounds, near = (0, ext_planes), APART
    others = [p for p in range(1, ext_planes - 1) if p not in weighed]
    for p, w in stiffness_sum(quarter, others, bounds, lane):
        q, s = quarter[p], shift[p]
        total = w + s
        weight_out[p] = total + 8.0 * q
        st = step_of(s, total + (4.0 * COUPLING) * q)
        step_out[p] = st
        for k in range(3):
            v1_out[k, p] = st * source[k, p]

    numbers = [x for _, x in kept_planes(planes)]
    kept_rows = slice(WIDE - HALO, WIDE + rows + HALO)

    def put_v2(k, p, value):
        v2_out[k, p] = value
        kept[0][k, numbers[0].index(p)] = value[kept_rows]

    sweep(
        lambda k, p: v1[k, p], quarter, weight, step, source,
        [p for p in range(2, ext_planes - 2) if p not in swept], bounds, lane, put_v2, near,
    )

    half = rows // 2 + 2 * HALO
    outer = slice(WIDE - 2 * HALO, WIDE + rows + 2 * HALO)
    beyond = slice(outer.start - 2, outer.stop + 2)
    coarse_planes = planes // 2
    rest = {(k, p): rest_in[k, p - left[0]] for p in left for k in range(3)}
    height = outer.stop - outer.start
    lane_outer = Lane(height, 1)
    for k, p, _, r in defects_rows(
        lambda k, p, r: v2.cut((k, p), r), quarter, weight, source,
        [p for p in here if p not in left], outer, lane_outer, apart=True,
    ):
        rest[k, p] = r
    for i in range(coarse_planes):
        p = HALO + 2 * i
        for k in range(3):
            work[k, i, pl.ds(0, height), :] = rest[k, p] + rest[k, p + 1]
    for j, p in enumerate((HALO - 2, HALO + planes)):
        work[3, j] = quarter[p] + quarter[p + 1]
    for i in range(coarse_planes):
        for k in range(3):
            work[k, i, pl.ds(0, height), :] = lane_outer.pair(work[k, i, pl.ds(0, height), :])
    for j in range(2):
        work[3, j] = lane.pair(work[3, j])
    for i in range(coarse_planes):
        for k in range(3):
            own_coarse[k, i] = 0.125 * halves(work.at[k, i], slice(0, height))

    for j in range(2):
        coarse_q[j, pl.ds(7, half + 2), :] = (0.25 * 0.125) * halves(work.at[3, j], beyond)

    def quarter1(i):
        if i < 0:
            return coarse_q.at[0]
        return coarse_q.at[1] if i == coarse_planes else coarse_q_in.at[i]

    lane1 = Lane(half, 2)
    for i in range(coarse_planes):
        own_coarse[3, i] = coarse_q_in[i, pl.ds(8, half), :]
        if 0 < i < coarse_planes - 1:
            own_coarse[4, i] = sums_in[i - 1]
        else:
            s = shift1[i]
            w = coarse_weight(lane1, quarter1, i, half)
            own_coarse[4, i] = jnp.where(s > 0.0, w + s, 0.0)

    even = (lane_ids((half, LANES)) & 1) == 0
    for k in range(5):
        for i in range(coarse_planes // 2):
            to_len[k, i] = jnp.where(even, own_coarse[k, 2 * i], own_coarse[k, 2 * i + 1])

    keep(kept_rows, kept, (v2, source, quarter, weight, step), [[]] + numbers[1:])


def middle_before(
    own, cells, from_b, from_a,
    to_all, v2, source, quarter, weight, step,
    v1, work,
):
    planes, ext_rows = own.shape[1], own.shape[2]
    rows = ext_rows - 2 * HALO
    ext_planes = planes + 2 * HALO
    lane = Lane(ext_rows, 2)

    def put(k, p, value):
        if k < 3:
            source[k, p] = value
        elif k == 3:
            quarter[p] = value
        else:
            weight[p] = value

    is_odd = odd("len")
    even = (lane_ids((ext_rows, LANES)) & 1) == 0
    for k in range(5):
        for p in range(planes):
            put(k, HALO + p, own[k, p])
        for i in range(HALO // 2):
            a, b = from_a[k, i], from_b[k, i]
            for start, x in (
                (0, jnp.where(is_odd, a, b)),
                (HALO + planes, jnp.where(is_odd, b, a)),
            ):
                put(k, start + 2 * i, jnp.where(even, x, turn(x, 1, 1)))
                put(k, start + 2 * i + 1, jnp.where(even, turn(x, -1, 1), x))

    for p in range(ext_planes):
        q, total = quarter[p], weight[p]
        st = step_of(total, total + (4.0 * COUPLING) * q)
        step[p] = st
        weight[p] = total + 8.0 * q
        for k in range(3):
            v1[k, p] = st * source[k, p]

    def put_v2(k, p, value):
        v2[k, p] = value

    bounds, near = (0, ext_planes), {}
    sweep(
        lambda k, p: v1[k, p], quarter, weight, step, source,
        range(1, ext_planes - 1), bounds, lane, put_v2, near,
    )
    held = {}
    half = rows // 2
    for p, _, r in defects(
        lambda k, p: v2[k, p], quarter, weight, source,
        range(HALO, HALO + planes), bounds, lane, near,
    ):
        if p % 2 == 0:
            held = r
            continue
        i = (p - HALO) // 2
        for k in range(3):
            work[k, i] = held[k] + r[k]
    for i in range(planes // 2):
        for k in range(3):
            work[k, i] = lane.pair(work[k, i])
    depth = planes // 2
    ids = lane_ids((depth * half, LANES))
    row = lax.broadcasted_iota(jnp.int32, ids.shape, 0)
    mine = ids // ROW == row % half
    lines = []
    for k in range(5):
        parts = [
            cells[k - 3, i]
            if k >= 3
            else 0.125
            * (
                work[k, i, pl.ds(HALO, half, stride=2), :]
                + work[k, i, pl.ds(HALO + 1, half, stride=2), :]
            )
            for i in range(depth)
        ]
        x = pick(jnp.concatenate(parts, axis=0), (ids % ROW) * (LANES // ROW))
        x = jnp.where(mine, x, 0.0)
        x = x + turn(x, -1, 0)
        x = x + turn(x, -2, 0)
        lines += [x[i * half : i * half + 1] for i in range(depth)]
    block = jnp.concatenate(lines * 4, axis=0)
    count = block.shape[0]
    for at in range(0, to_all.shape[0], count):
        to_all[at : at + count, :] = block


def coarse_and_after(
    bricks_before,
    table, v2_mid, source_mid, quarter_mid, weight_mid, step_mid, *more,
):
    kept_inner, kept_outer = more[:5], more[5:10]
    out, wide2, u_mid, x_mid, u_fine, x_fine = more[10:]
    brick = lax.axis_index("brick")
    slab = lax.axis_index("len")
    bricks, planes2 = wide2.shape[2] - 16, wide2.shape[1] - 4
    depth = (v2_mid.shape[1] - 2 * HALO) // 2
    lines = 5 * depth

    def field(f):
        return jnp.stack(
            [
                table[pl.ds((i // depth) * bricks * lines + f * depth + i % depth, bricks, stride=lines), :]
                for i in range(planes2)
            ],
            axis=0,
        )

    lane2, lane3 = Packed(bricks, 1), Packed(bricks, 2)
    b2, q2, s2 = [field(k) for k in range(3)], field(3), field(4)
    e2, x2 = lane2.terms(q2, s2)
    u2 = lane2.sweep([x2 * b for b in b2], e2, x2, b2)

    rest = lane2.defects(u2, e2, b2)
    joint = lane2.restrict(jnp.concatenate(rest + [0.25 * q2, s2], axis=0))
    count = planes2 // 2
    *b3, q3, s3 = [joint[i * count : (i + 1) * count] for i in range(5)]
    e3, x3 = lane3.terms(q3, s3)
    u3 = [x3 * b for b in b3]
    for _ in range(3):
        u3 = lane3.sweep(u3, e3, x3, b3)

    u2 = [u2[k] + twice_planes(u3[k]) for k in range(3)]
    for _ in range(2):
        u2 = lane2.sweep(u2, e2, x2, b2)
    wide2[...] = jnp.zeros_like(wide2)
    for k in range(3):
        wide2[k, pl.ds(2, planes2), pl.ds(8, bricks), :] = u2[k]

    v2_fine, source_fine, quarter_fine, weight_fine, step_fine = [
        Stack((inner, numbers[0]), (outer, numbers[1]))
        for inner, outer, numbers in zip(
            kept_inner, kept_outer, kept_planes(x_fine.shape[1] - 2 * HALO)
        )
    ]
    planes1 = v2_mid.shape[1]
    rows1 = v2_mid.shape[2]
    lane1 = Lane(rows1, 2)
    bounds1, beside1 = (0, planes1), {}
    line_at = brick - bricks_before(brick) + 8
    half_shape = (rows1 // 2, LANES)
    ids, row = lane_ids(half_shape), lax.broadcasted_iota(jnp.int32, half_shape, 0)
    lanes = ROW * ((row + 2) % 4) + ids // (LANES // ROW)
    for k in range(3):
        for i in range(planes1 // 2):
            low, own, high = [
                jnp.broadcast_to(
                    wide2[k, depth * slab + i, pl.ds(line_at + at, 1), :], half_shape
                )
                for at in (-1, 0, 1)
            ]
            piece = pick(jnp.where(row < 2, low, jnp.where(row < 6, own, high)), lanes)
            for half in range(2):
                x_mid[k, i, pl.ds(half, rows1 // 2, stride=2), :] = piece
            both = x_mid[k, i]
            for p in (2 * i, 2 * i + 1):
                if 1 <= p < planes1 - 1:
                    u_mid[k, p] = v2_mid[k, p] + both

    def put_mid(k, p, value):
        x_mid[k, p] = value

    sweep(
        lambda k, p: u_mid[k, p], quarter_mid, weight_mid, step_mid, source_mid,
        range(2, planes1 - 2), bounds1, lane1, put_mid, beside1,
    )

    def put_mid_last(k, p, value):
        u_mid[k, p] = value

    sweep(
        lambda k, p: x_mid[k, p], quarter_mid, weight_mid, step_mid, source_mid,
        range(3, planes1 - 3), bounds1, lane1, put_mid_last, beside1,
    )

    planes0, rows0 = x_fine.shape[1], x_fine.shape[2]
    lane0 = Lane(rows0, 1)
    bounds0, beside0 = (0, planes0), {}
    half_rows = rows0 // 2
    for k in range(3):
        for i in range(3, planes1 - 3):
            piece = u_mid[k, i, pl.ds(2, half_rows), :]
            p = 2 * i - HALO
            for half in range(2):
                x_fine[k, p, pl.ds(half, half_rows, stride=2), :] = piece
            both = x_fine[k, p]
            for at in (p, p + 1):
                u_fine[k, at] = v2_fine[k, at] + both

    def put_fine(k, p, value):
        x_fine[k, p] = value

    sweep(
        lambda k, p: u_fine[k, p], quarter_fine, weight_fine, step_fine, source_fine,
        range(3, planes0 - 3), bounds0, lane0, put_fine, beside0,
    )

    own_rows = slice(HALO, rows0 - HALO)
    for k, p, v, r in defects_rows(
        lambda k, p, r: x_fine[k, p, r, :], quarter_fine, weight_fine, source_fine,
        range(HALO, planes0 - HALO), own_rows, Lane(rows0 - 2 * HALO, 1),
    ):
        out[k, p - HALO] = v + step_fine.cut(p, own_rows) * r


def call(kernel, outs, scratch=(), name=None, **more):
    return pl.pallas_call(
        kernel,
        out_shape=[jax.ShapeDtypeStruct(shape, F32) for shape in outs],
        scratch_shapes=[vmem(x) if isinstance(x, tuple) else x for x in scratch],
        compiler_params=pltpu.CompilerParams(vmem_limit_bytes=40 * 1024 * 1024),
        name=name,
        **more,
    )


def swap(x, axis, first):
    count = lax.axis_size(axis)
    pairs = []
    for i in range(first, count - 1, 2):
        pairs += [(i, i + 1), (i + 1, i)]
    return lax.ppermute(x, axis, pairs)


def body(forces, modulus, occupancy, bonded):
    planes, rows = modulus.shape[0], modulus.shape[1]
    slabs, bricks = lax.axis_size("len"), lax.axis_size("brick")
    ext, ext_rows = planes + 2 * HALO, rows + 2 * WIDE
    half, half_rows = planes // 2, rows // 2
    mid, mid_rows = half + 2 * HALO, half_rows + 2 * HALO

    side, block = (row_spots(planes)[1], LANES), (planes, rows, LANES)
    middle_side, corner = (middle_spots(rows)[1], LANES), (corner_spots()[1], LANES)
    here = [
        pltpu.with_memory_space_constraint(x, pltpu.HBM)
        for x in (forces, modulus, occupancy, bonded)
    ]
    own, to_c, to_d, to_a, to_b = call(
        pack_rows,
        [(5,) + block, side, side, middle_side, middle_side],
        [block, pltpu.VMEM(block, jnp.int32), pltpu.VMEM(block, jnp.int32)]
        + [pltpu.SemaphoreType.DMA((6,))],
        name="pack_rows",
        in_specs=[pl.BlockSpec(memory_space=pltpu.HBM)] * 4,
    )(*here)
    from_c = swap(to_c, "brick", 0)
    middle_b = swap(to_b, "len", 1)
    from_d = swap(to_d, "brick", 1)
    middle_a = swap(to_a, "len", 0)
    to_a, to_b = call(
        functools.partial(pack_corners, planes),
        [corner, corner],
        name="pack_corners",
        in_specs=[pl.BlockSpec(memory_space=x) for x in (pltpu.VMEM, pl.ANY) * 2],
    )(from_c, middle_b, from_d, middle_a)
    corner_a = swap(to_a, "len", 0)
    corner_b = swap(to_b, "len", 1)

    field, cell = (3, ext, ext_rows, LANES), (ext, ext_rows, LANES)
    line = (rows + 2 * HALO, LANES)
    block = (planes, ext_rows, LANES)
    weighed, swept, left = [(len(x), ext_rows, LANES) for x in inner_planes(planes)]
    kept_inner, kept_outer = [
        [
            ((3,) if k < 2 else ()) + (len(numbers[part]),) + line
            for k, numbers in enumerate(kept_planes(planes))
        ]
        for part in range(2)
    ]
    coarse = (half, mid_rows + 16, LANES)
    inner = call(
        fine_inner,
        [(3,) + block, block, block, weighed, weighed]
        + [(3,) + weighed, (3,) + swept, (3, left[0], 2 * mid_rows, LANES)]
        + [coarse, (half, mid_rows, LANES), (half - 2, mid_rows, LANES)]
        + [(2, half // 2, half_rows // 2, LANES)]
        + kept_inner,
        [(2, half, ext_rows, LANES)],
        name="fine_inner",
        in_specs=[pl.BlockSpec(memory_space=pltpu.VMEM)] * 3
        + [pl.BlockSpec(memory_space=pl.ANY)],
        cost_estimate=pl.CostEstimate(flops=10**7, bytes_accessed=4 * 10**6, transcendentals=0),
    )(own, from_c, from_d, to_b)
    inner, cells, kept_inner = inner[:11], inner[11], inner[12:]
    own, to_len, *kept_outer = call(
        fine_before,
        [(5, half, mid_rows, LANES), (5, half // 2, mid_rows, LANES)] + kept_outer,
        [field, field, cell, cell, cell, cell, field]
        + [(4, half, ext_rows, LANES), (2,) + coarse[1:]],
        name="fine_before",
    )(*inner, middle_b, middle_a, corner_b, corner_a)
    from_a = swap(to_len, "len", 0)
    from_b = swap(to_len, "len", 1)

    field1, cell1 = (3, mid, mid_rows, LANES), (mid, mid_rows, LANES)
    depth = half // 2
    lines = 5 * depth
    to_all, *middle = call(
        middle_before,
        [(slabs * bricks * lines, LANES)] + [field1, field1, cell1, cell1, cell1],
        [field1, (3, depth, mid_rows, LANES)],
        name="middle_before",
    )(own, cells, from_b, from_a)

    to_all = to_all.reshape(-1, 2, LANES)
    table = lax.all_to_all(to_all, BOTH, 0, 0, tiled=True).reshape(-1, LANES)
    window = bricks if bricks <= 8 else 16

    def first_brick(brick):
        return jnp.clip(brick - 4, 0, bricks - window)

    if window < bricks:
        table = lax.dynamic_slice_in_dim(
            table.reshape(slabs, bricks * lines, LANES),
            first_brick(lax.axis_index("brick")) * lines, window * lines, axis=1,
        ).reshape(slabs * window * lines, LANES)
    planes2 = slabs * depth
    (out,) = call(
        functools.partial(coarse_and_after, first_brick),
        [forces.shape],
        [(3, planes2 + 4, window + 16, LANES), field1, field1]
        + [(3, ext, rows + 2 * HALO, LANES)] * 2,
        name="coarse_and_after",
    )(table, *middle, *kept_inner, *kept_outer)
    return out


def solution(mesh):
    cells = P("len", "brick", None)
    forces = P(None, "len", "brick", None)
    return jax.shard_map(
        body, mesh=mesh, in_specs=(forces, cells, cells, cells), out_specs=forces, check_vma=False
    )
```

```python
import functools

import jax
import jax.numpy as jnp
from jax import lax
from jax.experimental import pallas as pl
from jax.experimental.pallas import tpu as pltpu
from jax.sharding import PartitionSpec as P

DAMPING = 0.6
COUPLING = 0.2
MASS_TERM = 0.1
PENALTY = 20.0

HALO = 4
WIDE = 12
ROWS = (10, 10, 10, 11, 10)
PLANES = (3, 3, 3, 4, 3)
LANES = 128
ROW = 32
F32 = jnp.float32
BOTH = ("len", "brick")


def lane_ids(shape):
    return lax.broadcasted_iota(jnp.int32, shape, len(shape) - 1)


def turn(x, by, axis):
    return pltpu.roll(x, by % x.shape[axis], axis)


def pick(x, lanes):
    return jnp.take_along_axis(x, lanes, axis=1, mode="promise_in_bounds")


class Lane:
    def __init__(self, rows, wide):
        ids = lane_ids((rows, LANES))
        self.wide = wide
        self.low = jnp.where(ids >= wide, 0.5, 0.0).astype(F32)
        self.high = jnp.where(ids < LANES - wide, 0.5, 0.0).astype(F32)
        self.first = (ids & wide) == 0

    def smooth(self, x):
        return x + self.low * turn(x, self.wide, 1) + self.high * turn(x, -self.wide, 1)

    def beside(self, q):
        return turn(q, self.wide, 1), turn(q, -self.wide, 1)

    def blend(self, x, y, q, before, after):
        return (q * x + y) + (
            self.low * turn(after * x + y, self.wide, 1)
            + self.high * turn(before * x + y, -self.wide, 1)
        )

    def pair(self, x):
        return x + swap_lanes(x, self.wide, self.first)

    def rows(self, x):
        pair = x + turn(x, 1, 0)
        return pair + turn(pair, -1, 0)


def swap_lanes(x, by, first):
    return jnp.where(first, turn(x, -by, 1), turn(x, by, 1))


class Packed:
    def __init__(self, bricks, wide):
        shape = (1, bricks, LANES)
        ids = lane_ids(shape)
        line = lax.broadcasted_iota(jnp.int32, shape, 1)
        self.wide = wide
        top, bottom = ids < ROW * wide, ids >= LANES - ROW * wide

        def number(mask, value):
            return jnp.where(mask, value, 0.0).astype(F32)

        self.low = number((ids & (ROW - 1)) >= wide, 0.5)
        self.high = number((ids & (ROW - 1)) < ROW - wide, 0.5)
        self.not_top, self.not_bottom = number(~top, 1.0), number(~bottom, 1.0)
        self.top = number(top & (line > 0), 1.0)
        self.bottom = number(bottom & (line < bricks - 1), 1.0)
        self.odd_row, self.odd_lane = number((ids & ROW) > 0, 1.0), number((ids & 1) > 0, 1.0)

    def smooth(self, x):
        return x + (self.low * turn(x, self.wide, 2) + self.high * turn(x, -self.wide, 2))

    def rows(self, x):
        back = turn(x, ROW * self.wide, 2)
        ahead = back if self.wide == 2 else turn(x, -ROW, 2)
        before = self.not_top * back + self.top * turn(back, 1, 1)
        after = self.not_bottom * ahead + self.bottom * turn(ahead, -1, 1)
        return (x + x) + (before + after)

    def pair(self, x):
        for by, is_odd in ((ROW, self.odd_row), (1, self.odd_lane)):
            x = x + (is_odd * turn(x, by, 2) + (1.0 - is_odd) * turn(x, -by, 2))
        return x

    def planes(self, x):
        none = jnp.zeros_like(x[:1])
        above = jnp.concatenate([x[1:], none], axis=0)
        below = jnp.concatenate([none, x[:-1]], axis=0)
        return (x + x) + (above + below)

    def full(self, x):
        return self.smooth(self.rows(self.planes(x)))

    def terms(self, q, s):
        total = 24.0 * q + self.full(q) + s
        q = [jnp.concatenate([x] * 3, axis=0) for x in (q, turn(q, self.wide, 2), turn(q, -self.wide, 2))]
        weight = total + 8.0 * q[0][: total.shape[0]]
        return (q, weight), DAMPING / (total + (4.0 * COUPLING) * q[0][: total.shape[0]])

    def defects(self, v, terms, source):
        (q3, before, after), weight = terms
        count = weight.shape[0]
        q = q3[:count]
        stack = [self.planes(x) for x in v] + [self.planes(q * x) for x in v]
        both = self.rows(jnp.concatenate(stack, axis=0))
        x, y = both[: 3 * count], both[3 * count :]
        sums = (q3 * x + y) + (
            self.low * turn(after * x + y, self.wide, 2)
            + self.high * turn(before * x + y, -self.wide, 2)
        )
        coupled = (4.0 * COUPLING) * q * (v[0] + v[1] + v[2])
        return [
            source[k] - weight * v[k] + sums[k * count : (k + 1) * count] - coupled
            for k in range(3)
        ]

    def sweep(self, v, terms, step, source):
        r = self.defects(v, terms, source)
        return [v[k] + step * r[k] for k in range(3)]

    def restrict(self, x):
        x = x.reshape((x.shape[0] // 2, 2) + x.shape[1:])
        return 0.125 * self.pair(x[:, 0] + x[:, 1])


def twice_planes(x):
    return jnp.concatenate([x[i // 2 : i // 2 + 1] for i in range(2 * x.shape[0])], axis=0)


def smooth_planes(get, p):
    below, here, above = get(p - 1), get(p), get(p + 1)
    total = here + here
    if below is not None:
        total = total + below
    if above is not None:
        total = total + above
    return total


def remember(get):
    seen = {}

    def cached(p):
        if p not in seen:
            seen[p] = get(p)
        return seen[p]

    return cached


def within(get, low, high):
    return lambda p: get(p) if low <= p < high else None


APART = {}


def gathered(field, quarter, planes, bounds, lane, beside=None):
    beside = {} if beside is None else beside
    q_at = remember(lambda p: quarter[p])
    v_at = [remember(lambda p, k=k: field(k, p)) for k in range(3)]
    w_at = [remember(lambda p, k=k: q_at(p) * v_at[k](p)) for k in range(3)]
    pairs = [
        [remember(lambda p, x=x: x(p) + x(p + 1)) for x in group] for group in (v_at, w_at)
    ]
    for p in planes:
        q = q_at(p)
        if p not in beside and beside is not APART:
            beside[p] = lane.beside(q)
        sums = []
        for k in range(3):
            x, y = [lane.rows(group[k](p - 1) + group[k](p)) for group in pairs]
            if beside is APART:
                sums.append(q * lane.smooth(x) + lane.smooth(y))
            else:
                sums.append(lane.blend(x, y, q, *beside[p]))
        yield p, [v_at[k](p) for k in range(3)], q, sums


def defects(field, quarter, weight, source, planes, bounds, lane, beside=None):
    for p, v, q, sums in gathered(field, quarter, planes, bounds, lane, beside):
        coupled = (4.0 * COUPLING) * q * (v[0] + v[1] + v[2])
        e = weight[p]
        yield p, v, [source[k, p] - e * v[k] + sums[k] - coupled for k in range(3)]


def sweep(field, quarter, weight, step, source, planes, bounds, lane, put, beside=None):
    for p, v, r in defects(field, quarter, weight, source, planes, bounds, lane, beside):
        s = step[p]
        for k in range(3):
            put(k, p, v[k] + s * r[k])


def sweep_rows(field, quarter, weight, step, source, planes, rows, lane, put, beside_at):
    near = [slice(rows.start + by, rows.stop + by) for by in (-1, 0, 1)]
    q_at = remember(lambda p: [quarter.cut(p, r) for r in near])
    v_at = [remember(lambda p, k=k: [field(k, p, r) for r in near]) for k in range(3)]

    def over_rows(x):
        return (x[0] + x[2]) + (x[1] + x[1])

    rows_v = [remember(lambda p, k=k: over_rows(v_at[k](p))) for k in range(3)]
    rows_w = [
        remember(lambda p, k=k: over_rows([q * v for q, v in zip(q_at(p), v_at[k](p))]))
        for k in range(3)
    ]
    pairs = [
        [remember(lambda p, x=x: x(p) + x(p + 1)) for x in group] for group in (rows_v, rows_w)
    ]
    for p in planes:
        q = q_at(p)[1]
        beside = beside_at(p)
        v = [x(p)[1] for x in v_at]
        coupled = (4.0 * COUPLING) * q * (v[0] + v[1] + v[2])
        e, s = weight.cut(p, rows), step.cut(p, rows)
        for k in range(3):
            x, y = [group[k](p - 1) + group[k](p) for group in pairs]
            sums = lane.blend(x, y, q, *beside)
            put(k, p, v[k] + s * (source.cut((k, p), rows) - e * v[k] + sums - coupled))


def stiffness_sum(quarter, planes, bounds, lane):
    q_at = remember(within(lambda p: quarter[p], *bounds))
    for p in planes:
        yield p, 24.0 * q_at(p) + lane.smooth(lane.rows(smooth_planes(q_at, p)))


def step_of(inside, diagonal):
    return jnp.where(inside > 0.0, DAMPING / diagonal, 0.0)


def odd(axis):
    return lax.rem(lax.axis_index(axis), 2) == 1


class From:
    def __init__(self, ref, first):
        self.ref, self.first = ref, first

    def __getitem__(self, at):
        if isinstance(at, tuple):
            return self.ref[at[0], at[1] - self.first]
        return self.ref[at - self.first]


class Either:
    def __init__(self, inner, span, outer):
        self.inner, self.span, self.outer = From(inner, span[0]), span, outer

    def __getitem__(self, at):
        p = at[1] if isinstance(at, tuple) else at
        return self.inner[at] if p in self.span else self.outer[at]


class Stack:
    def __init__(self, *parts):
        self.spots = {p: (ref, i) for ref, planes in parts for i, p in enumerate(planes)}

    def __getitem__(self, at):
        if isinstance(at, tuple):
            ref, i = self.spots[at[1]]
            return ref[at[0], i]
        ref, i = self.spots[at]
        return ref[i]

    def cut(self, at, rows):
        if isinstance(at, tuple):
            ref, i = self.spots[at[1]]
            return ref[at[0], i, rows, :]
        ref, i = self.spots[at]
        return ref[i, rows, :]


def vmem(shape):
    return pltpu.VMEM(shape, F32)


def row_spots(planes):
    spots, at = {}, 0
    for k, reach in enumerate(ROWS):
        for p in range(planes):
            spots[k, p] = slice(at, at + reach)
            at += reach
    return spots, at


def plane_spots(heights):
    spots, at = {}, 0
    for k, count in enumerate(PLANES):
        for i in range(count):
            spots[k, i] = slice(at, at + heights[k])
            at += heights[k]
    return spots, at


def middle_spots(rows):
    return plane_spots([rows] * 5)


def corner_spots():
    spots, at = {}, 0
    for k, count in enumerate(PLANES):
        for distance in range(1, count + 1):
            reach = ROWS[k] if distance < count else count
            spots[k, distance] = at, reach
            at += 2 * reach
    return spots, at


def pack_rows(
    forces, modulus, occupancy, bonded, own, to_c, to_d, to_a, to_b,
    modulus_here, occupancy_here, bonded_here, arrived,
):
    pairs = [(modulus, modulus_here), (occupancy, occupancy_here), (bonded, bonded_here)]
    pairs += [(forces.at[k], own.at[k]) for k in range(3)]
    copies = [pltpu.make_async_copy(*pair, arrived.at[i]) for i, pair in enumerate(pairs)]
    for copy in copies:
        copy.start()
    planes, rows = own.shape[1], own.shape[2]
    for copy in copies[:2]:
        copy.wait()
    for p in range(planes):
        own[3, p] = modulus_here[p] * occupancy_here[p].astype(F32)
    copies[2].wait()
    for p in range(planes):
        own[4, p] = MASS_TERM + PENALTY * bonded_here[p].astype(F32)
    for copy in copies[3:]:
        copy.wait()
    is_odd = odd("brick")
    spots, _ = row_spots(planes)
    for (k, p), spot in spots.items():
        first = own[k, p, 0 : ROWS[k], :]
        last = own[k, p, rows - ROWS[k] : rows, :]
        to_c[spot, :] = jnp.where(is_odd, first, last)
        to_d[spot, :] = jnp.where(is_odd, last, first)
    is_odd = odd("len")
    for (k, i), spot in middle_spots(rows)[0].items():
        first, last = own[k, i], own[k, planes - PLANES[k] + i]
        to_a[spot, :] = jnp.where(is_odd, first, last)
        to_b[spot, :] = jnp.where(is_odd, last, first)


def rows_beside(from_c, from_d):
    is_odd = odd("brick")

    def get(spot, reach):
        low, high = slice(spot.stop - reach, spot.stop), slice(spot.start, spot.start + reach)
        return (
            jnp.where(is_odd, from_c[low, :], from_d[low, :]),
            jnp.where(is_odd, from_d[high, :], from_c[high, :]),
        )

    return get


def pack_corners(planes, from_c, middle_b, from_d, middle_a, to_a, to_b):
    del middle_a, middle_b
    is_odd = odd("len")
    from_rows, _ = row_spots(planes)
    beside = rows_beside(from_c, from_d)
    for (k, distance), (at, reach) in corner_spots()[0].items():
        firsts = beside(from_rows[k, distance - 1], reach)
        lasts = beside(from_rows[k, planes - distance], reach)
        for half, (first, last) in enumerate(zip(firsts, lasts)):
            span = slice(at + half * reach, at + (half + 1) * reach)
            to_a[span, :] = jnp.where(is_odd, first, last)
            to_b[span, :] = jnp.where(is_odd, last, first)


def inner_planes(planes):
    return [range(HALO + i, HALO + planes - i) for i in (1, 2, 3)]


def kept_planes(planes):
    weighed, swept, _ = inner_planes(planes)
    own = range(HALO, HALO + planes)
    end = planes + 2 * HALO
    wide, close = range(2, end - 2), range(3, end - 3)
    pairs = ((swept, wide), (own, close), (own, wide), (weighed, close), (weighed, close))
    return [(inner, [p for p in every if p not in inner]) for inner, every in pairs]


def keep(kept_rows, targets, arrays, numbers):
    for k in range(2):
        for i, p in enumerate(numbers[k]):
            for c in range(3):
                targets[k][c, i] = arrays[k][c, p][kept_rows]
    for k in range(2, 5):
        for i, p in enumerate(numbers[k]):
            targets[k][i] = arrays[k][p][kept_rows]


def halves(x, rows):
    count = (rows.stop - rows.start) // 2
    return x[pl.ds(rows.start, count, stride=2), :] + x[pl.ds(rows.start + 1, count, stride=2), :]


def coarse_weight(lane, quarter_at, i, rows):
    sides, here, others = [
        smooth_planes(lambda j, at=at: quarter_at(j)[pl.ds(at, rows), :], i) for at in (7, 8, 9)
    ]
    return 24.0 * quarter_at(i)[pl.ds(8, rows), :] + lane.smooth(sides + 2.0 * here + others)


def fine_inner(
    own, from_c, from_d, to_a,
    source, quarter, shift, weight, step, v1, v2, rest, coarse_q, shift1, sums, cells, *more,
):
    del to_a
    planes, rows = own.shape[1], own.shape[2]
    lane = Lane(rows + 2 * WIDE, 1)
    beside = rows_beside(from_c, from_d)

    def put(k, p, r, value):
        if k < 3:
            source[k, p, r, :] = value
        elif k == 3:
            quarter[p, r, :] = 0.25 * value
        else:
            shift[p, r, :] = value

    for (k, p), spot in row_spots(planes)[0].items():
        low, high = beside(spot, ROWS[k])
        put(k, p, slice(WIDE - ROWS[k], WIDE), low)
        put(k, p, slice(WIDE, WIDE + rows), own[k, p])
        put(k, p, slice(WIDE + rows, WIDE + rows + ROWS[k]), high)

    weighed, swept, left = inner_planes(planes)
    bounds = (HALO, HALO + planes)
    source_at, quarter_at = From(source, HALO), From(quarter, HALO)
    for p, w in stiffness_sum(quarter_at, weighed, bounds, lane):
        q, s, i = quarter_at[p], shift[p - HALO], p - weighed[0]
        total = w + s
        weight[i] = total + 8.0 * q
        st = step_of(s, total + (4.0 * COUPLING) * q)
        step[i] = st
        for k in range(3):
            v1[k, i] = st * source_at[k, p]
    weight_at, step_at = From(weight, weighed[0]), From(step, weighed[0])

    def put_v2(k, p, value):
        v2[k, p - swept[0]] = value

    v1_at, v2_at, near = From(v1, weighed[0]), From(v2, swept[0]), APART
    sweep(
        lambda k, p: v1_at[k, p], quarter_at, weight_at, step_at, source_at,
        swept, (weighed[0], weighed[-1] + 1), lane, put_v2, near,
    )
    for p, _, r in defects(
        lambda k, p: v2_at[k, p], quarter_at, weight_at, source_at,
        left, (swept[0], swept[-1] + 1), lane, near,
    ):
        for k in range(3):
            rest[k, p - left[0]] = r[k]

    *kept, q_before, q_after, work = more
    half = rows // 2 + 2 * HALO
    outer = slice(WIDE - 2 * HALO, WIDE + rows + 2 * HALO)
    beyond = slice(outer.start - 2, outer.stop + 2)
    count = planes // 2
    for i in range(count):
        work[0, i] = quarter[2 * i] + quarter[2 * i + 1]
        work[1, i] = shift[2 * i] + shift[2 * i + 1]
    for f in range(2):
        for i in range(count):
            work[f, i] = lane.pair(work[f, i])
    for i in range(count):
        coarse_q[i, pl.ds(7, half + 2), :] = (0.25 * 0.125) * halves(work.at[0, i], beyond)
        shift1[i] = 0.125 * halves(work.at[1, i], outer)
    lane1 = Lane(half, 2)
    for i in range(1, count - 1):
        s = shift1[i]
        w = coarse_weight(lane1, lambda j: coarse_q.at[j], i, half)
        sums[i - 1] = jnp.where(s > 0.0, w + s, 0.0)

    for i in range(planes):
        rolled = lane.beside(quarter[i])
        for target, x in zip((q_before, q_after), rolled):
            target[i] = x[WIDE - HALO : WIDE + rows + HALO]

    inner = slice(HALO, HALO + rows // 2)
    for i in range(count // 2):
        pair = [coarse_q[2 * i + j, pl.ds(8, half), :] for j in range(2)]
        work[0, i, pl.ds(0, half), :] = lane1.pair(pair[0] + pair[1])
        work[1, i, pl.ds(0, half), :] = lane1.pair(shift1[2 * i] + shift1[2 * i + 1])
        for f, scale in enumerate((0.25 * 0.125, 0.125)):
            cells[f, i] = scale * halves(work.at[f, i], inner)
    keep(
        slice(WIDE - HALO, WIDE + rows + HALO), kept,
        (v2_at, source_at, quarter_at, weight_at, step_at),
        [x for x, _ in kept_planes(planes)],
    )


def fine_before(
    source_in, quarter_in, shift_in, weight_in, step_in, v1_in, v2_in, rest_in,
    coarse_q_in, shift1, sums_in, middle_b, middle_a, corner_b, corner_a,
    own_coarse, to_len, *more,
):
    *kept, v2_out, source_out, quarter_out, weight_out, step_out, shift_out, v1_out, work, coarse_q = more
    planes, ext_rows = quarter_in.shape[0], quarter_in.shape[1]
    ext_planes, rows = planes + 2 * HALO, ext_rows - 2 * WIDE
    lane = Lane(ext_rows, 1)

    def put(k, p, r, value):
        if k < 3:
            source_out[k, p, r, :] = value
        elif k == 3:
            quarter_out[p, r, :] = 0.25 * value
        else:
            shift_out[p, r, :] = value

    is_odd = odd("len")
    def put_both(k, distance, start, low, high):
        r = slice(start, start + low.shape[0])
        put(k, HALO - distance, r, low)
        put(k, HALO + planes - 1 + distance, r, high)

    def sides(a, b):
        return jnp.where(is_odd, a, b), jnp.where(is_odd, b, a)

    spots = middle_spots(rows)[0]
    for k, count in enumerate(PLANES):
        for distance in range(1, count + 1):
            low = sides(*[x[spots[k, count - distance], :] for x in (middle_a, middle_b)])[0]
            high = sides(*[x[spots[k, distance - 1], :] for x in (middle_a, middle_b)])[1]
            put_both(k, distance, WIDE, low, high)
    for (k, distance), (at, reach) in corner_spots()[0].items():
        for half, start in enumerate((WIDE - reach, WIDE + rows)):
            span = slice(at + half * reach, at + (half + 1) * reach)
            put_both(k, distance, start, *sides(corner_a[span, :], corner_b[span, :]))

    weighed, swept, left = inner_planes(planes)
    here = range(HALO, HALO + planes)
    source, quarter, shift = [
        Either(x, here, y)
        for x, y in ((source_in, source_out), (quarter_in, quarter_out), (shift_in, shift_out))
    ]
    weight, step, v1 = [
        Either(x, weighed, y)
        for x, y in ((weight_in, weight_out), (step_in, step_out), (v1_in, v1_out))
    ]
    v2 = Either(v2_in, swept, v2_out)

    bounds, near = (0, ext_planes), APART
    others = [p for p in range(1, ext_planes - 1) if p not in weighed]
    for p, w in stiffness_sum(quarter, others, bounds, lane):
        q, s = quarter[p], shift[p]
        total = w + s
        weight_out[p] = total + 8.0 * q
        st = step_of(s, total + (4.0 * COUPLING) * q)
        step_out[p] = st
        for k in range(3):
            v1_out[k, p] = st * source[k, p]

    numbers = [x for _, x in kept_planes(planes)]
    kept_rows = slice(WIDE - HALO, WIDE + rows + HALO)

    def put_v2(k, p, value):
        v2_out[k, p] = value
        kept[0][k, numbers[0].index(p)] = value[kept_rows]

    sweep(
        lambda k, p: v1[k, p], quarter, weight, step, source,
        [p for p in range(2, ext_planes - 2) if p not in swept], bounds, lane, put_v2, near,
    )

    half = rows // 2 + 2 * HALO
    outer = slice(WIDE - 2 * HALO, WIDE + rows + 2 * HALO)
    beyond = slice(outer.start - 2, outer.stop + 2)
    coarse_planes = planes // 2
    rest = {p: [rest_in[k, p - left[0]] for k in range(3)] for p in left}
    for p, _, r in defects(
        lambda k, p: v2[k, p], quarter, weight, source,
        [p for p in here if p not in left], bounds, lane, near,
    ):
        rest[p] = r
    for i in range(coarse_planes):
        p = HALO + 2 * i
        for k in range(3):
            work[k, i] = rest[p][k] + rest[p + 1][k]
    for j, p in enumerate((HALO - 2, HALO + planes)):
        work[3, j] = quarter[p] + quarter[p + 1]
    for k in range(4):
        for i in range(2 if k == 3 else coarse_planes):
            work[k, i] = lane.pair(work[k, i])
    for i in range(coarse_planes):
        for k in range(3):
            own_coarse[k, i] = 0.125 * halves(work.at[k, i], outer)

    for j in range(2):
        coarse_q[j, pl.ds(7, half + 2), :] = (0.25 * 0.125) * halves(work.at[3, j], beyond)

    def quarter1(i):
        if i < 0:
            return coarse_q.at[0]
        return coarse_q.at[1] if i == coarse_planes else coarse_q_in.at[i]

    lane1 = Lane(half, 2)
    for i in range(coarse_planes):
        own_coarse[3, i] = coarse_q_in[i, pl.ds(8, half), :]
        if 0 < i < coarse_planes - 1:
            own_coarse[4, i] = sums_in[i - 1]
        else:
            s = shift1[i]
            w = coarse_weight(lane1, quarter1, i, half)
            own_coarse[4, i] = jnp.where(s > 0.0, w + s, 0.0)

    even = (lane_ids((half, LANES)) & 1) == 0
    for k in range(5):
        for i in range(coarse_planes // 2):
            to_len[k, i] = jnp.where(even, own_coarse[k, 2 * i], own_coarse[k, 2 * i + 1])

    keep(kept_rows, kept, (v2, source, quarter, weight, step), [[]] + numbers[1:])


def middle_before(
    own, cells, from_b, from_a,
    to_all, v2, source, quarter, weight, step,
    v1, work,
):
    planes, ext_rows = own.shape[1], own.shape[2]
    rows = ext_rows - 2 * HALO
    ext_planes = planes + 2 * HALO
    lane = Lane(ext_rows, 2)

    def put(k, p, value):
        if k < 3:
            source[k, p] = value
        elif k == 3:
            quarter[p] = value
        else:
            weight[p] = value

    is_odd = odd("len")
    even = (lane_ids((ext_rows, LANES)) & 1) == 0
    for k in range(5):
        for p in range(planes):
            put(k, HALO + p, own[k, p])
        for i in range(HALO // 2):
            a, b = from_a[k, i], from_b[k, i]
            for start, x in (
                (0, jnp.where(is_odd, a, b)),
                (HALO + planes, jnp.where(is_odd, b, a)),
            ):
                put(k, start + 2 * i, jnp.where(even, x, turn(x, 1, 1)))
                put(k, start + 2 * i + 1, jnp.where(even, turn(x, -1, 1), x))

    for p in range(ext_planes):
        q, total = quarter[p], weight[p]
        st = step_of(total, total + (4.0 * COUPLING) * q)
        step[p] = st
        weight[p] = total + 8.0 * q
        for k in range(3):
            v1[k, p] = st * source[k, p]

    def put_v2(k, p, value):
        v2[k, p] = value

    bounds, near = (0, ext_planes), {}
    sweep(
        lambda k, p: v1[k, p], quarter, weight, step, source,
        range(1, ext_planes - 1), bounds, lane, put_v2, near,
    )
    held = {}
    half = rows // 2
    for p, _, r in defects(
        lambda k, p: v2[k, p], quarter, weight, source,
        range(HALO, HALO + planes), bounds, lane, near,
    ):
        if p % 2 == 0:
            held = r
            continue
        i = (p - HALO) // 2
        for k in range(3):
            work[k, i] = held[k] + r[k]
    for i in range(planes // 2):
        for k in range(3):
            work[k, i] = lane.pair(work[k, i])
    depth = planes // 2
    ids = lane_ids((depth * half, LANES))
    row = lax.broadcasted_iota(jnp.int32, ids.shape, 0)
    mine = ids // ROW == row % half
    lines = []
    for k in range(5):
        parts = [
            cells[k - 3, i]
            if k >= 3
            else 0.125
            * (
                work[k, i, pl.ds(HALO, half, stride=2), :]
                + work[k, i, pl.ds(HALO + 1, half, stride=2), :]
            )
            for i in range(depth)
        ]
        x = pick(jnp.concatenate(parts, axis=0), (ids % ROW) * (LANES // ROW))
        x = jnp.where(mine, x, 0.0)
        x = x + turn(x, -1, 0)
        x = x + turn(x, -2, 0)
        lines += [x[i * half : i * half + 1] for i in range(depth)]
    block = jnp.concatenate(lines * 4, axis=0)
    count = block.shape[0]
    for at in range(0, to_all.shape[0], count):
        to_all[at : at + count, :] = block


def coarse_and_after(
    bricks_before,
    table, v2_mid, source_mid, quarter_mid, weight_mid, step_mid, *more,
):
    kept_inner, kept_outer = more[:5], more[5:10]
    q_before, q_after, out, wide2, u_mid, x_mid, u_fine, x_fine = more[10:]
    brick = lax.axis_index("brick")
    slab = lax.axis_index("len")
    bricks, planes2 = wide2.shape[2] - 16, wide2.shape[1] - 4
    depth = (v2_mid.shape[1] - 2 * HALO) // 2
    lines = 5 * depth

    def field(f):
        return jnp.stack(
            [
                table[pl.ds((i // depth) * bricks * lines + f * depth + i % depth, bricks, stride=lines), :]
                for i in range(planes2)
            ],
            axis=0,
        )

    lane2, lane3 = Packed(bricks, 1), Packed(bricks, 2)
    b2, q2, s2 = [field(k) for k in range(3)], field(3), field(4)
    e2, x2 = lane2.terms(q2, s2)
    u2 = lane2.sweep([x2 * b for b in b2], e2, x2, b2)

    rest = lane2.defects(u2, e2, b2)
    joint = lane2.restrict(jnp.concatenate(rest + [0.25 * q2, s2], axis=0))
    count = planes2 // 2
    *b3, q3, s3 = [joint[i * count : (i + 1) * count] for i in range(5)]
    e3, x3 = lane3.terms(q3, s3)
    u3 = [x3 * b for b in b3]
    for _ in range(3):
        u3 = lane3.sweep(u3, e3, x3, b3)

    u2 = [u2[k] + twice_planes(u3[k]) for k in range(3)]
    for _ in range(2):
        u2 = lane2.sweep(u2, e2, x2, b2)
    wide2[...] = jnp.zeros_like(wide2)
    for k in range(3):
        wide2[k, pl.ds(2, planes2), pl.ds(8, bricks), :] = u2[k]

    v2_fine, source_fine, quarter_fine, weight_fine, step_fine = [
        Stack((inner, numbers[0]), (outer, numbers[1]))
        for inner, outer, numbers in zip(
            kept_inner, kept_outer, kept_planes(x_fine.shape[1] - 2 * HALO)
        )
    ]
    planes1 = v2_mid.shape[1]
    rows1 = v2_mid.shape[2]
    lane1 = Lane(rows1, 2)
    bounds1, beside1 = (0, planes1), {}
    line_at = brick - bricks_before(brick) + 8
    half_shape = (rows1 // 2, LANES)
    ids, row = lane_ids(half_shape), lax.broadcasted_iota(jnp.int32, half_shape, 0)
    lanes = ROW * ((row + 2) % 4) + ids // (LANES // ROW)
    for k in range(3):
        for i in range(planes1 // 2):
            low, own, high = [
                jnp.broadcast_to(
                    wide2[k, depth * slab + i, pl.ds(line_at + at, 1), :], half_shape
                )
                for at in (-1, 0, 1)
            ]
            piece = pick(jnp.where(row < 2, low, jnp.where(row < 6, own, high)), lanes)
            for half in range(2):
                x_mid[k, i, pl.ds(half, rows1 // 2, stride=2), :] = piece
            both = x_mid[k, i]
            for p in (2 * i, 2 * i + 1):
                if 1 <= p < planes1 - 1:
                    u_mid[k, p] = v2_mid[k, p] + both

    def put_mid(k, p, value):
        x_mid[k, p] = value

    sweep(
        lambda k, p: u_mid[k, p], quarter_mid, weight_mid, step_mid, source_mid,
        range(2, planes1 - 2), bounds1, lane1, put_mid, beside1,
    )

    def put_mid_last(k, p, value):
        u_mid[k, p] = value

    sweep(
        lambda k, p: x_mid[k, p], quarter_mid, weight_mid, step_mid, source_mid,
        range(3, planes1 - 3), bounds1, lane1, put_mid_last, beside1,
    )

    planes0, rows0 = x_fine.shape[1], x_fine.shape[2]
    lane0 = Lane(rows0, 1)
    bounds0 = (0, planes0)
    beside0 = {
        i + HALO: (q_before[i], q_after[i]) for i in range(planes0 - 2 * HALO)
    }
    half_rows = rows0 // 2
    for k in range(3):
        for i in range(3, planes1 - 3):
            piece = u_mid[k, i, pl.ds(2, half_rows), :]
            p = 2 * i - HALO
            for half in range(2):
                x_fine[k, p, pl.ds(half, half_rows, stride=2), :] = piece
            both = x_fine[k, p]
            for at in (p, p + 1):
                u_fine[k, at] = v2_fine[k, at] + both

    def put_fine(k, p, value):
        x_fine[k, p] = value

    sweep(
        lambda k, p: u_fine[k, p], quarter_fine, weight_fine, step_fine, source_fine,
        range(3, planes0 - 3), bounds0, lane0, put_fine, beside0,
    )

    def put_out(k, p, value):
        out[k, p - HALO] = value

    own_rows = slice(HALO, rows0 - HALO)
    sweep_rows(
        lambda k, p, r: x_fine[k, p, r, :], quarter_fine, weight_fine, step_fine, source_fine,
        range(HALO, planes0 - HALO), own_rows, Lane(rows0 - 2 * HALO, 1), put_out,
        lambda p: (q_before[p - HALO, own_rows, :], q_after[p - HALO, own_rows, :]),
    )


def call(kernel, outs, scratch=(), name=None, **more):
    return pl.pallas_call(
        kernel,
        out_shape=[jax.ShapeDtypeStruct(shape, F32) for shape in outs],
        scratch_shapes=[vmem(x) if isinstance(x, tuple) else x for x in scratch],
        compiler_params=pltpu.CompilerParams(vmem_limit_bytes=40 * 1024 * 1024),
        name=name,
        **more,
    )


def swap(x, axis, first):
    count = lax.axis_size(axis)
    pairs = []
    for i in range(first, count - 1, 2):
        pairs += [(i, i + 1), (i + 1, i)]
    return lax.ppermute(x, axis, pairs)


def body(forces, modulus, occupancy, bonded):
    planes, rows = modulus.shape[0], modulus.shape[1]
    slabs, bricks = lax.axis_size("len"), lax.axis_size("brick")
    ext, ext_rows = planes + 2 * HALO, rows + 2 * WIDE
    half, half_rows = planes // 2, rows // 2
    mid, mid_rows = half + 2 * HALO, half_rows + 2 * HALO

    side, block = (row_spots(planes)[1], LANES), (planes, rows, LANES)
    middle_side, corner = (middle_spots(rows)[1], LANES), (corner_spots()[1], LANES)
    here = [
        pltpu.with_memory_space_constraint(x, pltpu.HBM)
        for x in (forces, modulus, occupancy, bonded)
    ]
    own, to_c, to_d, to_a, to_b = call(
        pack_rows,
        [(5,) + block, side, side, middle_side, middle_side],
        [block, pltpu.VMEM(block, jnp.int32), pltpu.VMEM(block, jnp.int32)]
        + [pltpu.SemaphoreType.DMA((6,))],
        name="pack_rows",
        in_specs=[pl.BlockSpec(memory_space=pltpu.HBM)] * 4,
    )(*here)
    from_c = swap(to_c, "brick", 0)
    middle_b = swap(to_b, "len", 1)
    from_d = swap(to_d, "brick", 1)
    middle_a = swap(to_a, "len", 0)
    to_a, to_b = call(
        functools.partial(pack_corners, planes),
        [corner, corner],
        name="pack_corners",
        in_specs=[pl.BlockSpec(memory_space=x) for x in (pltpu.VMEM, pl.ANY) * 2],
    )(from_c, middle_b, from_d, middle_a)
    corner_a = swap(to_a, "len", 0)
    corner_b = swap(to_b, "len", 1)

    field, cell = (3, ext, ext_rows, LANES), (ext, ext_rows, LANES)
    line = (rows + 2 * HALO, LANES)
    block = (planes, ext_rows, LANES)
    weighed, swept, left = [(len(x), ext_rows, LANES) for x in inner_planes(planes)]
    kept_inner, kept_outer = [
        [
            ((3,) if k < 2 else ()) + (len(numbers[part]),) + line
            for k, numbers in enumerate(kept_planes(planes))
        ]
        for part in range(2)
    ]
    coarse = (half, mid_rows + 16, LANES)
    inner = call(
        fine_inner,
        [(3,) + block, block, block, weighed, weighed]
        + [(3,) + weighed, (3,) + swept, (3,) + left]
        + [coarse, (half, mid_rows, LANES), (half - 2, mid_rows, LANES)]
        + [(2, half // 2, half_rows // 2, LANES)]
        + kept_inner
        + [(planes,) + line] * 2,
        [(2, half, ext_rows, LANES)],
        name="fine_inner",
        in_specs=[pl.BlockSpec(memory_space=pltpu.VMEM)] * 3
        + [pl.BlockSpec(memory_space=pl.ANY)],
        cost_estimate=pl.CostEstimate(flops=10**7, bytes_accessed=4 * 10**6, transcendentals=0),
    )(own, from_c, from_d, to_b)
    inner, cells, kept_inner, rolled = inner[:11], inner[11], inner[12:17], inner[17:]
    own, to_len, *kept_outer = call(
        fine_before,
        [(5, half, mid_rows, LANES), (5, half // 2, mid_rows, LANES)] + kept_outer,
        [field, field, cell, cell, cell, cell, field]
        + [(4, half, ext_rows, LANES), (2,) + coarse[1:]],
        name="fine_before",
    )(*inner, middle_b, middle_a, corner_b, corner_a)
    from_a = swap(to_len, "len", 0)
    from_b = swap(to_len, "len", 1)

    field1, cell1 = (3, mid, mid_rows, LANES), (mid, mid_rows, LANES)
    depth = half // 2
    lines = 5 * depth
    to_all, *middle = call(
        middle_before,
        [(slabs * bricks * lines, LANES)] + [field1, field1, cell1, cell1, cell1],
        [field1, (3, depth, mid_rows, LANES)],
        name="middle_before",
    )(own, cells, from_b, from_a)

    to_all = to_all.reshape(-1, 2, LANES)
    table = lax.all_to_all(to_all, BOTH, 0, 0, tiled=True).reshape(-1, LANES)
    window = bricks if bricks <= 8 else 16

    def first_brick(brick):
        return jnp.clip(brick - 4, 0, bricks - window)

    if window < bricks:
        table = lax.dynamic_slice_in_dim(
            table.reshape(slabs, bricks * lines, LANES),
            first_brick(lax.axis_index("brick")) * lines, window * lines, axis=1,
        ).reshape(slabs * window * lines, LANES)
    planes2 = slabs * depth
    (out,) = call(
        functools.partial(coarse_and_after, first_brick),
        [forces.shape],
        [(3, planes2 + 4, window + 16, LANES), field1, field1]
        + [(3, ext, rows + 2 * HALO, LANES)] * 2,
        name="coarse_and_after",
    )(table, *middle, *kept_inner, *kept_outer, *rolled)
    return out


def solution(mesh):
    cells = P("len", "brick", None)
    forces = P(None, "len", "brick", None)
    return jax.shard_map(
        body, mesh=mesh, in_specs=(forces, cells, cells, cells), out_specs=forces, check_vma=False
    )
```
